512 devices in a mesh: row: 16 (over z, core), col: 32 (over x, y).
Axes of the slice: x: 4, y: 8, z: 8, core: 2. Of those that a mesh axis runs over, the one named last changes fastest.
Arguments:
- factor: float32 [2, 512, 24576], P(None, 'row', 'col'), may hold values from -0.0390625 to 0.0390625
- solved: float32 [1024, 24576], P('row', 'col'), may hold values from -6 to 6
- rhs_window: float32 [1024, 2, 512], P('col', None, 'row'), may hold values from -6 to 6
- inverses: float32 [2, 512, 512], replicated, as said below
- coupling: float32 [512, 512], replicated, may hold values from -0.25 to 0.25
Outputs:
- solution: float32 [1024, 2, 512], P('col', None, 'row')
- updated: float32 [1024, 24576], P('row', 'col')
The draws below stay inside these ranges and needn't reach their ends.
Inputs may be any that keep to these rules, and one draw needn't show every extreme that they name: inverses[k] is lower triangular; its diagonal entries lie between 0.5 and 1.5.
All inputs are finite; a program needn't handle non-finite values.
Results may differ from the reference program's by a relative error of at most 0.00011.
Values sent between devices are 32-bit elements; how exact they have to be, the bound alone decides.
No kernel may reach another device: no remote copies, remote signals or barrier semaphores. Data moves between devices by JAX's collectives and lax.ppermute only.
A program may use at most 64 MiB of HBM per device.

```python
import jax
import jax.numpy as jnp
from jax import lax

NB = 512
RHS = 1024
LEAD = 24576


def draw_inverses(key, part):
    key_lower, key_diag = jax.random.split(jax.random.fold_in(key, 17))
    lower = jax.random.normal(key_lower, (2, NB, NB), jnp.float32) * NB ** (-0.5)
    diagonal = jax.random.uniform(key_diag, (2, NB), jnp.float32, minval=0.5, maxval=1.5)
    return jnp.tril(lower, -1) + diagonal[:, :, None] * jnp.eye(NB, dtype=jnp.float32)[None, :, :]


def block_levels(key, dims, pieces, least, largest):
    def one(axis_at, blocks):
        heights = jax.random.uniform(jax.random.fold_in(jax.random.fold_in(key, 6), axis_at), (blocks,), jnp.float32, least / len(pieces), largest / len(pieces))
        return jnp.repeat(jnp.exp(heights), dims[axis_at] // blocks).reshape((-1,) + (1,) * (len(dims) - axis_at - 1))

    factor_of = one(*pieces[0])
    for cut in pieces[1:]:
        factor_of = factor_of * one(*cut)
    return factor_of


def centred(stream_key, dims, deviation, reach, cuts=(), held_as=jnp.bfloat16):
    loudness = block_levels(stream_key, dims, cuts, -0.22, 0.18) if cuts else 1.0
    values = jax.random.normal(stream_key, dims, jnp.float32) * deviation * loudness
    return jnp.minimum(jnp.maximum(values, -reach), reach).astype(held_as)


def setup_inputs(seed: int = 0) -> dict:
    seeds = jax.random.split(jax.random.key(seed), 6)
    factor = centred(seeds[0], (2, NB, LEAD), LEAD ** -0.5, 0.0390625, ((1, 16), (2, 32)), jnp.float32)
    solved = centred(seeds[1], (RHS, LEAD), 1.0, 6.0, ((0, 16), (1, 32)), jnp.float32)
    rhs_window = centred(seeds[2], (RHS, 2, NB), 1.0, 6.0, ((0, 32), (2, 16)), jnp.float32)
    inverses = draw_inverses(jax.random.fold_in(seeds[5], 71), 0)
    coupling = centred(seeds[4], (NB, NB), NB ** -0.5, 0.25, (), jnp.float32)
    return dict(factor=factor, solved=solved, rhs_window=rhs_window, inverses=inverses, coupling=coupling)


precise = lax.Precision.HIGHEST


def panel_solve(residual, inverses, coupling):
    forward_lead = jnp.dot(residual[:, 0, :], inverses[0].T, precision=precise)
    forward_next = jnp.dot(residual[:, 1, :] - jnp.dot(forward_lead, coupling.T, precision=precise), inverses[1].T, precision=precise)
    backward_next = jnp.dot(forward_next, inverses[1], precision=precise)
    backward_lead = jnp.dot(forward_lead - jnp.dot(backward_next, coupling, precision=precise), inverses[0], precision=precise)
    return jnp.stack([backward_lead, backward_next], axis=1)


def reference(factor, solved, rhs_window, inverses, coupling):
    totals = jnp.einsum('rj,kij->rki', solved, factor, precision=precise)
    residual = rhs_window - totals
    solution = panel_solve(residual, inverses, coupling)
    updated = solved - jnp.einsum('rki,kij->rj', solution, factor, precision=precise)
    return solution, updated
```

```python
import jax
import jax.numpy as jnp
from jax import lax
from jax.sharding import PartitionSpec as P

precise = lax.Precision.HIGHEST

PLANES = 8
CORES = 2
COLS = 32


def core_swap():
    return [(row, row ^ 1) for row in range(PLANES * CORES)]


def plane_shift(step):
    return [
        (plane * CORES + core, (plane + step) % PLANES * CORES + core)
        for plane in range(PLANES)
        for core in range(CORES)
    ]


def window_to_work():
    pairs = []
    for row in range(PLANES * CORES):
        plane, core = divmod(row, CORES)
        for col in range(COLS):
            rhs_row, half = divmod(col, 2)
            rhs_plane, rhs_core = divmod(rhs_row, CORES)
            target = (rhs_core * 2 + half) * PLANES + plane
            pairs.append((row * COLS + col, (rhs_plane * CORES + core) * COLS + target))
    return pairs


def work_to_window():
    return [
        (row * COLS + col, (col // 2) * COLS + 2 * row + col % 2)
        for row in range(PLANES * CORES)
        for col in range(COLS)
    ]


def panel_solve(lead, follow, inverses, coupling):
    forward_lead = jnp.dot(lead, inverses[0].T, precision=precise)
    forward_next = jnp.dot(
        follow - jnp.dot(forward_lead, coupling.T, precision=precise),
        inverses[1].T,
        precision=precise,
    )
    backward_next = jnp.dot(forward_next, inverses[1], precision=precise)
    backward_lead = jnp.dot(
        forward_lead - jnp.dot(backward_next, coupling, precision=precise),
        inverses[0],
        precision=precise,
    )
    return backward_lead, backward_next


def turn(blocks, start):
    twice = jnp.concatenate([blocks, blocks], axis=2)
    return lax.dynamic_slice_in_dim(twice, start, PLANES, 2)


def shards(factor, solved, rhs_window, inverses, coupling):
    rows, width = solved.shape
    part = factor.shape[1]
    row = lax.axis_index("row")
    col = lax.axis_index("col")
    plane, core = row // CORES, row % CORES

    window = lax.ppermute(rhs_window, ("row", "col"), window_to_work())
    own = factor.reshape(2 * part, width)
    behind1 = lax.ppermute(own, "row", plane_shift(1))
    ahead1 = lax.ppermute(own, "row", plane_shift(-1))
    behind2 = lax.ppermute(own, "row", plane_shift(2))
    ahead2 = lax.ppermute(own, "row", plane_shift(-2))
    solved_pair = jnp.concatenate([solved, lax.ppermute(solved, "row", core_swap())], axis=0)
    behind3 = lax.ppermute(behind2, "row", plane_shift(1))
    ahead3 = lax.ppermute(ahead2, "row", plane_shift(-1))
    across = jnp.concatenate(
        [
            lax.ppermute(ahead2[:part], "row", plane_shift(-2)),
            lax.ppermute(behind2[part:], "row", plane_shift(2)),
        ],
        axis=0,
    )
    panel = jnp.concatenate(
        [own, ahead1, ahead2, ahead3, across, behind3, behind2, behind1], axis=0
    )
    totals = jnp.einsum("rj,ij->ri", solved_pair, panel, precision=precise)
    panel_other = lax.ppermute(panel, "row", core_swap())

    rhs_core, rhs_half, rhs_plane = col // 16, col // 8 % 2, col % 8
    at = (
        (rhs_core ^ core) * rows + rhs_half * (rows // 2),
        (rhs_plane - plane) % PLANES * 2 * part,
    )
    block = window.reshape(rows // 2, 2 * part)
    totals = lax.dynamic_update_slice(
        totals, lax.dynamic_slice(totals, at, block.shape) - block, at
    )
    each = rows // COLS
    spread = lax.all_to_all(
        totals.reshape(2, COLS, each, -1), "col", split_axis=1, concat_axis=0, tiled=True
    )
    residual = -jnp.sum(spread.reshape(COLS, 2, each, -1), axis=0)
    other = lax.ppermute(residual[1], "row", core_swap())
    pair = jnp.stack([residual[0], other], axis=0).reshape(2, each, PLANES, 2, part)
    by_core = jnp.where(core == 0, pair, pair[::-1])
    whole = turn(by_core, PLANES - plane)
    whole = jnp.transpose(whole, (3, 1, 2, 0, 4)).reshape(2, each, -1)
    backward_lead, backward_next = panel_solve(whole[0], whole[1], inverses, coupling)
    found = jnp.stack([backward_lead, backward_next], axis=0)
    found = found.reshape(2, each, PLANES, CORES, part)
    found = turn(jnp.transpose(found, (3, 1, 2, 0, 4)), plane)
    found = jnp.where(core == 0, found, found[::-1])
    found = jnp.transpose(found, (1, 0, 2, 3, 4)).reshape(each, -1)
    gathered = lax.all_to_all(
        jnp.broadcast_to(found, (COLS,) + found.shape), "col", 0, 0, tiled=True
    ).reshape(rows, -1)

    out_row, out_half = col // 2, col % 2
    out_plane, out_core = out_row // CORES, out_row % CORES
    grid = gathered.reshape(rows, CORES * PLANES, 2, part)
    mine = lax.dynamic_slice(
        grid,
        (out_half * (rows // 2), (out_core ^ core) * PLANES + (out_plane - plane) % PLANES, 0, 0),
        (rows // 2, 1, 2, part),
    )
    owned = lax.ppermute(mine[:, 0], ("row", "col"), work_to_window())
    half = panel.shape[0]
    correction = jnp.dot(gathered[:, :half], panel, precision=precise)
    correction += jnp.dot(gathered[:, half:], panel_other, precision=precise)
    return owned, solved - correction


def solution(mesh):
    in_specs = (P(None, "row", "col"), P("row", "col"), P("col", None, "row"), P(), P())
    out_specs = (P("col", None, "row"), P("row", "col"))
    return jax.shard_map(shards, mesh=mesh, in_specs=in_specs, out_specs=out_specs, check_vma=False)
```

```python
import jax
import jax.numpy as jnp
from jax import lax
from jax.experimental import pallas as pl
from jax.experimental.pallas import tpu as pltpu
from jax.sharding import PartitionSpec as P

precise = lax.Precision.HIGHEST
VMEM_BYTES = 32 * 1024 * 1024

PLANES = 8
CORES = 2
COLS = 32


def core_swap():
    return [(row, row ^ 1) for row in range(PLANES * CORES)]


def plane_shift(step):
    return [
        (plane * CORES + core, (plane + step) % PLANES * CORES + core)
        for plane in range(PLANES)
        for core in range(CORES)
    ]


def plane_groups():
    size = CORES * COLS
    return [list(range(plane * size, (plane + 1) * size)) for plane in range(PLANES)]


def window_to_work():
    pairs = []
    for row in range(PLANES * CORES):
        plane, core = divmod(row, CORES)
        for col in range(COLS):
            rhs_row, half = divmod(col, 2)
            rhs_plane, rhs_core = divmod(rhs_row, CORES)
            target = (rhs_core * 2 + half) * PLANES + plane
            pairs.append((row * COLS + col, (rhs_plane * CORES + core) * COLS + target))
    return pairs


def work_to_window():
    return [
        (row * COLS + col, (col // 2) * COLS + 2 * row + col % 2)
        for row in range(PLANES * CORES)
        for col in range(COLS)
    ]


def halves(x):
    high = x.astype(jnp.bfloat16)
    return high, (x - high.astype(jnp.float32)).astype(jnp.bfloat16)


def in_vmem():
    return pl.BlockSpec(memory_space=pltpu.VMEM)


def kernel_call(body, out_shape, in_specs, out_specs, flops=0, moved=0):
    return pl.pallas_call(
        body,
        out_shape=out_shape,
        in_specs=in_specs,
        out_specs=out_specs,
        compiler_params=pltpu.CompilerParams(vmem_limit_bytes=VMEM_BYTES),
        cost_estimate=pl.CostEstimate(flops=flops, bytes_accessed=moved, transcendentals=0),
    )


def hold(values, arrivals):
    def body(*refs):
        count = len(values)
        for source, target in zip(refs[:count], refs[count + len(arrivals) :]):
            target[...] = source[...]

    return kernel_call(
        body,
        [jax.ShapeDtypeStruct(v.shape, v.dtype) for v in values],
        [in_vmem()] * len(values) + [pl.BlockSpec(memory_space=pl.ANY)] * len(arrivals),
        [in_vmem()] * len(values),
    )(*values, *arrivals)


def rounded_dot(left, right, contract):
    (left_up, left_down), (right_up, right_down) = left, right

    def one(x, y):
        return lax.dot_general(x, y, (contract, ((), ())), preferred_element_type=jnp.float32)

    return one(left_up, right_up) + one(left_down, right_up) + one(left_up, right_down)


def reduce_panel(solved_pair, placed, pieces):
    rows, width = solved_pair.shape
    unknowns = placed.shape[1]
    each = rows // (CORES * COLS)

    def body(solved_ref, placed_ref, *refs):
        *piece_refs, out_ref, panel_ref = refs
        at = 0
        for ref in piece_refs:
            panel_ref[at : at + ref.shape[0]] = ref[...]
            at += ref.shape[0]
        total = rounded_dot(halves(panel_ref[...]), halves(solved_ref[...]), ((1,), (1,)))
        partial = placed_ref[...] - total.T
        for member in range(CORES * COLS):
            out_ref[member] = partial[member * each : (member + 1) * each]

    return kernel_call(
        body,
        [
            jax.ShapeDtypeStruct((CORES * COLS, each, unknowns), jnp.float32),
            jax.ShapeDtypeStruct((unknowns, width), jnp.float32),
        ],
        [in_vmem()] * (2 + len(pieces)),
        [in_vmem()] * 2,
        flops=6 * rows * unknowns * width,
        moved=8 * unknowns * width,
    )(solved_pair, placed, *pieces)


def correct(solved, found, panel, panel_other):
    def body(solved_ref, found_ref, panel_ref, other_ref, out_ref):
        half = panel_ref.shape[0]
        contract = ((1,), (0,))
        total = rounded_dot(halves(found_ref[:, :half]), halves(panel_ref[...]), contract)
        total += rounded_dot(halves(found_ref[:, half:]), halves(other_ref[...]), contract)
        out_ref[...] = solved_ref[...] - total

    rows, width = solved.shape
    return kernel_call(
        body,
        jax.ShapeDtypeStruct(solved.shape, solved.dtype),
        [in_vmem()] * 4,
        in_vmem(),
        flops=36 * rows * found.shape[1] * width,
        moved=4 * found.shape[1] * width,
    )(solved, found, panel, panel_other)


def panel_solve(lead, follow, inverses, coupling):
    forward_lead = jnp.dot(lead, inverses[0].T, precision=precise)
    forward_next = jnp.dot(
        follow - jnp.dot(forward_lead, coupling.T, precision=precise),
        inverses[1].T,
        precision=precise,
    )
    backward_next = jnp.dot(forward_next, inverses[1], precision=precise)
    backward_lead = jnp.dot(
        forward_lead - jnp.dot(backward_next, coupling, precision=precise),
        inverses[0],
        precision=precise,
    )
    return backward_lead, backward_next


def turn(blocks, start):
    twice = jnp.concatenate([blocks, blocks], axis=2)
    return lax.dynamic_slice_in_dim(twice, start, PLANES, 2)


def shards(factor, solved, rhs_window, inverses, coupling):
    rows, width = solved.shape
    part = factor.shape[1]
    row = lax.axis_index("row")
    col = lax.axis_index("col")
    plane, core = row // CORES, row % CORES

    own = factor.reshape(2 * part, width)
    behind2 = lax.ppermute(own, "row", plane_shift(2))
    ahead2 = lax.ppermute(own, "row", plane_shift(-2))
    behind1 = lax.ppermute(own, "row", plane_shift(1))
    ahead1 = lax.ppermute(own, "row", plane_shift(-1))
    behind3 = lax.ppermute(behind2, "row", plane_shift(1))
    ahead3 = lax.ppermute(ahead2, "row", plane_shift(-1))
    across = [
        lax.ppermute(ahead2[:part], "row", plane_shift(-2)),
        lax.ppermute(behind2[part:], "row", plane_shift(2)),
    ]
    window = lax.ppermute(rhs_window, ("row", "col"), window_to_work())
    (solved_held,) = hold((solved,), (behind1, ahead1))
    solved_other = lax.ppermute(solved_held, "row", core_swap())
    pair = jnp.stack([solved, solved_other], axis=0)
    solved_pair = jnp.where(core == 0, pair, pair[::-1]).reshape(2 * rows, width)

    rhs_core, rhs_half, rhs_plane = col // 16, col // 8 % 2, col % 8
    block = window.reshape(rows // 2, 2 * part)
    at = (rhs_core * rows + rhs_half * (rows // 2), (rhs_plane - plane) % PLANES * 2 * part)
    placed = jnp.zeros((2 * rows, PLANES * 2 * part), jnp.float32)
    placed = lax.dynamic_update_slice(placed, block, at)

    pieces = [own, ahead1, ahead2, ahead3, *across, behind3, behind2, behind1]
    partial, panel = reduce_panel(solved_pair, placed, pieces)
    panel_other = lax.ppermute(panel, "row", core_swap())

    each = rows // COLS
    spread = lax.all_to_all(
        partial,
        ("row", "col"),
        0,
        0,
        axis_index_groups=plane_groups(),
        tiled=True,
    )
    residual = jnp.sum(spread.reshape(CORES, COLS, each, -1), axis=1)
    residual = turn(residual.reshape(CORES, each, PLANES, 2, part), PLANES - plane)
    whole = jnp.transpose(residual, (3, 1, 2, 0, 4)).reshape(2, each, -1)
    solved_panels = panel_solve(whole[0], whole[1], inverses, coupling)
    found = jnp.stack(lax.optimization_barrier(solved_panels), axis=0)
    found = found.reshape(2, each, PLANES, CORES, part)
    found = turn(jnp.transpose(found, (3, 1, 2, 0, 4)), plane)
    found = jnp.where(core == 0, found, found[::-1])
    found = jnp.transpose(found, (1, 0, 2, 3, 4)).reshape(each, -1)
    gathered = lax.all_to_all(
        jnp.broadcast_to(found, (COLS,) + found.shape), "col", 0, 0, tiled=True
    ).reshape(rows, -1)

    out_row, out_half = col // 2, col % 2
    out_plane, out_core = out_row // CORES, out_row % CORES
    grid = gathered.reshape(rows, CORES * PLANES, 2, part)
    mine = lax.dynamic_slice(
        grid,
        (out_half * (rows // 2), (out_core ^ core) * PLANES + (out_plane - plane) % PLANES, 0, 0),
        (rows // 2, 1, 2, part),
    )
    owned = lax.ppermute(mine[:, 0], ("row", "col"), work_to_window())
    return owned, correct(solved, gathered, panel, panel_other)


def solution(mesh):
    in_specs = (P(None, "row", "col"), P("row", "col"), P("col", None, "row"), P(), P())
    out_specs = (P("col", None, "row"), P("row", "col"))
    return jax.shard_map(shards, mesh=mesh, in_specs=in_specs, out_specs=out_specs, check_vma=False)
```

```python
import jax
import jax.numpy as jnp
from jax import lax
from jax.experimental import pallas as pl
from jax.experimental.pallas import tpu as pltpu
from jax.sharding import PartitionSpec as P

PLANES = 8
CORES = 2
ROWS = PLANES * CORES
HALF_RING = ROWS // 2
COLS = 32
VMEM_BYTES = 16 * 1024 * 1024


def core_swap():
    return [(row, row ^ 1) for row in range(ROWS)]


def apart(step):
    return [
        (plane * CORES + core, (plane + (step, -step)[core]) % PLANES * CORES + core)
        for plane in range(PLANES)
        for core in range(CORES)
    ]


def ring_place(unknown_row, plane):
    return (unknown_row - CORES * plane + HALF_RING - 1) % ROWS


def window_to_work():
    pairs = []
    for row in range(ROWS):
        for col in range(COLS):
            rhs_row, half = divmod(col, 2)
            plane, rhs_core = divmod(rhs_row, CORES)
            keeper, slot = divmod(ring_place(row, plane), HALF_RING)
            target = (rhs_core * 2 + half) * HALF_RING + slot
            pairs.append((row * COLS + col, (plane * CORES + keeper) * COLS + target))
    return pairs


def work_to_window():
    return [
        (row * COLS + col, (col // 2) * COLS + 2 * row + col % 2)
        for row in range(ROWS)
        for col in range(COLS)
    ]


def halves(x):
    high = x.astype(jnp.bfloat16)
    return high, (x - high.astype(jnp.float32)).astype(jnp.bfloat16)


def rounded_dot(left, right, contract):
    (left_up, left_down), (right_up, right_down) = left, right

    def one(x, y):
        return lax.dot_general(x, y, (contract, ((), ())), preferred_element_type=jnp.float32)

    return one(left_up, right_up) + one(left_down, right_up) + one(left_up, right_down)


def in_vmem():
    return pl.BlockSpec(memory_space=pltpu.VMEM)


def kernel_call(body, out_shape, in_specs, out_specs, scratch=(), flops=0, moved=0):
    return pl.pallas_call(
        body,
        out_shape=out_shape,
        in_specs=in_specs,
        out_specs=out_specs,
        scratch_shapes=scratch,
        compiler_params=pltpu.CompilerParams(vmem_limit_bytes=VMEM_BYTES),
        cost_estimate=pl.CostEstimate(flops=flops, bytes_accessed=moved, transcendentals=0),
    )


def reduce_panel(places, solved, solved_other, window, pieces):
    rows, width = solved.shape
    unit = pieces[0].shape[0]
    unknowns = HALF_RING * unit
    each = rows // COLS

    def body(places_ref, solved_ref, other_ref, window_ref, *refs):
        own, one, two, three, four, out_ref, panel_out, panel, partial, sem = refs
        core = places_ref[0]

        def put(place, ref, at):
            start = pl.multiple_of(jnp.where(core == 0, HALF_RING - 1 - place, place) * unit, unit)
            panel[pl.ds(start, unit)] = ref[at * unit : (at + 1) * unit]

        put(0, own, 0)
        for step, ref in ((1, one), (2, two), (3, three)):
            put(2 * step, ref, 0)
            put(2 * step - 1, ref, 1)
        put(HALF_RING - 1, four, 0)
        copy = pltpu.make_async_copy(panel, panel_out, sem)
        copy.start()
        solved_pair = jnp.concatenate([solved_ref[...], other_ref[...]], axis=0)
        total = rounded_dot(halves(panel[...]), halves(solved_pair), ((1,), (1,)))
        partial[...] = -total.T
        lane = lax.broadcasted_iota(jnp.int32, (rows // 2, unknowns), 1)
        spread = jnp.concatenate([window_ref[...]] * HALF_RING, axis=1)
        first = pl.multiple_of(places_ref[1], rows // 2)
        partial[pl.ds(first, rows // 2)] += jnp.where(lane // unit == places_ref[2], spread, 0.0)
        for member in range(COLS):
            at = member * each
            out_ref[member, :each] = partial[at : at + each]
            out_ref[member, each:] = partial[rows + at : rows + at + each]
        copy.wait()

    return kernel_call(
        body,
        [
            jax.ShapeDtypeStruct((COLS, 2 * each, unknowns), jnp.float32),
            jax.ShapeDtypeStruct((unknowns, width), jnp.float32),
        ],
        [pl.BlockSpec(memory_space=pltpu.SMEM)] + [in_vmem()] * (3 + len(pieces)),
        [in_vmem(), pl.BlockSpec(memory_space=pltpu.MemorySpace.HBM)],
        scratch=[
            pltpu.VMEM((unknowns, width), jnp.float32),
            pltpu.VMEM((2 * rows, unknowns), jnp.float32),
            pltpu.SemaphoreType.DMA,
        ],
        flops=12 * rows * unknowns * width,
        moved=8 * unknowns * width,
    )(places, solved, solved_other, window, *pieces)


def panel_solve(residual, inverses, coupling):
    each, size = residual.shape[1:]
    deep = 16

    def body(residual_ref, inverses_ref, coupling_ref, out_ref, padded):
        def times(x, matrix, across):
            up, down = halves(x)
            contract = (((1,), (1 if across else 0,)), ((), ()))
            both = lax.dot_general(
                jnp.concatenate([up, down], axis=0),
                matrix[0],
                contract,
                preferred_element_type=jnp.float32,
            )
            rest = lax.dot_general(up, matrix[1], contract, preferred_element_type=jnp.float32)
            return both[:deep] + both[deep:] + rest

        padded[...] = jnp.zeros_like(padded)
        padded[0, :each] = residual_ref[0]
        padded[1, :each] = residual_ref[1]
        lead, follow, link = halves(inverses_ref[0]), halves(inverses_ref[1]), halves(coupling_ref[...])
        forward_lead = times(padded[0], lead, True)
        forward_next = times(padded[1] - times(forward_lead, link, True), follow, True)
        backward_next = times(forward_next, follow, False)
        backward_lead = times(forward_lead - times(backward_next, link, False), lead, False)
        out_ref[0] = backward_lead[:each]
        out_ref[1] = backward_next[:each]

    return kernel_call(
        body,
        jax.ShapeDtypeStruct(residual.shape, residual.dtype),
        [in_vmem()] * 3,
        in_vmem(),
        scratch=[pltpu.VMEM((2, deep, size), jnp.float32)],
        flops=36 * deep * size * size,
        moved=12 * size * size,
    )(residual, inverses, coupling)


def correct(solved, found, panel, panel_other):
    def body(solved_ref, found_ref, panel_ref, other_ref, out_ref):
        half = panel_ref.shape[0]
        contract = ((1,), (0,))
        total = rounded_dot(halves(found_ref[:, :half]), halves(panel_ref[...]), contract)
        total += rounded_dot(halves(found_ref[:, half:]), halves(other_ref[...]), contract)
        out_ref[...] = solved_ref[...] - total

    rows, width = solved.shape
    return kernel_call(
        body,
        jax.ShapeDtypeStruct(solved.shape, solved.dtype),
        [in_vmem()] * 4,
        in_vmem(),
        flops=36 * rows * found.shape[1] * width,
        moved=4 * found.shape[1] * width,
    )(solved, found, panel, panel_other)


def turn(blocks, start):
    twice = jnp.concatenate([blocks, blocks], axis=1)
    return lax.dynamic_slice_in_dim(twice, start, ROWS, 1)


def shards(factor, solved, rhs_window, inverses, coupling):
    rows, width = solved.shape
    part = factor.shape[1]
    row = lax.axis_index("row")
    col = lax.axis_index("col")
    plane, core = row // CORES, row % CORES

    own = factor.reshape(2 * part, width)
    both = jnp.concatenate([own, lax.ppermute(own, "row", core_swap())], axis=0)
    two = lax.ppermute(both, "row", apart(2))
    one = lax.ppermute(both, "row", apart(1))
    solved_other = lax.ppermute(solved, "row", core_swap())
    window = lax.ppermute(rhs_window, ("row", "col"), window_to_work())
    four = lax.ppermute(two[2 * part :], "row", apart(2))
    three = lax.ppermute(two, "row", apart(1))

    places = jnp.stack(
        [core, ((col // 16) ^ core) * rows + col // 8 % 2 * (rows // 2), col % 8]
    ).astype(jnp.int32)
    partial, panel = reduce_panel(
        places,
        solved,
        solved_other,
        window.reshape(rows // 2, 2 * part),
        [own, one, two, three, four],
    )
    panel_other = lax.ppermute(panel, "row", core_swap())

    each = rows // COLS
    spread = lax.all_to_all(partial, "col", 0, 0, tiled=True)
    residual = jnp.sum(spread, axis=0)
    residual_other = lax.ppermute(residual[each:], "row", core_swap())
    pair = jnp.stack([residual[:each], residual_other], axis=1)
    pair = jnp.where(core == 0, pair, pair[:, ::-1]).reshape(each, ROWS, 2, part)
    start = (HALF_RING - 1 - CORES * plane) % ROWS
    whole = jnp.transpose(turn(pair, start), (2, 0, 1, 3)).reshape(2, each, -1)
    found = panel_solve(whole, inverses, coupling).reshape(2, each, ROWS, part)
    found = turn(jnp.transpose(found, (1, 2, 0, 3)), (ROWS - start) % ROWS)
    found = found.reshape(each, CORES, -1)
    found = jnp.where(core == 0, found, found[:, ::-1]).reshape(each, -1)
    gathered = lax.all_to_all(
        jnp.broadcast_to(found, (COLS,) + found.shape), "col", 0, 0, tiled=True
    ).reshape(rows, -1)

    place = ring_place(col // 2, plane)
    slot = (place // HALF_RING ^ core) * HALF_RING + place % HALF_RING
    mine = lax.dynamic_slice(
        gathered, (col % 2 * (rows // 2), slot * 2 * part), (rows // 2, 2 * part)
    ).reshape(rows // 2, 2, part)
    owned = lax.ppermute(mine, ("row", "col"), work_to_window())
    return owned, correct(solved, gathered, panel, panel_other)


def solution(mesh):
    in_specs = (P(None, "row", "col"), P("row", "col"), P("col", None, "row"), P(), P())
    out_specs = (P("col", None, "row"), P("row", "col"))
    return jax.shard_map(shards, mesh=mesh, in_specs=in_specs, out_specs=out_specs, check_vma=False)
```

```python
import jax
import jax.numpy as jnp
from jax import lax
from jax.experimental import pallas as pl
from jax.experimental.pallas import tpu as pltpu
from jax.sharding import PartitionSpec as P

PLANES = 8
CORES = 2
ROWS = PLANES * CORES
HALF_RING = ROWS // 2
COLS = 32
MIB = 1024 * 1024


def core_swap():
    return [(row, row ^ 1) for row in range(ROWS)]


def apart(step):
    return [
        (plane * CORES + core, (plane + (step, -step)[core]) % PLANES * CORES + core)
        for plane in range(PLANES)
        for core in range(CORES)
    ]


def ring_place(unknown_row, plane):
    return (unknown_row - CORES * plane + HALF_RING - 1) % ROWS


def window_to_work():
    pairs = []
    for row in range(ROWS):
        for col in range(COLS):
            rhs_row, half = divmod(col, 2)
            plane, rhs_core = divmod(rhs_row, CORES)
            keeper, slot = divmod(ring_place(row, plane), HALF_RING)
            target = (rhs_core * 2 + half) * HALF_RING + slot
            pairs.append((row * COLS + col, (plane * CORES + keeper) * COLS + target))
    return pairs


def work_to_window():
    return [
        (row * COLS + col, (col // 2) * COLS + 2 * row + col % 2)
        for row in range(ROWS)
        for col in range(COLS)
    ]


def halves(x):
    high = x.astype(jnp.bfloat16)
    return high, (x - high.astype(jnp.float32)).astype(jnp.bfloat16)


def rounded_dot(left, right, contract):
    (left_up, left_down), (right_up, right_down) = left, right

    def one(x, y):
        return lax.dot_general(x, y, (contract, ((), ())), preferred_element_type=jnp.float32)

    return one(left_up, right_up) + one(left_down, right_up) + one(left_up, right_down)


def in_vmem():
    return pl.BlockSpec(memory_space=pltpu.VMEM)


def kernel_call(body, out_shape, in_specs, out_specs, scratch=(), mib=16, flops=0, moved=0):
    return pl.pallas_call(
        body,
        out_shape=out_shape,
        in_specs=in_specs,
        out_specs=out_specs,
        scratch_shapes=scratch,
        compiler_params=pltpu.CompilerParams(vmem_limit_bytes=mib * MIB),
        cost_estimate=pl.CostEstimate(flops=flops, bytes_accessed=moved, transcendentals=0),
    )


def position():
    row = lax.axis_index("row")
    return row // CORES, row % CORES


def anywhere():
    return pl.BlockSpec(memory_space=pl.ANY)


def join(one, two, arrivals=()):
    def body(one_ref, two_ref, *refs):
        out_ref, sems = refs[-2:]
        rows = one_ref.shape[0]
        first = pltpu.make_async_copy(one_ref, out_ref.at[:rows], sems.at[0])
        second = pltpu.make_async_copy(two_ref, out_ref.at[rows:], sems.at[1])
        first.start()
        second.start()
        first.wait()
        second.wait()

    shape = (one.shape[0] + two.shape[0], one.shape[1])
    return kernel_call(
        body,
        jax.ShapeDtypeStruct(shape, one.dtype),
        [anywhere()] * (2 + len(arrivals)),
        anywhere(),
        scratch=[pltpu.SemaphoreType.DMA((2,))],
        mib=2,
        moved=16 * one.size,
    )(one, two, *arrivals)


def second_half(both):
    def body(both_ref, out_ref, sem):
        copy = pltpu.make_async_copy(both_ref.at[out_ref.shape[0] :], out_ref, sem)
        copy.start()
        copy.wait()

    shape = (both.shape[0] // 2, both.shape[1])
    return kernel_call(
        body,
        jax.ShapeDtypeStruct(shape, both.dtype),
        [anywhere()],
        anywhere(),
        scratch=[pltpu.SemaphoreType.DMA],
        mib=2,
        moved=4 * both.size,
    )(both)


def reduce_panel(solved, solved_other, window, pieces):
    rows, width = solved.shape
    part = pieces[0].shape[0] // 2
    side = HALF_RING * part
    unknowns = 2 * side
    each = rows // COLS

    def body(solved_ref, other_ref, window_ref, *refs):
        own, one, two, three, four, out_ref, panel, partial = refs
        core, col = position()[1], lax.axis_index("col")

        def put(place, ref, at):
            first = jnp.where(core == 0, HALF_RING - 1 - place, place) * part
            for k in range(2):
                start = pl.multiple_of(first + k * side, part)
                panel[pl.ds(start, part)] = ref[(2 * at + k) * part : (2 * at + k + 1) * part]

        put(0, own, 0)
        for step, ref in ((1, one), (2, two), (3, three)):
            put(2 * step, ref, 0)
            put(2 * step - 1, ref, 1)
        put(HALF_RING - 1, four, 0)
        solved_pair = jnp.concatenate([solved_ref[...], other_ref[...]], axis=0)
        total = rounded_dot(halves(panel[...]), halves(solved_pair), ((1,), (1,)))
        partial[...] = -total.T
        spread = jnp.concatenate(
            [jnp.concatenate([window_ref[:, k]] * HALF_RING, axis=1) for k in range(2)], axis=1
        )
        lane = lax.broadcasted_iota(jnp.int32, spread.shape, 1)
        slot = lane % side // part
        first = ((col // (2 * HALF_RING)) ^ core) * rows + col // HALF_RING % 2 * (rows // 2)
        first = pl.multiple_of(first, rows // 2)
        partial[pl.ds(first, rows // 2)] += jnp.where(slot == col % HALF_RING, spread, 0.0)
        for member in range(COLS):
            at = member * each
            out_ref[member, :each] = partial[at : at + each]
            out_ref[member, each:] = partial[rows + at : rows + at + each]

    return kernel_call(
        body,
        [
            jax.ShapeDtypeStruct((COLS, 2 * each, unknowns), jnp.float32),
            jax.ShapeDtypeStruct((unknowns, width), jnp.float32),
        ],
        [in_vmem()] * (3 + len(pieces)),
        [in_vmem()] * 2,
        scratch=[pltpu.VMEM((2 * rows, unknowns), jnp.float32)],
        mib=32,
        flops=12 * rows * unknowns * width,
        moved=8 * unknowns * width,
    )(solved, solved_other, window, *pieces)


def panel_solve(residual, residual_other, inverses, coupling):
    each, size = residual.shape
    side = size // 2
    part = side // HALF_RING
    deep = 16

    def body(residual_ref, other_ref, inverses_ref, coupling_ref, out_ref, padded):
        plane, core = position()
        first = (CORES * plane + HALF_RING + 1 + core * HALF_RING) % ROWS

        def times(x, matrix, across):
            up, down = halves(x)
            contract = (((1,), (1 if across else 0,)), ((), ()))
            both = lax.dot_general(
                jnp.concatenate([up, down], axis=0),
                matrix[0],
                contract,
                preferred_element_type=jnp.float32,
            )
            rest = lax.dot_general(up, matrix[1], contract, preferred_element_type=jnp.float32)
            return both[:deep] + both[deep:] + rest

        padded[...] = jnp.zeros_like(padded)
        for k in range(2):
            padded[k, :each, :side] = residual_ref[:, k * side : (k + 1) * side]
            padded[k, :each, side:] = other_ref[:, k * side : (k + 1) * side]
        turned = [pltpu.roll(padded[k], first * part, 1) for k in range(2)]
        lead, follow, link = halves(inverses_ref[0]), halves(inverses_ref[1]), halves(coupling_ref[...])
        forward_lead = times(turned[0], lead, True)
        forward_next = times(turned[1] - times(forward_lead, link, True), follow, True)
        backward_next = times(forward_next, follow, False)
        backward_lead = times(forward_lead - times(backward_next, link, False), lead, False)
        back = (ROWS - first) % ROWS
        for k, found in enumerate((backward_lead, backward_next)):
            found = pltpu.roll(found, back * part, 1)[:each]
            out_ref[:, k * side : (k + 1) * side] = found[:, :side]
            out_ref[:, size + k * side : size + (k + 1) * side] = found[:, side:]

    return kernel_call(
        body,
        jax.ShapeDtypeStruct((each, 2 * size), residual.dtype),
        [in_vmem()] * 4,
        in_vmem(),
        scratch=[pltpu.VMEM((2, deep, size), jnp.float32)],
        flops=36 * deep * size * size,
        moved=12 * size * size,
    )(residual, residual_other, inverses, coupling)


def correct(solved, found, panel, panel_other):
    rows, width = solved.shape
    size = panel.shape[0]
    side = size // 2
    part = side // HALF_RING

    def body(solved_ref, found_ref, panel_ref, other_ref, out_ref, owned_ref):
        (plane, core), col = position(), lax.axis_index("col")
        total = jnp.zeros((rows, width), jnp.float32)
        for start, ref in ((0, panel_ref), (size, other_ref)):
            up, down = halves(found_ref[:, start : start + size])
            panel_up, panel_down = halves(ref[...])
            both = jnp.dot(
                jnp.concatenate([up, down], axis=0), panel_up, preferred_element_type=jnp.float32
            )
            rest = jnp.dot(up, panel_down, preferred_element_type=jnp.float32)
            total += both[:rows] + both[rows:] + rest
        out_ref[...] = solved_ref[...] - total
        place = (col // 2 - CORES * plane + ROWS + HALF_RING - 1) % ROWS
        keeper = (place // HALF_RING) ^ core
        first = pl.multiple_of(col % 2 * (rows // 2), rows // 2)
        back = (HALF_RING - place % HALF_RING) % HALF_RING
        for k in range(2):
            start = pl.multiple_of(keeper * size + k * side, side)
            block = found_ref[pl.ds(first, rows // 2), pl.ds(start, side)]
            owned_ref[:, k] = pltpu.roll(block, back * part, 1)[:, :part]

    return kernel_call(
        body,
        [
            jax.ShapeDtypeStruct(solved.shape, solved.dtype),
            jax.ShapeDtypeStruct((rows // 2, 2, part), solved.dtype),
        ],
        [in_vmem()] * 4,
        [in_vmem()] * 2,
        flops=36 * rows * found.shape[1] * width,
        moved=4 * found.shape[1] * width,
    )(solved, found, panel, panel_other)


def shards(factor, solved, rhs_window, inverses, coupling):
    rows, width = solved.shape
    part = factor.shape[1]

    own = factor.reshape(2 * part, width)
    other = lax.ppermute(own, "row", core_swap())
    two = lax.ppermute(join(own, other), "row", apart(2))
    solved_other = lax.ppermute(solved, "row", core_swap())
    window = lax.ppermute(rhs_window, ("row", "col"), window_to_work())
    one = lax.ppermute(join(own, other, (solved_other, window)), "row", apart(1))
    three = lax.ppermute(two, "row", apart(1))
    four = lax.ppermute(second_half(two), "row", apart(2))

    partial, panel = reduce_panel(
        solved, solved_other, window, [own, one, two, three, four]
    )
    panel_other = lax.ppermute(panel, "row", core_swap())

    each = rows // COLS
    residual = jnp.sum(lax.all_to_all(partial, "col", 0, 0, tiled=True), axis=0)
    residual_other = lax.ppermute(residual[each:], "row", core_swap())
    found = panel_solve(residual[:each], residual_other, inverses, coupling)
    gathered = lax.all_to_all(
        jnp.broadcast_to(found, (COLS,) + found.shape), "col", 0, 0, tiled=True
    ).reshape(rows, -1)
    updated, mine = correct(solved, gathered, panel, panel_other)
    owned = lax.ppermute(mine, ("row", "col"), work_to_window())
    return owned, updated


def solution(mesh):
    in_specs = (P(None, "row", "col"), P("row", "col"), P("col", None, "row"), P(), P())
    out_specs = (P("col", None, "row"), P("row", "col"))
    return jax.shard_map(shards, mesh=mesh, in_specs=in_specs, out_specs=out_specs, check_vma=False)
```

```python
import jax
import jax.numpy as jnp
from jax import lax
from jax.experimental import pallas as pl
from jax.experimental.pallas import tpu as pltpu
from jax.sharding import PartitionSpec as P

PLANES = 8
CORES = 2
ROWS = PLANES * CORES
HALF_RING = ROWS // 2
COLS = 32
MIB = 1024 * 1024


def core_swap():
    return [(row, row ^ 1) for row in range(ROWS)]


def apart(step):
    return [
        (plane * CORES + core, (plane + (step, -step)[core]) % PLANES * CORES + core)
        for plane in range(PLANES)
        for core in range(CORES)
    ]


def ring_place(unknown_row, plane):
    return (unknown_row - CORES * plane + HALF_RING - 1) % ROWS


def window_to_work():
    pairs = []
    for row in range(ROWS):
        for col in range(COLS):
            rhs_row, half = divmod(col, 2)
            plane, rhs_core = divmod(rhs_row, CORES)
            keeper, slot = divmod(ring_place(row, plane), HALF_RING)
            target = (rhs_core * 2 + half) * HALF_RING + slot
            pairs.append((row * COLS + col, (plane * CORES + keeper) * COLS + target))
    return pairs


def work_to_window():
    return [
        (row * COLS + col, (col // 2) * COLS + 2 * row + col % 2)
        for row in range(ROWS)
        for col in range(COLS)
    ]


def halves(x):
    high = x.astype(jnp.bfloat16)
    return high, (x - high.astype(jnp.float32)).astype(jnp.bfloat16)


def rounded_dot(left, right, contract):
    (left_up, left_down), (right_up, right_down) = left, right

    def one(x, y):
        return lax.dot_general(x, y, (contract, ((), ())), preferred_element_type=jnp.float32)

    return one(left_up, right_up) + one(left_down, right_up) + one(left_up, right_down)


def in_vmem():
    return pl.BlockSpec(memory_space=pltpu.VMEM)


def kernel_call(body, out_shape, in_specs, out_specs, scratch=(), mib=16, flops=0, moved=0):
    return pl.pallas_call(
        body,
        out_shape=out_shape,
        in_specs=in_specs,
        out_specs=out_specs,
        scratch_shapes=scratch,
        compiler_params=pltpu.CompilerParams(vmem_limit_bytes=mib * MIB),
        cost_estimate=pl.CostEstimate(flops=flops, bytes_accessed=moved, transcendentals=0),
    )


def position():
    row = lax.axis_index("row")
    return row // CORES, row % CORES


def anywhere():
    return pl.BlockSpec(memory_space=pl.ANY)


def join(one, two):
    def body(one_ref, two_ref, out_ref, sems):
        rows = one_ref.shape[0]
        first = pltpu.make_async_copy(one_ref, out_ref.at[:rows], sems.at[0])
        second = pltpu.make_async_copy(two_ref, out_ref.at[rows:], sems.at[1])
        first.start()
        second.start()
        first.wait()
        second.wait()

    shape = (one.shape[0] + two.shape[0], one.shape[1])
    return kernel_call(
        body,
        jax.ShapeDtypeStruct(shape, one.dtype),
        [anywhere()] * 2,
        anywhere(),
        scratch=[pltpu.SemaphoreType.DMA((2,))],
        mib=2,
        moved=16 * one.size,
    )(one, two)


def after(block, arrivals):
    def body(*refs):
        del refs

    return pl.pallas_call(
        body,
        out_shape=jax.ShapeDtypeStruct(block.shape, block.dtype),
        in_specs=[anywhere()] * (1 + len(arrivals)),
        out_specs=anywhere(),
        input_output_aliases={0: 0},
        compiler_params=pltpu.CompilerParams(vmem_limit_bytes=MIB),
    )(block, *arrivals)


def reduce_panel(solved, solved_other, window, pieces):
    rows, width = solved.shape
    part = pieces[0].shape[0] // 2
    side = HALF_RING * part
    unknowns = 2 * side
    each = rows // COLS

    def body(solved_ref, other_ref, window_ref, *refs):
        own, one, *pairs, four, out_ref, panel, partial = refs
        core, col = position()[1], lax.axis_index("col")

        def put(place, ref, at):
            first = jnp.where(core == 0, HALF_RING - 1 - place, place) * part
            for k in range(2):
                start = pl.multiple_of(first + k * side, part)
                panel[pl.ds(start, part)] = ref[(2 * at + k) * part : (2 * at + k + 1) * part]

        put(0, own, 0)
        put(2, one, 0)
        put(1, one, 1)
        for place, ref in zip((4, 3, 6, 5), pairs):
            put(place, ref, 0)
        put(HALF_RING - 1, four, 0)
        solved_pair = jnp.concatenate([solved_ref[...], other_ref[...]], axis=0)
        total = rounded_dot(halves(panel[...]), halves(solved_pair), ((1,), (1,)))
        partial[...] = -total.T
        spread = jnp.concatenate(
            [jnp.concatenate([window_ref[:, k]] * HALF_RING, axis=1) for k in range(2)], axis=1
        )
        lane = lax.broadcasted_iota(jnp.int32, spread.shape, 1)
        slot = lane % side // part
        first = ((col // (2 * HALF_RING)) ^ core) * rows + col // HALF_RING % 2 * (rows // 2)
        first = pl.multiple_of(first, rows // 2)
        partial[pl.ds(first, rows // 2)] += jnp.where(slot == col % HALF_RING, spread, 0.0)
        for member in range(COLS):
            at = member * each
            out_ref[member, :each] = partial[at : at + each]
            out_ref[member, each:] = partial[rows + at : rows + at + each]

    return kernel_call(
        body,
        [
            jax.ShapeDtypeStruct((COLS, 2 * each, unknowns), jnp.float32),
            jax.ShapeDtypeStruct((unknowns, width), jnp.float32),
        ],
        [in_vmem()] * (3 + len(pieces)),
        [in_vmem()] * 2,
        scratch=[pltpu.VMEM((2 * rows, unknowns), jnp.float32)],
        mib=32,
        flops=12 * rows * unknowns * width,
        moved=8 * unknowns * width,
    )(solved, solved_other, window, *pieces)


def panel_solve(residual, residual_other, inverses, coupling):
    each, size = residual.shape
    side = size // 2
    part = side // HALF_RING
    deep = 16

    def body(residual_ref, other_ref, inverses_ref, coupling_ref, out_ref, padded):
        plane, core = position()
        first = (CORES * plane + HALF_RING + 1 + core * HALF_RING) % ROWS

        def times(x, matrix, across):
            up, down = halves(x)
            contract = (((1,), (1 if across else 0,)), ((), ()))
            both = lax.dot_general(
                jnp.concatenate([up, down], axis=0),
                matrix[0],
                contract,
                preferred_element_type=jnp.float32,
            )
            rest = lax.dot_general(up, matrix[1], contract, preferred_element_type=jnp.float32)
            return both[:deep] + both[deep:] + rest

        padded[...] = jnp.zeros_like(padded)
        for k in range(2):
            padded[k, :each, :side] = residual_ref[:, k * side : (k + 1) * side]
            padded[k, :each, side:] = other_ref[:, k * side : (k + 1) * side]
        turned = [pltpu.roll(padded[k], first * part, 1) for k in range(2)]
        lead, follow, link = halves(inverses_ref[0]), halves(inverses_ref[1]), halves(coupling_ref[...])
        forward_lead = times(turned[0], lead, True)
        forward_next = times(turned[1] - times(forward_lead, link, True), follow, True)
        backward_next = times(forward_next, follow, False)
        backward_lead = times(forward_lead - times(backward_next, link, False), lead, False)
        back = (ROWS - first) % ROWS
        for k, found in enumerate((backward_lead, backward_next)):
            found = pltpu.roll(found, back * part, 1)[:each]
            out_ref[:, k * side : (k + 1) * side] = found[:, :side]
            out_ref[:, size + k * side : size + (k + 1) * side] = found[:, side:]

    return kernel_call(
        body,
        jax.ShapeDtypeStruct((each, 2 * size), residual.dtype),
        [in_vmem()] * 4,
        in_vmem(),
        scratch=[pltpu.VMEM((2, deep, size), jnp.float32)],
        flops=36 * deep * size * size,
        moved=12 * size * size,
    )(residual, residual_other, inverses, coupling)


def correct(solved, found, panel, panel_other):
    rows, width = solved.shape
    size = panel.shape[0]
    side = size // 2
    part = side // HALF_RING

    def body(solved_ref, found_ref, panel_ref, other_ref, out_ref, owned_ref):
        (plane, core), col = position(), lax.axis_index("col")
        total = jnp.zeros((rows, width), jnp.float32)
        for start, ref in ((0, panel_ref), (size, other_ref)):
            up, down = halves(found_ref[:, start : start + size])
            panel_up, panel_down = halves(ref[...])
            both = jnp.dot(
                jnp.concatenate([up, down], axis=0), panel_up, preferred_element_type=jnp.float32
            )
            rest = jnp.dot(up, panel_down, preferred_element_type=jnp.float32)
            total += both[:rows] + both[rows:] + rest
        out_ref[...] = solved_ref[...] - total
        place = (col // 2 - CORES * plane + ROWS + HALF_RING - 1) % ROWS
        keeper = (place // HALF_RING) ^ core
        first = pl.multiple_of(col % 2 * (rows // 2), rows // 2)
        back = (HALF_RING - place % HALF_RING) % HALF_RING
        for k in range(2):
            start = pl.multiple_of(keeper * size + k * side, side)
            block = found_ref[pl.ds(first, rows // 2), pl.ds(start, side)]
            owned_ref[:, k] = pltpu.roll(block, back * part, 1)[:, :part]

    return kernel_call(
        body,
        [
            jax.ShapeDtypeStruct(solved.shape, solved.dtype),
            jax.ShapeDtypeStruct((rows // 2, 2, part), solved.dtype),
        ],
        [in_vmem()] * 4,
        [in_vmem()] * 2,
        flops=36 * rows * found.shape[1] * width,
        moved=4 * found.shape[1] * width,
    )(solved, found, panel, panel_other)


def shards(factor, solved, rhs_window, inverses, coupling):
    rows, width = solved.shape
    part = factor.shape[1]

    own = factor.reshape(2 * part, width)
    two_own = lax.ppermute(own, "row", apart(2))
    other = lax.ppermute(own, "row", core_swap())
    two_other = lax.ppermute(other, "row", apart(2))
    one = lax.ppermute(join(own, other), "row", apart(1))
    three_own = lax.ppermute(two_own, "row", apart(1))
    solved_other = lax.ppermute(solved, "row", core_swap())
    window = lax.ppermute(rhs_window, ("row", "col"), window_to_work())
    two_other = after(two_other, (solved_other, window))
    four = lax.ppermute(two_other, "row", apart(2))
    three_other = lax.ppermute(two_other, "row", apart(1))

    partial, panel = reduce_panel(
        solved,
        solved_other,
        window,
        [own, one, two_own, two_other, three_own, three_other, four],
    )
    panel_other = lax.ppermute(panel, "row", core_swap())

    each = rows // COLS
    residual = jnp.sum(lax.all_to_all(partial, "col", 0, 0, tiled=True), axis=0)
    residual_other = lax.ppermute(residual[each:], "row", core_swap())
    found = panel_solve(residual[:each], residual_other, inverses, coupling)
    gathered = lax.all_to_all(
        jnp.broadcast_to(found, (COLS,) + found.shape), "col", 0, 0, tiled=True
    ).reshape(rows, -1)
    updated, mine = correct(solved, gathered, panel, panel_other)
    owned = lax.ppermute(mine, ("row", "col"), work_to_window())
    return owned, updated


def solution(mesh):
    in_specs = (P(None, "row", "col"), P("row", "col"), P("col", None, "row"), P(), P())
    out_specs = (P("col", None, "row"), P("row", "col"))
    return jax.shard_map(shards, mesh=mesh, in_specs=in_specs, out_specs=out_specs, check_vma=False)
```

```python
import jax
import jax.numpy as jnp
from jax import lax
from jax.experimental import pallas as pl
from jax.experimental.pallas import tpu as pltpu
from jax.sharding import PartitionSpec as P

PLANES = 8
CORES = 2
ROWS = PLANES * CORES
HALF_RING = ROWS // 2
COLS = 32
TAIL = 8
MIB = 1024 * 1024


def core_swap():
    return [(row, row ^ 1) for row in range(ROWS)]


def apart(step):
    return [
        (plane * CORES + core, (plane + (step, -step)[core]) % PLANES * CORES + core)
        for plane in range(PLANES)
        for core in range(CORES)
    ]


def work_to_window():
    return [
        (row * COLS + col, (col // 2) * COLS + 2 * row + col % 2)
        for row in range(ROWS)
        for col in range(COLS)
    ]


def halves(x):
    high = x.astype(jnp.bfloat16)
    return high, (x - high.astype(jnp.float32)).astype(jnp.bfloat16)


def rounded_dot(left, right, contract):
    (left_up, left_down), (right_up, right_down) = left, right

    def one(x, y):
        return lax.dot_general(x, y, (contract, ((), ())), preferred_element_type=jnp.float32)

    return one(left_up, right_up) + one(left_down, right_up) + one(left_up, right_down)


def in_vmem():
    return pl.BlockSpec(memory_space=pltpu.VMEM)


def kernel_call(body, out_shape, in_specs, out_specs, scratch=(), mib=16, flops=0, moved=0):
    return pl.pallas_call(
        body,
        out_shape=out_shape,
        in_specs=in_specs,
        out_specs=out_specs,
        scratch_shapes=scratch,
        compiler_params=pltpu.CompilerParams(vmem_limit_bytes=mib * MIB),
        cost_estimate=pl.CostEstimate(flops=flops, bytes_accessed=moved, transcendentals=0),
    )


def position():
    row = lax.axis_index("row")
    return row // CORES, row % CORES


def anywhere():
    return pl.BlockSpec(memory_space=pl.ANY)


def with_window(block, rhs_window):
    rows, width = block.shape

    def body(block_ref, window_ref, out_ref):
        out_ref[:rows] = block_ref[...]
        out_ref[rows:] = jnp.zeros((TAIL, width), jnp.float32)
        count, _, part = window_ref.shape
        for k in range(2):
            turned = window_ref[:, k].T
            for g in range(part // TAIL):
                at = (k * (part // TAIL) + g) * count
                out_ref[rows:, at : at + count] = turned[g * TAIL : (g + 1) * TAIL]

    return kernel_call(
        body,
        jax.ShapeDtypeStruct((rows + TAIL, width), block.dtype),
        [in_vmem()] * 2,
        in_vmem(),
        moved=8 * block.size,
    )(block, rhs_window)


def join(one, two, three):
    def body(one_ref, two_ref, three_ref, out_ref, copy_ref, sems):
        rows = one_ref.shape[0]
        copies = [
            pltpu.make_async_copy(one_ref, out_ref.at[:rows], sems.at[0]),
            pltpu.make_async_copy(two_ref, out_ref.at[rows:], sems.at[1]),
            pltpu.make_async_copy(three_ref, copy_ref, sems.at[2]),
        ]
        for copy in copies:
            copy.start()
        for copy in copies:
            copy.wait()

    shape = (one.shape[0] + two.shape[0], one.shape[1])
    return kernel_call(
        body,
        [
            jax.ShapeDtypeStruct(shape, one.dtype),
            jax.ShapeDtypeStruct(three.shape, three.dtype),
        ],
        [anywhere()] * 3,
        [anywhere()] * 2,
        scratch=[pltpu.SemaphoreType.DMA((3,))],
        mib=2,
        moved=24 * one.size,
    )(one, two, three)


def after(block, arrivals):
    def body(*refs):
        del refs

    return pl.pallas_call(
        body,
        out_shape=jax.ShapeDtypeStruct(block.shape, block.dtype),
        in_specs=[anywhere()] * (1 + len(arrivals)),
        out_specs=anywhere(),
        input_output_aliases={0: 0},
        compiler_params=pltpu.CompilerParams(vmem_limit_bytes=MIB),
    )(block, *arrivals)


def reduce_panel(solved, solved_other, both, one, others):
    rows, width = solved.shape
    block = both.shape[0] // 2
    part = (block - TAIL) // 2
    side = HALF_RING * part
    unknowns = 2 * side
    each = rows // COLS
    count = rows // 2

    def body(solved_ref, other_ref, both_ref, one_ref, *refs):
        *block_refs, out_ref, panel, window, partial = refs
        (plane, core), col = position(), lax.axis_index("col")

        def put(place, ref, at):
            base = at * block
            first = jnp.where(core == 0, HALF_RING - 1 - place, place) * part
            for k in range(2):
                start = pl.multiple_of(first + k * side, part)
                panel[pl.ds(start, part)] = ref[base + k * part : base + (k + 1) * part]
                for g in range(part // TAIL):
                    lanes = (k * (part // TAIL) + g) * count
                    window[pl.ds(start + g * TAIL, TAIL)] = ref[
                        base + 2 * part : base + block, lanes : lanes + count
                    ]

        put(0, both_ref, 0)
        put(2, one_ref, 0)
        put(1, one_ref, 1)
        for place, ref in zip((4, 3, 6, 5, 7), block_refs):
            put(place, ref, 0)
        solved_pair = jnp.concatenate([solved_ref[...], other_ref[...]], axis=0)
        total = rounded_dot(halves(panel[...]), halves(solved_pair), ((1,), (1,)))
        spread = jnp.concatenate([window[...]] * (2 * rows // count), axis=1)
        lane = lax.broadcasted_iota(jnp.int32, spread.shape, 1)
        mine = 2 * ((col // 2 % CORES) ^ core) + col % 2
        mine = jnp.where(plane == col // (2 * CORES), mine, -1)
        partial[...] = (jnp.where(lane // count == mine, spread, 0.0) - total).T
        for member in range(COLS):
            at = member * each
            out_ref[member, :each] = partial[at : at + each]
            out_ref[member, each:] = partial[rows + at : rows + at + each]

    return kernel_call(
        body,
        [
            jax.ShapeDtypeStruct((COLS, 2 * each, unknowns), jnp.float32),
            jax.ShapeDtypeStruct((unknowns, width), jnp.float32),
        ],
        [in_vmem()] * (4 + len(others)),
        [in_vmem()] * 2,
        scratch=[
            pltpu.VMEM((unknowns, count), jnp.float32),
            pltpu.VMEM((2 * rows, unknowns), jnp.float32),
        ],
        mib=32,
        flops=12 * rows * unknowns * width,
        moved=8 * unknowns * width,
    )(solved, solved_other, both, one, *others)


def panel_solve(residual, residual_other, inverses, coupling):
    each, size = residual.shape
    side = size // 2
    part = side // HALF_RING
    deep = 16

    def body(residual_ref, other_ref, inverses_ref, coupling_ref, out_ref, padded):
        plane, core = position()
        first = (CORES * plane + HALF_RING + 1 + core * HALF_RING) % ROWS

        def times(x, matrix, across):
            up, down = halves(x)
            contract = (((1,), (1 if across else 0,)), ((), ()))
            both = lax.dot_general(
                jnp.concatenate([up, down], axis=0),
                matrix[0],
                contract,
                preferred_element_type=jnp.float32,
            )
            rest = lax.dot_general(up, matrix[1], contract, preferred_element_type=jnp.float32)
            return both[:deep] + both[deep:] + rest

        padded[...] = jnp.zeros_like(padded)
        for k in range(2):
            padded[k, :each, :side] = residual_ref[:, k * side : (k + 1) * side]
            padded[k, :each, side:] = other_ref[:, k * side : (k + 1) * side]
        turned = [pltpu.roll(padded[k], first * part, 1) for k in range(2)]
        lead, follow, link = halves(inverses_ref[0]), halves(inverses_ref[1]), halves(coupling_ref[...])
        forward_lead = times(turned[0], lead, True)
        forward_next = times(turned[1] - times(forward_lead, link, True), follow, True)
        backward_next = times(forward_next, follow, False)
        backward_lead = times(forward_lead - times(backward_next, link, False), lead, False)
        back = (ROWS - first) % ROWS
        for k, found in enumerate((backward_lead, backward_next)):
            found = pltpu.roll(found, back * part, 1)[:each]
            out_ref[:, k * side : (k + 1) * side] = found[:, :side]
            out_ref[:, size + k * side : size + (k + 1) * side] = found[:, side:]

    return kernel_call(
        body,
        jax.ShapeDtypeStruct((each, 2 * size), residual.dtype),
        [in_vmem()] * 4,
        in_vmem(),
        scratch=[pltpu.VMEM((2, deep, size), jnp.float32)],
        flops=36 * deep * size * size,
        moved=12 * size * size,
    )(residual, residual_other, inverses, coupling)


def correct(solved, found, panel, panel_other):
    rows, width = solved.shape
    size = panel.shape[0]
    side = size // 2
    part = side // HALF_RING

    def body(solved_ref, found_ref, panel_ref, other_ref, out_ref, owned_ref):
        (plane, core), col = position(), lax.axis_index("col")
        total = jnp.zeros((rows, width), jnp.float32)
        for start, ref in ((0, panel_ref), (size, other_ref)):
            up, down = halves(found_ref[:, start : start + size])
            panel_up, panel_down = halves(ref[...])
            both = jnp.dot(
                jnp.concatenate([up, down], axis=0), panel_up, preferred_element_type=jnp.float32
            )
            rest = jnp.dot(up, panel_down, preferred_element_type=jnp.float32)
            total += both[:rows] + both[rows:] + rest
        out_ref[...] = solved_ref[...] - total
        place = (col // 2 - CORES * plane + ROWS + HALF_RING - 1) % ROWS
        keeper = (place // HALF_RING) ^ core
        first = pl.multiple_of(col % 2 * (rows // 2), rows // 2)
        back = (HALF_RING - place % HALF_RING) % HALF_RING
        for k in range(2):
            start = pl.multiple_of(keeper * size + k * side, side)
            block = found_ref[pl.ds(first, rows // 2), pl.ds(start, side)]
            owned_ref[:, k] = pltpu.roll(block, back * part, 1)[:, :part]

    return kernel_call(
        body,
        [
            jax.ShapeDtypeStruct(solved.shape, solved.dtype),
            jax.ShapeDtypeStruct((rows // 2, 2, part), solved.dtype),
        ],
        [in_vmem()] * 4,
        [in_vmem()] * 2,
        flops=36 * rows * found.shape[1] * width,
        moved=4 * found.shape[1] * width,
    )(solved, found, panel, panel_other)


def shards(factor, solved, rhs_window, inverses, coupling):
    rows, width = solved.shape
    part = factor.shape[1]

    own = with_window(factor.reshape(2 * part, width), rhs_window)
    two_own = lax.ppermute(own, "row", apart(2))
    other = lax.ppermute(own, "row", core_swap())
    two_other = lax.ppermute(other, "row", apart(2))
    both, solved_own = join(own, other, solved)
    one = lax.ppermute(both, "row", apart(1))
    three_own = lax.ppermute(two_own, "row", apart(1))
    solved_other = lax.ppermute(solved, "row", core_swap())
    two_other = after(two_other, (solved_other,))
    four = lax.ppermute(two_other, "row", apart(2))
    three_other = lax.ppermute(two_other, "row", apart(1))
    partial, panel = reduce_panel(
        solved_own, solved_other, both, one, [two_own, two_other, three_own, three_other, four]
    )

    panel_other = lax.ppermute(panel, "row", core_swap())

    each = rows // COLS
    residual = jnp.sum(lax.all_to_all(partial, "col", 0, 0, tiled=True), axis=0)
    residual_other = lax.ppermute(residual[each:], "row", core_swap())
    found = panel_solve(residual[:each], residual_other, inverses, coupling)
    gathered = lax.all_to_all(
        jnp.broadcast_to(found, (COLS,) + found.shape), "col", 0, 0, tiled=True
    ).reshape(rows, -1)
    updated, mine = correct(solved, gathered, panel, panel_other)
    owned = lax.ppermute(mine, ("row", "col"), work_to_window())
    return owned, updated


def solution(mesh):
    in_specs = (P(None, "row", "col"), P("row", "col"), P("col", None, "row"), P(), P())
    out_specs = (P("col", None, "row"), P("row", "col"))
    return jax.shard_map(shards, mesh=mesh, in_specs=in_specs, out_specs=out_specs, check_vma=False)
```

```python
import jax
import jax.numpy as jnp
from jax import lax
from jax.experimental import pallas as pl
from jax.experimental.pallas import tpu as pltpu
from jax.sharding import PartitionSpec as P

PLANES = 8
CORES = 2
ROWS = PLANES * CORES
HALF_RING = ROWS // 2
COLS = 32
TAIL = 8
LANES = 256
MIB = 1024 * 1024


def core_swap():
    return [(row, row ^ 1) for row in range(ROWS)]


def apart(step):
    return [
        (plane * CORES + core, (plane + (step, -step)[core]) % PLANES * CORES + core)
        for plane in range(PLANES)
        for core in range(CORES)
    ]


def work_to_window():
    return [
        (row * COLS + col, (col // 2) * COLS + 2 * row + col % 2)
        for row in range(ROWS)
        for col in range(COLS)
    ]


def halves(x):
    high = x.astype(jnp.bfloat16)
    return high, (x - high.astype(jnp.float32)).astype(jnp.bfloat16)


def rounded_dot(left, right, contract):
    (left_up, left_down), (right_up, right_down) = left, right

    def one(x, y):
        return lax.dot_general(x, y, (contract, ((), ())), preferred_element_type=jnp.float32)

    return one(left_up, right_up) + one(left_down, right_up) + one(left_up, right_down)


def in_vmem():
    return pl.BlockSpec(memory_space=pltpu.VMEM)


def kernel_call(body, out_shape, in_specs, out_specs, scratch=(), mib=16, flops=0, moved=0):
    return pl.pallas_call(
        body,
        out_shape=out_shape,
        in_specs=in_specs,
        out_specs=out_specs,
        scratch_shapes=scratch,
        compiler_params=pltpu.CompilerParams(vmem_limit_bytes=mib * MIB),
        cost_estimate=pl.CostEstimate(flops=flops, bytes_accessed=moved, transcendentals=0),
    )


def position():
    row = lax.axis_index("row")
    return row // CORES, row % CORES


def anywhere():
    return pl.BlockSpec(memory_space=pl.ANY)


def in_hbm():
    return pl.BlockSpec(memory_space=pltpu.MemorySpace.HBM)


def with_window(factor, rhs_window):
    panels, part, width = factor.shape
    rows = panels * part
    groups = width // LANES

    def body(factor_ref, window_ref, out_ref):
        count = window_ref.shape[0]
        for k in range(panels):
            turned = window_ref[:, k].T
            for g in range(part // TAIL):
                at = (k * (part // TAIL) + g) * count
                out_ref[groups * rows :, at : at + count] = turned[g * TAIL : (g + 1) * TAIL]
            for g in range(groups):
                at = g * rows + k * part
                out_ref[at : at + part] = factor_ref[k, :, g * LANES : (g + 1) * LANES]

    return kernel_call(
        body,
        jax.ShapeDtypeStruct((groups * rows + TAIL, LANES), factor.dtype),
        [in_vmem()] * 2,
        in_vmem(),
        mib=56,
        moved=8 * factor.size,
    )(factor, rhs_window)


def join(one, two, arrivals=()):
    def body(one_ref, two_ref, *refs):
        out_ref, sems = refs[-2:]
        rows = one_ref.shape[0]
        first = pltpu.make_async_copy(one_ref, out_ref.at[:rows], sems.at[0])
        second = pltpu.make_async_copy(two_ref, out_ref.at[rows:], sems.at[1])
        first.start()
        second.start()
        first.wait()
        second.wait()

    shape = (one.shape[0] + two.shape[0], one.shape[1])
    return kernel_call(
        body,
        jax.ShapeDtypeStruct(shape, one.dtype),
        [anywhere()] * (2 + len(arrivals)),
        anywhere(),
        scratch=[pltpu.SemaphoreType.DMA((2,))],
        mib=2,
        moved=16 * one.size,
    )(one, two, *arrivals)


def anywhere():
    return pl.BlockSpec(memory_space=pl.ANY)


def reduce_panel(solved, solved_other, pairs, last):
    rows, width = solved.shape
    groups = width // LANES
    block = last.shape[0]
    part = (block - TAIL) // (2 * groups)
    side = HALF_RING * part
    unknowns = 2 * side
    each = rows // COLS
    count = rows // 2

    def body(solved_ref, other_ref, *refs):
        *pair_refs, last_ref, out_ref, panel, window, partial = refs
        (plane, core), col = position(), lax.axis_index("col")

        def put(place, ref, at):
            base = at * block
            first = jnp.where(core == 0, HALF_RING - 1 - place, place) * part
            for k in range(2):
                start = pl.multiple_of(first + k * side, part)
                for g in range(groups):
                    row = base + (2 * g + k) * part
                    panel[pl.ds(start, part), g * LANES : (g + 1) * LANES] = ref[row : row + part]
                for g in range(part // TAIL):
                    lanes = (k * (part // TAIL) + g) * count
                    window[pl.ds(start + g * TAIL, TAIL)] = ref[
                        base + block - TAIL : base + block, lanes : lanes + count
                    ]

        put(0, pair_refs[0], 0)
        for step, ref in enumerate(pair_refs[1:], start=1):
            put(2 * step, ref, 0)
            put(2 * step - 1, ref, 1)
        put(HALF_RING - 1, last_ref, 0)
        solved_pair = jnp.concatenate([solved_ref[...], other_ref[...]], axis=0)
        total = rounded_dot(halves(panel[...]), halves(solved_pair), ((1,), (1,)))
        spread = jnp.concatenate([window[...]] * (2 * rows // count), axis=1)
        lane = lax.broadcasted_iota(jnp.int32, spread.shape, 1)
        mine = 2 * ((col // 2 % CORES) ^ core) + col % 2
        mine = jnp.where(plane == col // (2 * CORES), mine, -1)
        partial[...] = (jnp.where(lane // count == mine, spread, 0.0) - total).T
        for member in range(COLS):
            at = member * each
            out_ref[member, :each] = partial[at : at + each]
            out_ref[member, each:] = partial[rows + at : rows + at + each]

    return kernel_call(
        body,
        [
            jax.ShapeDtypeStruct((COLS, 2 * each, unknowns), jnp.float32),
            jax.ShapeDtypeStruct((unknowns, width), jnp.float32),
        ],
        [in_vmem()] * (3 + len(pairs)),
        [in_vmem()] * 2,
        scratch=[
            pltpu.VMEM((unknowns, count), jnp.float32),
            pltpu.VMEM((2 * rows, unknowns), jnp.float32),
        ],
        mib=32,
        flops=12 * rows * unknowns * width,
        moved=8 * unknowns * width,
    )(solved, solved_other, *pairs, last)


def panel_solve(residual, residual_other, inverses, coupling):
    each, size = residual.shape
    side = size // 2
    part = side // HALF_RING
    deep = 16

    def body(residual_ref, other_ref, inverses_ref, coupling_ref, out_ref, padded):
        plane, core = position()
        first = (CORES * plane + HALF_RING + 1 + core * HALF_RING) % ROWS

        def times(x, matrix, across):
            up, down = halves(x)
            contract = (((1,), (1 if across else 0,)), ((), ()))
            both = lax.dot_general(
                jnp.concatenate([up, down], axis=0),
                matrix[0],
                contract,
                preferred_element_type=jnp.float32,
            )
            rest = lax.dot_general(up, matrix[1], contract, preferred_element_type=jnp.float32)
            return both[:deep] + both[deep:] + rest

        padded[...] = jnp.zeros_like(padded)
        for k in range(2):
            padded[k, :each, :side] = residual_ref[:, k * side : (k + 1) * side]
            padded[k, :each, side:] = other_ref[:, k * side : (k + 1) * side]
        turned = [pltpu.roll(padded[k], first * part, 1) for k in range(2)]
        lead, follow, link = halves(inverses_ref[0]), halves(inverses_ref[1]), halves(coupling_ref[...])
        forward_lead = times(turned[0], lead, True)
        forward_next = times(turned[1] - times(forward_lead, link, True), follow, True)
        backward_next = times(forward_next, follow, False)
        backward_lead = times(forward_lead - times(backward_next, link, False), lead, False)
        back = (ROWS - first) % ROWS
        for k, found in enumerate((backward_lead, backward_next)):
            found = pltpu.roll(found, back * part, 1)[:each]
            out_ref[:, k * side : (k + 1) * side] = found[:, :side]
            out_ref[:, size + k * side : size + (k + 1) * side] = found[:, side:]

    return kernel_call(
        body,
        jax.ShapeDtypeStruct((each, 2 * size), residual.dtype),
        [in_vmem()] * 4,
        in_vmem(),
        scratch=[pltpu.VMEM((2, deep, size), jnp.float32)],
        flops=36 * deep * size * size,
        moved=12 * size * size,
    )(residual, residual_other, inverses, coupling)


def correct(solved, found, panel, panel_other):
    rows, width = solved.shape
    size = panel.shape[0]
    side = size // 2
    part = side // HALF_RING

    chunk = size // 2

    def body(solved_ref, found_ref, panel_ref, other_ref, out_ref, owned_ref, held, sems):
        (plane, core), col = position(), lax.axis_index("col")
        copies = [
            pltpu.make_async_copy(ref.at[at : at + chunk], held.at[i], sems.at[i])
            for i, (ref, at) in enumerate(
                (ref, at) for ref in (panel_ref, other_ref) for at in range(0, size, chunk)
            )
        ]
        for copy in copies:
            copy.start()
        total = jnp.zeros((rows, width), jnp.float32)
        for i, copy in enumerate(copies):
            up, down = halves(found_ref[:, i * chunk : (i + 1) * chunk])
            copy.wait()
            panel_up, panel_down = halves(held[i])
            both = jnp.dot(
                jnp.concatenate([up, down], axis=0), panel_up, preferred_element_type=jnp.float32
            )
            rest = jnp.dot(up, panel_down, preferred_element_type=jnp.float32)
            total += both[:rows] + both[rows:] + rest
        out_ref[...] = solved_ref[...] - total
        place = (col // 2 - CORES * plane + ROWS + HALF_RING - 1) % ROWS
        keeper = (place // HALF_RING) ^ core
        first = pl.multiple_of(col % 2 * (rows // 2), rows // 2)
        back = (HALF_RING - place % HALF_RING) % HALF_RING
        for k in range(2):
            start = pl.multiple_of(keeper * size + k * side, side)
            block = found_ref[pl.ds(first, rows // 2), pl.ds(start, side)]
            owned_ref[:, k] = pltpu.roll(block, back * part, 1)[:, :part]

    return kernel_call(
        body,
        [
            jax.ShapeDtypeStruct(solved.shape, solved.dtype),
            jax.ShapeDtypeStruct((rows // 2, 2, part), solved.dtype),
        ],
        [in_vmem()] * 2 + [in_hbm()] * 2,
        [in_vmem()] * 2,
        scratch=[
            pltpu.VMEM((2 * size // chunk, chunk, width), jnp.float32),
            pltpu.SemaphoreType.DMA((2 * size // chunk,)),
        ],
        flops=36 * rows * found.shape[1] * width,
        moved=4 * found.shape[1] * width,
    )(solved, found, panel, panel_other)


def shards(factor, solved, rhs_window, inverses, coupling):
    rows = solved.shape[0]
    own = with_window(factor, rhs_window)
    other = lax.ppermute(own, "row", core_swap())
    two_own = lax.ppermute(own, "row", apart(2))
    two_other = lax.ppermute(other, "row", apart(2))
    both = join(own, other)
    one = lax.ppermute(both, "row", apart(1))
    solved_other = lax.ppermute(solved, "row", core_swap())
    four = lax.ppermute(two_other, "row", apart(2))
    two = join(two_own, two_other, (solved_other,))
    three = lax.ppermute(two, "row", apart(1))
    partial, panel = reduce_panel(solved, solved_other, [both, one, two, three], four)

    panel_other = lax.ppermute(panel, "row", core_swap())

    each = rows // COLS
    residual = jnp.sum(lax.all_to_all(partial, "col", 0, 0, tiled=True), axis=0)
    residual_other = lax.ppermute(residual[each:], "row", core_swap())
    found = panel_solve(residual[:each], residual_other, inverses, coupling)
    gathered = lax.all_to_all(
        jnp.broadcast_to(found, (COLS,) + found.shape), "col", 0, 0, tiled=True
    ).reshape(rows, -1)
    updated, mine = correct(solved, gathered, panel, panel_other)
    owned = lax.ppermute(mine, ("row", "col"), work_to_window())
    return owned, updated


def solution(mesh):
    in_specs = (P(None, "row", "col"), P("row", "col"), P("col", None, "row"), P(), P())
    out_specs = (P("col", None, "row"), P("row", "col"))
    return jax.shard_map(shards, mesh=mesh, in_specs=in_specs, out_specs=out_specs, check_vma=False)
```

```python
import jax
import jax.numpy as jnp
from jax import lax
from jax.experimental import pallas as pl
from jax.experimental.pallas import tpu as pltpu
from jax.sharding import PartitionSpec as P

PLANES = 8
CORES = 2
ROWS = PLANES * CORES
HALF_RING = ROWS // 2
COLS = 32
TAIL = 8
LANES = 256
DEPTH = 256
MIB = 1024 * 1024


def core_swap():
    return [(row, row ^ 1) for row in range(ROWS)]


def apart(step):
    return [
        (plane * CORES + core, (plane + (step, -step)[core]) % PLANES * CORES + core)
        for plane in range(PLANES)
        for core in range(CORES)
    ]


def work_to_window():
    return [
        (row * COLS + col, (col // 2) * COLS + 2 * row + col % 2)
        for row in range(ROWS)
        for col in range(COLS)
    ]


def halves(x):
    high = x.astype(jnp.bfloat16)
    return high, (x - high.astype(jnp.float32)).astype(jnp.bfloat16)


def rounded_dot(left, right, contract):
    (left_up, left_down), (right_up, right_down) = left, right

    def one(x, y):
        return lax.dot_general(x, y, (contract, ((), ())), preferred_element_type=jnp.float32)

    return one(left_up, right_up) + one(left_down, right_up) + one(left_up, right_down)


def in_vmem():
    return pl.BlockSpec(memory_space=pltpu.VMEM)


def kernel_call(body, out_shape, in_specs, out_specs, scratch=(), mib=16, flops=0, moved=0):
    return pl.pallas_call(
        body,
        out_shape=out_shape,
        in_specs=in_specs,
        out_specs=out_specs,
        scratch_shapes=scratch,
        compiler_params=pltpu.CompilerParams(vmem_limit_bytes=mib * MIB),
        cost_estimate=pl.CostEstimate(flops=flops, bytes_accessed=moved, transcendentals=0),
    )


def position():
    row = lax.axis_index("row")
    return row // CORES, row % CORES


def anywhere():
    return pl.BlockSpec(memory_space=pl.ANY)


def in_hbm():
    return pl.BlockSpec(memory_space=pltpu.MemorySpace.HBM)


def with_window(factor, rhs_window):
    panels, part, width = factor.shape
    rows = panels * part
    groups = width // LANES

    def body(factor_ref, window_ref, out_ref):
        count = window_ref.shape[0]
        for k in range(panels):
            turned = window_ref[:, k].T
            for g in range(part // TAIL):
                at = (k * (part // TAIL) + g) * count
                out_ref[groups * rows :, at : at + count] = turned[g * TAIL : (g + 1) * TAIL]
            for g in range(groups):
                at = g * rows + k * part
                out_ref[at : at + part] = factor_ref[k, :, g * LANES : (g + 1) * LANES]

    return kernel_call(
        body,
        jax.ShapeDtypeStruct((groups * rows + TAIL, LANES), factor.dtype),
        [in_vmem()] * 2,
        in_vmem(),
        mib=56,
        moved=8 * factor.size,
    )(factor, rhs_window)


def join(one, two, arrivals=()):
    def body(one_ref, two_ref, *refs):
        out_ref, sems = refs[-2:]
        rows = one_ref.shape[0]
        first = pltpu.make_async_copy(one_ref, out_ref.at[:rows], sems.at[0])
        second = pltpu.make_async_copy(two_ref, out_ref.at[rows:], sems.at[1])
        first.start()
        second.start()
        first.wait()
        second.wait()

    shape = (one.shape[0] + two.shape[0], one.shape[1])
    return kernel_call(
        body,
        jax.ShapeDtypeStruct(shape, one.dtype),
        [anywhere()] * (2 + len(arrivals)),
        anywhere(),
        scratch=[pltpu.SemaphoreType.DMA((2,))],
        mib=2,
        moved=16 * one.size,
    )(one, two, *arrivals)


def anywhere():
    return pl.BlockSpec(memory_space=pl.ANY)


def reduce_panel(solved, solved_other, pairs, last):
    rows, width = solved.shape
    groups = width // LANES
    block = last.shape[0]
    part = (block - TAIL) // (2 * groups)
    side = HALF_RING * part
    unknowns = 2 * side
    each = rows // COLS
    count = rows // 2

    def body(solved_ref, other_ref, *refs):
        *pair_refs, last_ref, out_ref, panel, window, partial = refs
        (plane, core), col = position(), lax.axis_index("col")

        def put(place, ref, at):
            base = at * block
            first = jnp.where(core == 0, HALF_RING - 1 - place, place) * part
            for k in range(2):
                start = pl.multiple_of(first + k * side, part)
                for g in range(groups):
                    row = base + (2 * g + k) * part
                    panel[pl.ds(start, part), g * LANES : (g + 1) * LANES] = ref[row : row + part]
                for g in range(part // TAIL):
                    lanes = (k * (part // TAIL) + g) * count
                    window[pl.ds(start + g * TAIL, TAIL)] = ref[
                        base + block - TAIL : base + block, lanes : lanes + count
                    ]

        put(0, pair_refs[0], 0)
        for step, ref in enumerate(pair_refs[1:], start=1):
            put(2 * step, ref, 0)
            put(2 * step - 1, ref, 1)
        put(HALF_RING - 1, last_ref, 0)
        solved_pair = jnp.concatenate([solved_ref[...], other_ref[...]], axis=0)
        total = rounded_dot(halves(panel[...]), halves(solved_pair), ((1,), (1,)))
        spread = jnp.concatenate([window[...]] * (2 * rows // count), axis=1)
        lane = lax.broadcasted_iota(jnp.int32, spread.shape, 1)
        mine = 2 * ((col // 2 % CORES) ^ core) + col % 2
        mine = jnp.where(plane == col // (2 * CORES), mine, -1)
        partial[...] = (jnp.where(lane // count == mine, spread, 0.0) - total).T
        for member in range(COLS):
            at = member * each
            out_ref[member, :each] = partial[at : at + each]
            out_ref[member, each:] = partial[rows + at : rows + at + each]

    return kernel_call(
        body,
        [
            jax.ShapeDtypeStruct((COLS, 2 * each, unknowns), jnp.float32),
            jax.ShapeDtypeStruct((unknowns, width), jnp.float32),
        ],
        [in_vmem()] * (3 + len(pairs)),
        [in_vmem()] * 2,
        scratch=[
            pltpu.VMEM((unknowns, count), jnp.float32),
            pltpu.VMEM((2 * rows, unknowns), jnp.float32),
        ],
        mib=32,
        flops=12 * rows * unknowns * width,
        moved=8 * unknowns * width,
    )(solved, solved_other, *pairs, last)


def panel_solve(residual, residual_other, inverses, coupling, arrival):
    each, size = residual.shape
    side = size // 2
    part = side // HALF_RING
    deep = 16

    def body(residual_ref, other_ref, inverses_ref, coupling_ref, _, out_ref, padded):
        plane, core = position()
        first = (CORES * plane + HALF_RING + 1 + core * HALF_RING) % ROWS

        def times(x, matrix, across):
            up, down = halves(x)
            contract = (((1,), (1 if across else 0,)), ((), ()))
            both = lax.dot_general(
                jnp.concatenate([up, down], axis=0),
                matrix[0],
                contract,
                preferred_element_type=jnp.float32,
            )
            rest = lax.dot_general(up, matrix[1], contract, preferred_element_type=jnp.float32)
            return both[:deep] + both[deep:] + rest

        padded[...] = jnp.zeros_like(padded)
        for k in range(2):
            padded[k, :each, :side] = residual_ref[:, k * side : (k + 1) * side]
            padded[k, :each, side:] = other_ref[:, k * side : (k + 1) * side]
        turned = [pltpu.roll(padded[k], first * part, 1) for k in range(2)]
        lead, follow, link = halves(inverses_ref[0]), halves(inverses_ref[1]), halves(coupling_ref[...])
        forward_lead = times(turned[0], lead, True)
        forward_next = times(turned[1] - times(forward_lead, link, True), follow, True)
        backward_next = times(forward_next, follow, False)
        backward_lead = times(forward_lead - times(backward_next, link, False), lead, False)
        back = (ROWS - first) % ROWS
        for k, found in enumerate((backward_lead, backward_next)):
            found = pltpu.roll(found, back * part, 1)[:each]
            out_ref[:, k * side : (k + 1) * side] = found[:, :side]
            out_ref[:, size + k * side : size + (k + 1) * side] = found[:, side:]

    return kernel_call(
        body,
        jax.ShapeDtypeStruct((each, 2 * size), residual.dtype),
        [in_vmem()] * 4 + [anywhere()],
        in_vmem(),
        scratch=[pltpu.VMEM((2, deep, size), jnp.float32)],
        flops=36 * deep * size * size,
        moved=12 * size * size,
    )(residual, residual_other, inverses, coupling, arrival)


def correct(values, found, parts):
    rows, width = values.shape

    def body(values_ref, found_ref, *refs):
        *panel_refs, out_ref, held, sems = refs
        copies = [
            pltpu.make_async_copy(ref.at[first : first + DEPTH], held.at[i], sems.at[i])
            for i, (ref, (_, first, _)) in enumerate(zip(panel_refs, parts))
        ]
        for copy in copies:
            copy.start()
        total = values_ref[...]
        for i, (copy, (_, _, at)) in enumerate(zip(copies, parts)):
            up, down = halves(found_ref[:, at : at + DEPTH])
            copy.wait()
            panel_up, panel_down = halves(held[i])
            both = jnp.dot(
                jnp.concatenate([up, down], axis=0), panel_up, preferred_element_type=jnp.float32
            )
            rest = jnp.dot(up, panel_down, preferred_element_type=jnp.float32)
            total -= both[:rows] + both[rows:] + rest
        out_ref[...] = total

    count = len(parts)
    return kernel_call(
        body,
        jax.ShapeDtypeStruct(values.shape, values.dtype),
        [in_vmem()] * 2 + [in_hbm()] * count,
        in_vmem(),
        scratch=[
            pltpu.VMEM((count, DEPTH, width), jnp.float32),
            pltpu.SemaphoreType.DMA((count,)),
        ],
        flops=18 * rows * count * DEPTH * width,
        moved=4 * count * DEPTH * width,
    )(values, found, *(panel for panel, _, _ in parts))


def cut(found, part):
    rows, width = found.shape
    size = width // 2
    side = size // 2

    def body(found_ref, owned_ref):
        (plane, core), col = position(), lax.axis_index("col")
        place = (col // 2 - CORES * plane + ROWS + HALF_RING - 1) % ROWS
        keeper = (place // HALF_RING) ^ core
        first = pl.multiple_of(col % 2 * (rows // 2), rows // 2)
        back = (HALF_RING - place % HALF_RING) % HALF_RING
        for k in range(2):
            start = pl.multiple_of(keeper * size + k * side, side)
            block = found_ref[pl.ds(first, rows // 2), pl.ds(start, side)]
            owned_ref[:, k] = pltpu.roll(block, back * part, 1)[:, : owned_ref.shape[2]]

    return kernel_call(
        body,
        jax.ShapeDtypeStruct((rows // 2, 2, part), found.dtype),
        [in_vmem()],
        in_vmem(),
        moved=4 * rows * part,
    )(found)


def shards(factor, solved, rhs_window, inverses, coupling):
    rows = solved.shape[0]
    own = with_window(factor, rhs_window)
    other = lax.ppermute(own, "row", core_swap())
    two_own = lax.ppermute(own, "row", apart(2))
    two_other = lax.ppermute(other, "row", apart(2))
    both = join(own, other)
    one = lax.ppermute(both, "row", apart(1))
    solved_other = lax.ppermute(solved, "row", core_swap())
    four = lax.ppermute(two_other, "row", apart(2))
    two = join(two_own, two_other, (solved_other,))
    three = lax.ppermute(two, "row", apart(1))
    partial, panel = reduce_panel(solved, solved_other, [both, one, two, three], four)

    panel_other = lax.ppermute(panel, "row", core_swap())

    each = rows // COLS
    residual = jnp.sum(lax.all_to_all(partial, "col", 0, 0, tiled=True), axis=0)
    residual_other = lax.ppermute(residual[each:], "row", core_swap())
    found = panel_solve(residual[:each], residual_other, inverses, coupling, panel_other)
    gathered = lax.all_to_all(
        jnp.broadcast_to(found, (COLS,) + found.shape), "col", 0, 0, tiled=True
    ).reshape(rows, -1)
    part = rhs_window.shape[2]
    owned = lax.ppermute(cut(gathered, part), ("row", "col"), work_to_window())
    size = panel.shape[0]
    parts = [
        (block, first, start + first)
        for block, start in ((panel, 0), (panel_other, size))
        for first in range(0, size, DEPTH)
    ]
    return owned, correct(solved, gathered, parts)


def solution(mesh):
    in_specs = (P(None, "row", "col"), P("row", "col"), P("col", None, "row"), P(), P())
    out_specs = (P("col", None, "row"), P("row", "col"))
    return jax.shard_map(shards, mesh=mesh, in_specs=in_specs, out_specs=out_specs, check_vma=False)
```

```python
import jax
import jax.numpy as jnp
from jax import lax
from jax.experimental import pallas as pl
from jax.experimental.pallas import tpu as pltpu
from jax.sharding import PartitionSpec as P

PLANES = 8
CORES = 2
ROWS = PLANES * CORES
HALF_RING = ROWS // 2
COLS = 32
TAIL = 8
LANES = 256
DEPTH = 256
MIB = 1024 * 1024


def core_swap():
    return [(row, row ^ 1) for row in range(ROWS)]


def apart(step):
    return [
        (plane * CORES + core, (plane + (step, -step)[core]) % PLANES * CORES + core)
        for plane in range(PLANES)
        for core in range(CORES)
    ]


def work_to_window():
    return [
        (row * COLS + col, (col // 2) * COLS + 2 * row + col % 2)
        for row in range(ROWS)
        for col in range(COLS)
    ]


def halves(x):
    high = x.astype(jnp.bfloat16)
    return high, (x - high.astype(jnp.float32)).astype(jnp.bfloat16)


def rounded_dot(left, right, contract):
    (left_up, left_down), (right_up, right_down) = left, right

    def one(x, y):
        return lax.dot_general(x, y, (contract, ((), ())), preferred_element_type=jnp.float32)

    return one(left_up, right_up) + one(left_down, right_up) + one(left_up, right_down)


def in_vmem():
    return pl.BlockSpec(memory_space=pltpu.VMEM)


def kernel_call(body, out_shape, in_specs, out_specs, scratch=(), mib=16, flops=0, moved=0):
    return pl.pallas_call(
        body,
        out_shape=out_shape,
        in_specs=in_specs,
        out_specs=out_specs,
        scratch_shapes=scratch,
        compiler_params=pltpu.CompilerParams(vmem_limit_bytes=mib * MIB),
        cost_estimate=pl.CostEstimate(flops=flops, bytes_accessed=moved, transcendentals=0),
    )


def position():
    row = lax.axis_index("row")
    return row // CORES, row % CORES


def anywhere():
    return pl.BlockSpec(memory_space=pl.ANY)


def in_hbm():
    return pl.BlockSpec(memory_space=pltpu.MemorySpace.HBM)


def with_window(factor, rhs_window):
    panels, part, width = factor.shape
    rows = panels * part
    groups = width // LANES

    def body(factor_ref, window_ref, out_ref):
        count = window_ref.shape[0]
        for k in range(panels):
            turned = window_ref[:, k].T
            for g in range(part // TAIL):
                at = (k * (part // TAIL) + g) * count
                out_ref[groups * rows :, at : at + count] = turned[g * TAIL : (g + 1) * TAIL]
            for g in range(groups):
                at = g * rows + k * part
                out_ref[at : at + part] = factor_ref[k, :, g * LANES : (g + 1) * LANES]

    return kernel_call(
        body,
        jax.ShapeDtypeStruct((groups * rows + TAIL, LANES), factor.dtype),
        [in_vmem()] * 2,
        in_vmem(),
        mib=16,
        moved=8 * factor.size,
    )(factor, rhs_window)


def join(one, two, arrivals=()):
    def body(one_ref, two_ref, *refs):
        out_ref, sems = refs[-2:]
        rows = one_ref.shape[0]
        first = pltpu.make_async_copy(one_ref, out_ref.at[:rows], sems.at[0])
        second = pltpu.make_async_copy(two_ref, out_ref.at[rows:], sems.at[1])
        first.start()
        second.start()
        first.wait()
        second.wait()

    shape = (one.shape[0] + two.shape[0], one.shape[1])
    return kernel_call(
        body,
        jax.ShapeDtypeStruct(shape, one.dtype),
        [anywhere()] * (2 + len(arrivals)),
        anywhere(),
        scratch=[pltpu.SemaphoreType.DMA((2,))],
        mib=2,
        moved=16 * one.size,
    )(one, two, *arrivals)


def anywhere():
    return pl.BlockSpec(memory_space=pl.ANY)


def reduce_panel(solved, solved_other, pairs, last):
    rows, width = solved.shape
    groups = width // LANES
    block = last.shape[0]
    part = (block - TAIL) // (2 * groups)
    side = HALF_RING * part
    unknowns = 2 * side
    each = rows // COLS
    count = rows // 2

    def body(solved_ref, other_ref, *refs):
        *pair_refs, last_ref, out_ref, panel, window, partial = refs
        (plane, core), col = position(), lax.axis_index("col")

        def put(place, ref, at):
            base = at * block
            first = jnp.where(core == 0, HALF_RING - 1 - place, place) * part
            for k in range(2):
                start = pl.multiple_of(first + k * side, part)
                for g in range(groups):
                    row = base + (2 * g + k) * part
                    panel[pl.ds(start, part), g * LANES : (g + 1) * LANES] = ref[row : row + part]
                for g in range(part // TAIL):
                    lanes = (k * (part // TAIL) + g) * count
                    window[pl.ds(start + g * TAIL, TAIL)] = ref[
                        base + block - TAIL : base + block, lanes : lanes + count
                    ]

        put(0, pair_refs[0], 0)
        for step, ref in enumerate(pair_refs[1:], start=1):
            put(2 * step, ref, 0)
            put(2 * step - 1, ref, 1)
        put(HALF_RING - 1, last_ref, 0)
        solved_pair = jnp.concatenate([solved_ref[...], other_ref[...]], axis=0)
        total = rounded_dot(halves(panel[...]), halves(solved_pair), ((1,), (1,)))
        spread = jnp.concatenate([window[...]] * (2 * rows // count), axis=1)
        lane = lax.broadcasted_iota(jnp.int32, spread.shape, 1)
        mine = 2 * ((col // 2 % CORES) ^ core) + col % 2
        mine = jnp.where(plane == col // (2 * CORES), mine, -1)
        partial[...] = (jnp.where(lane // count == mine, spread, 0.0) - total).T
        for member in range(COLS):
            at = member * each
            out_ref[member, :each] = partial[at : at + each]
            out_ref[member, each:] = partial[rows + at : rows + at + each]

    return kernel_call(
        body,
        [
            jax.ShapeDtypeStruct((COLS, 2 * each, unknowns), jnp.float32),
            jax.ShapeDtypeStruct((unknowns, width), jnp.float32),
        ],
        [in_vmem()] * (3 + len(pairs)),
        [in_vmem()] * 2,
        scratch=[
            pltpu.VMEM((unknowns, count), jnp.float32),
            pltpu.VMEM((2 * rows, unknowns), jnp.float32),
        ],
        mib=24,
        flops=12 * rows * unknowns * width,
        moved=8 * unknowns * width,
    )(solved, solved_other, *pairs, last)


def panel_solve(residual, residual_other, inverses, coupling, arrival):
    each, size = residual.shape
    side = size // 2
    part = side // HALF_RING
    deep = 16

    def body(residual_ref, other_ref, inverses_ref, coupling_ref, _, out_ref, padded):
        plane, core = position()
        first = (CORES * plane + HALF_RING + 1 + core * HALF_RING) % ROWS

        def times(x, matrix, across):
            up, down = halves(x)
            contract = (((1,), (1 if across else 0,)), ((), ()))
            both = lax.dot_general(
                jnp.concatenate([up, down], axis=0),
                matrix[0],
                contract,
                preferred_element_type=jnp.float32,
            )
            rest = lax.dot_general(up, matrix[1], contract, preferred_element_type=jnp.float32)
            return both[:deep] + both[deep:] + rest

        padded[...] = jnp.zeros_like(padded)
        for k in range(2):
            padded[k, :each, :side] = residual_ref[:, k * side : (k + 1) * side]
            padded[k, :each, side:] = other_ref[:, k * side : (k + 1) * side]
        turned = [pltpu.roll(padded[k], first * part, 1) for k in range(2)]
        lead, follow, link = halves(inverses_ref[0]), halves(inverses_ref[1]), halves(coupling_ref[...])
        forward_lead = times(turned[0], lead, True)
        forward_next = times(turned[1] - times(forward_lead, link, True), follow, True)
        backward_next = times(forward_next, follow, False)
        backward_lead = times(forward_lead - times(backward_next, link, False), lead, False)
        back = (ROWS - first) % ROWS
        for k, found in enumerate((backward_lead, backward_next)):
            found = pltpu.roll(found, back * part, 1)[:each]
            out_ref[:, k * side : (k + 1) * side] = found[:, :side]
            out_ref[:, size + k * side : size + (k + 1) * side] = found[:, side:]

    return kernel_call(
        body,
        jax.ShapeDtypeStruct((each, 2 * size), residual.dtype),
        [in_vmem()] * 4 + [anywhere()],
        in_vmem(),
        scratch=[pltpu.VMEM((2, deep, size), jnp.float32)],
        flops=36 * deep * size * size,
        moved=12 * size * size,
    )(residual, residual_other, inverses, coupling, arrival)


def correct(values, found, parts):
    rows, width = values.shape

    def body(values_ref, found_ref, *refs):
        *panel_refs, out_ref, held, sems = refs
        copies = [
            pltpu.make_async_copy(ref.at[first : first + DEPTH], held.at[i], sems.at[i])
            for i, (ref, (_, first, _)) in enumerate(zip(panel_refs, parts))
        ]
        for copy in copies:
            copy.start()
        total = values_ref[...]
        for i, (copy, (_, _, at)) in enumerate(zip(copies, parts)):
            up, down = halves(found_ref[:, at : at + DEPTH])
            copy.wait()
            panel_up, panel_down = halves(held[i])
            both = jnp.dot(
                jnp.concatenate([up, down], axis=0), panel_up, preferred_element_type=jnp.float32
            )
            rest = jnp.dot(up, panel_down, preferred_element_type=jnp.float32)
            total -= both[:rows] + both[rows:] + rest
        out_ref[...] = total

    count = len(parts)
    return kernel_call(
        body,
        jax.ShapeDtypeStruct(values.shape, values.dtype),
        [in_vmem()] * 2 + [in_hbm()] * count,
        in_vmem(),
        scratch=[
            pltpu.VMEM((count, DEPTH, width), jnp.float32),
            pltpu.SemaphoreType.DMA((count,)),
        ],
        flops=18 * rows * count * DEPTH * width,
        moved=4 * count * DEPTH * width,
    )(values, found, *(panel for panel, _, _ in parts))


def cut(found, part):
    rows, width = found.shape
    size = width // 2
    side = size // 2

    def body(found_ref, owned_ref):
        (plane, core), col = position(), lax.axis_index("col")
        place = (col // 2 - CORES * plane + ROWS + HALF_RING - 1) % ROWS
        keeper = (place // HALF_RING) ^ core
        first = pl.multiple_of(col % 2 * (rows // 2), rows // 2)
        back = (HALF_RING - place % HALF_RING) % HALF_RING
        for k in range(2):
            start = pl.multiple_of(keeper * size + k * side, side)
            block = found_ref[pl.ds(first, rows // 2), pl.ds(start, side)]
            owned_ref[:, k] = pltpu.roll(block, back * part, 1)[:, : owned_ref.shape[2]]

    return kernel_call(
        body,
        jax.ShapeDtypeStruct((rows // 2, 2, part), found.dtype),
        [in_vmem()],
        in_vmem(),
        moved=4 * rows * part,
    )(found)


def shards(factor, solved, rhs_window, inverses, coupling):
    rows = solved.shape[0]
    own = with_window(factor, rhs_window)
    other = lax.ppermute(own, "row", core_swap())
    two_own = lax.ppermute(own, "row", apart(2))
    two_other = lax.ppermute(other, "row", apart(2))
    both = join(own, other)
    one = lax.ppermute(both, "row", apart(1))
    solved_other = lax.ppermute(solved, "row", core_swap())
    four = lax.ppermute(two_other, "row", apart(2))
    two = join(two_own, two_other, (solved_other,))
    three = lax.ppermute(two, "row", apart(1))
    partial, panel = reduce_panel(solved, solved_other, [both, one, two, three], four)

    panel_other = lax.ppermute(panel, "row", core_swap())

    each = rows // COLS
    residual = jnp.sum(lax.all_to_all(partial, "col", 0, 0, tiled=True), axis=0)
    residual_other = lax.ppermute(residual[each:], "row", core_swap())
    found = panel_solve(residual[:each], residual_other, inverses, coupling, panel_other)
    gathered = lax.all_to_all(
        jnp.broadcast_to(found, (COLS,) + found.shape), "col", 0, 0, tiled=True
    ).reshape(rows, -1)
    part = rhs_window.shape[2]
    owned = lax.ppermute(cut(gathered, part), ("row", "col"), work_to_window())
    size = panel.shape[0]
    parts = [
        (block, first, start + first)
        for block, start in ((panel, 0), (panel_other, size))
        for first in range(0, size, DEPTH)
    ]
    return owned, correct(solved, gathered, parts)


def solution(mesh):
    in_specs = (P(None, "row", "col"), P("row", "col"), P("col", None, "row"), P(), P())
    out_specs = (P("col", None, "row"), P("row", "col"))
    return jax.shard_map(shards, mesh=mesh, in_specs=in_specs, out_specs=out_specs, check_vma=False)
```

```python
import jax
import jax.numpy as jnp
from jax import lax
from jax.experimental import pallas as pl
from jax.experimental.pallas import tpu as pltpu
from jax.sharding import PartitionSpec as P

PLANES = 8
CORES = 2
ROWS = PLANES * CORES
HALF_RING = ROWS // 2
COLS = 32
TAIL = 8
LANES = 256
DEPTH = 256
MIB = 1024 * 1024


def core_swap():
    return [(row, row ^ 1) for row in range(ROWS)]


def apart(step):
    return [
        (plane * CORES + core, (plane + (step, -step)[core]) % PLANES * CORES + core)
        for plane in range(PLANES)
        for core in range(CORES)
    ]


def work_to_window():
    return [
        (row * COLS + col, (col // 2) * COLS + 2 * row + col % 2)
        for row in range(ROWS)
        for col in range(COLS)
    ]


def halves(x):
    high = x.astype(jnp.bfloat16)
    return high, (x - high.astype(jnp.float32)).astype(jnp.bfloat16)


def rounded_dot(left, right, contract):
    (left_up, left_down), (right_up, right_down) = left, right

    def one(x, y):
        return lax.dot_general(x, y, (contract, ((), ())), preferred_element_type=jnp.float32)

    return one(left_up, right_up) + one(left_down, right_up) + one(left_up, right_down)


def in_vmem():
    return pl.BlockSpec(memory_space=pltpu.VMEM)


def kernel_call(body, out_shape, in_specs, out_specs, scratch=(), mib=16, flops=0, moved=0):
    return pl.pallas_call(
        body,
        out_shape=out_shape,
        in_specs=in_specs,
        out_specs=out_specs,
        scratch_shapes=scratch,
        compiler_params=pltpu.CompilerParams(vmem_limit_bytes=mib * MIB),
        cost_estimate=pl.CostEstimate(flops=flops, bytes_accessed=moved, transcendentals=0),
    )


def position():
    row = lax.axis_index("row")
    return row // CORES, row % CORES


def anywhere():
    return pl.BlockSpec(memory_space=pl.ANY)


def in_hbm():
    return pl.BlockSpec(memory_space=pltpu.MemorySpace.HBM)


def with_window(factor, rhs_window):
    panels, part, width = factor.shape
    rows = panels * part
    groups = width // LANES

    def body(factor_ref, window_ref, out_ref):
        count = window_ref.shape[0]
        for k in range(panels):
            turned = window_ref[:, k].T
            for g in range(part // TAIL):
                at = (k * (part // TAIL) + g) * count
                out_ref[groups * rows :, at : at + count] = turned[g * TAIL : (g + 1) * TAIL]
            for g in range(groups):
                at = g * rows + k * part
                out_ref[at : at + part] = factor_ref[k, :, g * LANES : (g + 1) * LANES]

    return kernel_call(
        body,
        jax.ShapeDtypeStruct((groups * rows + TAIL, LANES), factor.dtype),
        [in_vmem()] * 2,
        in_vmem(),
        mib=16,
        moved=8 * factor.size,
    )(factor, rhs_window)


def join(one, two, arrivals=()):
    def body(one_ref, two_ref, *refs):
        out_ref, sems = refs[-2:]
        rows = one_ref.shape[0]
        first = pltpu.make_async_copy(one_ref, out_ref.at[:rows], sems.at[0])
        second = pltpu.make_async_copy(two_ref, out_ref.at[rows:], sems.at[1])
        first.start()
        second.start()
        first.wait()
        second.wait()

    shape = (one.shape[0] + two.shape[0], one.shape[1])
    return kernel_call(
        body,
        jax.ShapeDtypeStruct(shape, one.dtype),
        [anywhere()] * (2 + len(arrivals)),
        anywhere(),
        scratch=[pltpu.SemaphoreType.DMA((2,))],
        mib=2,
        moved=16 * one.size,
    )(one, two, *arrivals)


def anywhere():
    return pl.BlockSpec(memory_space=pl.ANY)


def reduce_panel(solved, solved_other, pairs, last):
    rows, width = solved.shape
    groups = width // LANES
    block = last.shape[0]
    part = (block - TAIL) // (2 * groups)
    side = HALF_RING * part
    unknowns = 2 * side
    each = rows // COLS
    count = rows // 2

    def body(solved_ref, other_ref, *refs):
        *pair_refs, last_ref, out_ref, panel, window, partial = refs
        (plane, core), col = position(), lax.axis_index("col")

        def put(place, ref, at):
            base = at * block
            first = jnp.where(core == 0, HALF_RING - 1 - place, place) * part
            for k in range(2):
                start = pl.multiple_of(first + k * side, part)
                for g in range(groups):
                    row = base + (2 * g + k) * part
                    panel[pl.ds(start, part), g * LANES : (g + 1) * LANES] = ref[row : row + part]
                for g in range(part // TAIL):
                    lanes = (k * (part // TAIL) + g) * count
                    window[pl.ds(start + g * TAIL, TAIL)] = ref[
                        base + block - TAIL : base + block, lanes : lanes + count
                    ]

        put(0, pair_refs[0], 0)
        for step, ref in enumerate(pair_refs[1:], start=1):
            put(2 * step, ref, 0)
            put(2 * step - 1, ref, 1)
        put(HALF_RING - 1, last_ref, 0)
        solved_pair = jnp.concatenate([solved_ref[...], other_ref[...]], axis=0)
        total = rounded_dot(halves(panel[...]), halves(solved_pair), ((1,), (1,)))
        spread = jnp.concatenate([window[...]] * (2 * rows // count), axis=1)
        lane = lax.broadcasted_iota(jnp.int32, spread.shape, 1)
        mine = 2 * ((col // 2 % CORES) ^ core) + col % 2
        mine = jnp.where(plane == col // (2 * CORES), mine, -1)
        partial[...] = (jnp.where(lane // count == mine, spread, 0.0) - total).T
        for member in range(COLS):
            at = member * each
            out_ref[member, :each] = partial[at : at + each]
            out_ref[member, each:] = partial[rows + at : rows + at + each]

    return kernel_call(
        body,
        [
            jax.ShapeDtypeStruct((COLS, 2 * each, unknowns), jnp.float32),
            jax.ShapeDtypeStruct((unknowns, width), jnp.float32),
        ],
        [in_vmem()] * (3 + len(pairs)),
        [in_vmem()] * 2,
        scratch=[
            pltpu.VMEM((unknowns, count), jnp.float32),
            pltpu.VMEM((2 * rows, unknowns), jnp.float32),
        ],
        mib=24,
        flops=12 * rows * unknowns * width,
        moved=8 * unknowns * width,
    )(solved, solved_other, *pairs, last)


def panel_solve(residual, residual_other, inverses, coupling, arrival):
    each, size = residual.shape
    side = size // 2
    part = side // HALF_RING
    deep = 16

    def body(residual_ref, other_ref, inverses_ref, coupling_ref, _, out_ref, padded):
        plane, core = position()
        first = (CORES * plane + HALF_RING + 1 + core * HALF_RING) % ROWS

        def times(x, matrix, across):
            up, down = halves(x)
            contract = (((1,), (1 if across else 0,)), ((), ()))
            both = lax.dot_general(
                jnp.concatenate([up, down], axis=0),
                matrix[0],
                contract,
                preferred_element_type=jnp.float32,
            )
            rest = lax.dot_general(up, matrix[1], contract, preferred_element_type=jnp.float32)
            return both[:deep] + both[deep:] + rest

        padded[...] = jnp.zeros_like(padded)
        for k in range(2):
            padded[k, :each, :side] = residual_ref[:, k * side : (k + 1) * side]
            padded[k, :each, side:] = other_ref[:, k * side : (k + 1) * side]
        turned = [pltpu.roll(padded[k], first * part, 1) for k in range(2)]
        lead, follow, link = halves(inverses_ref[0]), halves(inverses_ref[1]), halves(coupling_ref[...])
        forward_lead = times(turned[0], lead, True)
        forward_next = times(turned[1] - times(forward_lead, link, True), follow, True)
        backward_next = times(forward_next, follow, False)
        backward_lead = times(forward_lead - times(backward_next, link, False), lead, False)
        back = (ROWS - first) % ROWS
        for k, found in enumerate((backward_lead, backward_next)):
            found = pltpu.roll(found, back * part, 1)[:each]
            out_ref[:, k * side : (k + 1) * side] = found[:, :side]
            out_ref[:, size + k * side : size + (k + 1) * side] = found[:, side:]

    return kernel_call(
        body,
        jax.ShapeDtypeStruct((each, 2 * size), residual.dtype),
        [in_vmem()] * 5,
        in_vmem(),
        scratch=[pltpu.VMEM((2, deep, size), jnp.float32)],
        flops=36 * deep * size * size,
        moved=12 * size * size,
    )(residual, residual_other, inverses, coupling, arrival)


def correct(values, found, parts):
    rows, width = values.shape

    def body(values_ref, found_ref, *refs):
        *panel_refs, out_ref, held, sems = refs
        copies = [
            pltpu.make_async_copy(ref.at[first : first + DEPTH], held.at[i], sems.at[i])
            for i, (ref, (_, first, _)) in enumerate(zip(panel_refs, parts))
        ]
        for copy in copies:
            copy.start()
        total = values_ref[...]
        for i, (copy, (_, _, at)) in enumerate(zip(copies, parts)):
            up, down = halves(found_ref[:, at : at + DEPTH])
            copy.wait()
            panel_up, panel_down = halves(held[i])
            both = jnp.dot(
                jnp.concatenate([up, down], axis=0), panel_up, preferred_element_type=jnp.float32
            )
            rest = jnp.dot(up, panel_down, preferred_element_type=jnp.float32)
            total -= both[:rows] + both[rows:] + rest
        out_ref[...] = total

    count = len(parts)
    return kernel_call(
        body,
        jax.ShapeDtypeStruct(values.shape, values.dtype),
        [in_vmem()] * 2 + [in_hbm()] * count,
        in_vmem(),
        scratch=[
            pltpu.VMEM((count, DEPTH, width), jnp.float32),
            pltpu.SemaphoreType.DMA((count,)),
        ],
        flops=18 * rows * count * DEPTH * width,
        moved=4 * count * DEPTH * width,
    )(values, found, *(panel for panel, _, _ in parts))


def cut(found, part):
    rows, width = found.shape
    size = width // 2
    side = size // 2

    def body(found_ref, owned_ref):
        (plane, core), col = position(), lax.axis_index("col")
        place = (col // 2 - CORES * plane + ROWS + HALF_RING - 1) % ROWS
        keeper = (place // HALF_RING) ^ core
        first = pl.multiple_of(col % 2 * (rows // 2), rows // 2)
        back = (HALF_RING - place % HALF_RING) % HALF_RING
        for k in range(2):
            start = pl.multiple_of(keeper * size + k * side, side)
            block = found_ref[pl.ds(first, rows // 2), pl.ds(start, side)]
            owned_ref[:, k] = pltpu.roll(block, back * part, 1)[:, : owned_ref.shape[2]]

    return kernel_call(
        body,
        jax.ShapeDtypeStruct((rows // 2, 2, part), found.dtype),
        [in_vmem()],
        in_vmem(),
        moved=4 * rows * part,
    )(found)


def shards(factor, solved, rhs_window, inverses, coupling):
    rows = solved.shape[0]
    own = with_window(factor, rhs_window)
    other = lax.ppermute(own, "row", core_swap())
    two_own = lax.ppermute(own, "row", apart(2))
    two_other = lax.ppermute(other, "row", apart(2))
    both = join(own, other)
    one = lax.ppermute(both, "row", apart(1))
    solved_other = lax.ppermute(solved, "row", core_swap())
    four = lax.ppermute(two_other, "row", apart(2))
    two = join(two_own, two_other, (solved_other,))
    three = lax.ppermute(two, "row", apart(1))
    partial, panel = reduce_panel(solved, solved_other, [both, one, two, three], four)

    panel_other = lax.ppermute(panel, "row", core_swap())

    each = rows // COLS
    residual = jnp.sum(lax.all_to_all(partial, "col", 0, 0, tiled=True), axis=0)
    residual_other = lax.ppermute(residual[each:], "row", core_swap())
    found = panel_solve(residual[:each], residual_other, inverses, coupling, panel_other[:8, :128])
    gathered = lax.all_to_all(
        jnp.broadcast_to(found, (COLS,) + found.shape), "col", 0, 0, tiled=True
    ).reshape(rows, -1)
    part = rhs_window.shape[2]
    owned = lax.ppermute(cut(gathered, part), ("row", "col"), work_to_window())
    size = panel.shape[0]
    parts = [
        (block, first, start + first)
        for block, start in ((panel, 0), (panel_other, size))
        for first in range(0, size, DEPTH)
    ]
    return owned, correct(solved, gathered, parts)


def solution(mesh):
    in_specs = (P(None, "row", "col"), P("row", "col"), P("col", None, "row"), P(), P())
    out_specs = (P("col", None, "row"), P("row", "col"))
    return jax.shard_map(shards, mesh=mesh, in_specs=in_specs, out_specs=out_specs, check_vma=False)
```

```python
import jax
import jax.numpy as jnp
from jax import lax
from jax.experimental import pallas as pl
from jax.experimental.pallas import tpu as pltpu
from jax.sharding import PartitionSpec as P

PLANES = 8
CORES = 2
ROWS = PLANES * CORES
HALF_RING = ROWS // 2
COLS = 32
TAIL = 8
LANES = 256
DEPTH = 256
MIB = 1024 * 1024


def core_swap():
    return [(row, row ^ 1) for row in range(ROWS)]


def apart(step):
    return [
        (plane * CORES + core, (plane + (step, -step)[core]) % PLANES * CORES + core)
        for plane in range(PLANES)
        for core in range(CORES)
    ]


def work_to_window():
    return [
        (row * COLS + col, (col // 2) * COLS + 2 * row + col % 2)
        for row in range(ROWS)
        for col in range(COLS)
    ]


def halves(x):
    high = x.astype(jnp.bfloat16)
    return high, (x - high.astype(jnp.float32)).astype(jnp.bfloat16)


def rounded_dot(left, right, contract):
    (left_up, left_down), (right_up, right_down) = left, right

    def one(x, y):
        return lax.dot_general(x, y, (contract, ((), ())), preferred_element_type=jnp.float32)

    return one(left_up, right_up) + one(left_down, right_up) + one(left_up, right_down)


def in_vmem():
    return pl.BlockSpec(memory_space=pltpu.VMEM)


def kernel_call(body, out_shape, in_specs, out_specs, scratch=(), mib=16, flops=0, moved=0):
    return pl.pallas_call(
        body,
        out_shape=out_shape,
        in_specs=in_specs,
        out_specs=out_specs,
        scratch_shapes=scratch,
        compiler_params=pltpu.CompilerParams(vmem_limit_bytes=mib * MIB),
        cost_estimate=pl.CostEstimate(flops=flops, bytes_accessed=moved, transcendentals=0),
    )


def position():
    row = lax.axis_index("row")
    return row // CORES, row % CORES


def anywhere():
    return pl.BlockSpec(memory_space=pl.ANY)


def in_hbm():
    return pl.BlockSpec(memory_space=pltpu.MemorySpace.HBM)


def with_window(factor, rhs_window):
    panels, part, width = factor.shape
    rows = panels * part
    groups = width // LANES

    def body(factor_ref, window_ref, out_ref):
        count = window_ref.shape[0]
        for k in range(panels):
            turned = window_ref[:, k].T
            for g in range(part // TAIL):
                at = (k * (part // TAIL) + g) * count
                out_ref[groups * rows :, at : at + count] = turned[g * TAIL : (g + 1) * TAIL]
            for g in range(groups):
                at = g * rows + k * part
                out_ref[at : at + part] = factor_ref[k, :, g * LANES : (g + 1) * LANES]

    return kernel_call(
        body,
        jax.ShapeDtypeStruct((groups * rows + TAIL, LANES), factor.dtype),
        [in_vmem()] * 2,
        in_vmem(),
        mib=16,
        moved=8 * factor.size,
    )(factor, rhs_window)


def join(one, two, arrivals=()):
    def body(one_ref, two_ref, *refs):
        out_ref, sems = refs[-2:]
        rows = one_ref.shape[0]
        first = pltpu.make_async_copy(one_ref, out_ref.at[:rows], sems.at[0])
        second = pltpu.make_async_copy(two_ref, out_ref.at[rows:], sems.at[1])
        first.start()
        second.start()
        first.wait()
        second.wait()

    shape = (one.shape[0] + two.shape[0], one.shape[1])
    return kernel_call(
        body,
        jax.ShapeDtypeStruct(shape, one.dtype),
        [anywhere()] * (2 + len(arrivals)),
        anywhere(),
        scratch=[pltpu.SemaphoreType.DMA((2,))],
        mib=2,
        moved=16 * one.size,
    )(one, two, *arrivals)


def anywhere():
    return pl.BlockSpec(memory_space=pl.ANY)


def reduce_panel(solved, solved_other, pairs, last):
    rows, width = solved.shape
    groups = width // LANES
    block = last.shape[0]
    part = (block - TAIL) // (2 * groups)
    side = HALF_RING * part
    unknowns = 2 * side
    each = rows // COLS
    count = rows // 2

    def body(solved_ref, other_ref, *refs):
        *pair_refs, last_ref, out_ref, panel, window, partial = refs
        (plane, core), col = position(), lax.axis_index("col")

        def put(place, ref, at):
            base = at * block
            first = jnp.where(core == 0, HALF_RING - 1 - place, place) * part
            for k in range(2):
                start = pl.multiple_of(first + k * side, part)
                for g in range(groups):
                    row = base + (2 * g + k) * part
                    panel[pl.ds(start, part), g * LANES : (g + 1) * LANES] = ref[row : row + part]
                for g in range(part // TAIL):
                    lanes = (k * (part // TAIL) + g) * count
                    window[pl.ds(start + g * TAIL, TAIL)] = ref[
                        base + block - TAIL : base + block, lanes : lanes + count
                    ]

        put(0, pair_refs[0], 0)
        for step, ref in enumerate(pair_refs[1:], start=1):
            put(2 * step, ref, 0)
            put(2 * step - 1, ref, 1)
        put(HALF_RING - 1, last_ref, 0)
        solved_pair = jnp.concatenate([solved_ref[...], other_ref[...]], axis=0)
        total = rounded_dot(halves(panel[...]), halves(solved_pair), ((1,), (1,)))
        spread = jnp.concatenate([window[...]] * (2 * rows // count), axis=1)
        lane = lax.broadcasted_iota(jnp.int32, spread.shape, 1)
        mine = 2 * ((col // 2 % CORES) ^ core) + col % 2
        mine = jnp.where(plane == col // (2 * CORES), mine, -1)
        partial[...] = (jnp.where(lane // count == mine, spread, 0.0) - total).T
        for member in range(COLS):
            at = member * each
            out_ref[member, :each] = partial[at : at + each]
            out_ref[member, each:] = partial[rows + at : rows + at + each]

    return kernel_call(
        body,
        [
            jax.ShapeDtypeStruct((COLS, 2 * each, unknowns), jnp.float32),
            jax.ShapeDtypeStruct((unknowns, width), jnp.float32),
        ],
        [in_vmem()] * (3 + len(pairs)),
        [in_vmem()] * 2,
        scratch=[
            pltpu.VMEM((unknowns, count), jnp.float32),
            pltpu.VMEM((2 * rows, unknowns), jnp.float32),
        ],
        mib=32,
        flops=12 * rows * unknowns * width,
        moved=8 * unknowns * width,
    )(solved, solved_other, *pairs, last)


def panel_solve(residual, residual_other, inverses, coupling, arrival):
    each, size = residual.shape
    side = size // 2
    part = side // HALF_RING
    deep = 16

    def body(residual_ref, other_ref, inverses_ref, coupling_ref, _, out_ref, padded):
        plane, core = position()
        first = (CORES * plane + HALF_RING + 1 + core * HALF_RING) % ROWS

        def times(x, matrix, across):
            up, down = halves(x)
            contract = (((1,), (1 if across else 0,)), ((), ()))
            both = lax.dot_general(
                jnp.concatenate([up, down], axis=0),
                matrix[0],
                contract,
                preferred_element_type=jnp.float32,
            )
            rest = lax.dot_general(up, matrix[1], contract, preferred_element_type=jnp.float32)
            return both[:deep] + both[deep:] + rest

        padded[...] = jnp.zeros_like(padded)
        for k in range(2):
            padded[k, :each, :side] = residual_ref[:, k * side : (k + 1) * side]
            padded[k, :each, side:] = other_ref[:, k * side : (k + 1) * side]
        turned = [pltpu.roll(padded[k], first * part, 1) for k in range(2)]
        lead, follow, link = halves(inverses_ref[0]), halves(inverses_ref[1]), halves(coupling_ref[...])
        forward_lead = times(turned[0], lead, True)
        forward_next = times(turned[1] - times(forward_lead, link, True), follow, True)
        backward_next = times(forward_next, follow, False)
        backward_lead = times(forward_lead - times(backward_next, link, False), lead, False)
        back = (ROWS - first) % ROWS
        for k, found in enumerate((backward_lead, backward_next)):
            found = pltpu.roll(found, back * part, 1)[:each]
            out_ref[:, k * side : (k + 1) * side] = found[:, :side]
            out_ref[:, size + k * side : size + (k + 1) * side] = found[:, side:]

    return kernel_call(
        body,
        jax.ShapeDtypeStruct((each, 2 * size), residual.dtype),
        [in_vmem()] * 5,
        in_vmem(),
        scratch=[pltpu.VMEM((2, deep, size), jnp.float32)],
        flops=36 * deep * size * size,
        moved=12 * size * size,
    )(residual, residual_other, inverses, coupling, arrival)


def correct(values, found, parts):
    rows, width = values.shape

    def body(values_ref, found_ref, *refs):
        *panel_refs, out_ref, held, sems = refs
        copies = [
            pltpu.make_async_copy(ref.at[first : first + DEPTH], held.at[i], sems.at[i])
            for i, (ref, (_, first, _)) in enumerate(zip(panel_refs, parts))
        ]
        for copy in copies:
            copy.start()
        total = values_ref[...]
        for i, (copy, (_, _, at)) in enumerate(zip(copies, parts)):
            up, down = halves(found_ref[:, at : at + DEPTH])
            copy.wait()
            panel_up, panel_down = halves(held[i])
            both = jnp.dot(
                jnp.concatenate([up, down], axis=0), panel_up, preferred_element_type=jnp.float32
            )
            rest = jnp.dot(up, panel_down, preferred_element_type=jnp.float32)
            total -= both[:rows] + both[rows:] + rest
        out_ref[...] = total

    count = len(parts)
    return kernel_call(
        body,
        jax.ShapeDtypeStruct(values.shape, values.dtype),
        [in_vmem()] * 2 + [in_hbm()] * count,
        in_vmem(),
        scratch=[
            pltpu.VMEM((count, DEPTH, width), jnp.float32),
            pltpu.SemaphoreType.DMA((count,)),
        ],
        flops=18 * rows * count * DEPTH * width,
        moved=4 * count * DEPTH * width,
    )(values, found, *(panel for panel, _, _ in parts))


def cut(found, part):
    rows, width = found.shape
    size = width // 2
    side = size // 2

    def body(found_ref, owned_ref):
        (plane, core), col = position(), lax.axis_index("col")
        place = (col // 2 - CORES * plane + ROWS + HALF_RING - 1) % ROWS
        keeper = (place // HALF_RING) ^ core
        first = pl.multiple_of(col % 2 * (rows // 2), rows // 2)
        back = (HALF_RING - place % HALF_RING) % HALF_RING
        for k in range(2):
            start = pl.multiple_of(keeper * size + k * side, side)
            block = found_ref[pl.ds(first, rows // 2), pl.ds(start, side)]
            owned_ref[:, k] = pltpu.roll(block, back * part, 1)[:, : owned_ref.shape[2]]

    return kernel_call(
        body,
        jax.ShapeDtypeStruct((rows // 2, 2, part), found.dtype),
        [in_vmem()],
        in_vmem(),
        moved=4 * rows * part,
    )(found)


def shards(factor, solved, rhs_window, inverses, coupling):
    rows = solved.shape[0]
    own = with_window(factor, rhs_window)
    other = lax.ppermute(own, "row", core_swap())
    two_own = lax.ppermute(own, "row", apart(2))
    two_other = lax.ppermute(other, "row", apart(2))
    both = join(own, other)
    one = lax.ppermute(both, "row", apart(1))
    solved_other = lax.ppermute(solved, "row", core_swap())
    four = lax.ppermute(two_other, "row", apart(2))
    two = join(two_own, two_other, (solved_other,))
    three = lax.ppermute(two, "row", apart(1))
    partial, panel = reduce_panel(solved, solved_other, [both, one, two, three], four)

    panel_other = lax.ppermute(panel, "row", core_swap())

    each = rows // COLS
    residual = jnp.sum(lax.all_to_all(partial, "col", 0, 0, tiled=True), axis=0)
    residual_other = lax.ppermute(residual[each:], "row", core_swap())
    found = panel_solve(residual[:each], residual_other, inverses, coupling, panel_other[:8, :128])
    gathered = lax.all_to_all(
        jnp.broadcast_to(found, (COLS,) + found.shape), "col", 0, 0, tiled=True
    ).reshape(rows, -1)
    part = rhs_window.shape[2]
    owned = lax.ppermute(cut(gathered, part), ("row", "col"), work_to_window())
    size = panel.shape[0]
    parts = [
        (block, first, start + first)
        for block, start in ((panel, 0), (panel_other, size))
        for first in range(0, size, DEPTH)
    ]
    return owned, correct(solved, gathered, parts)


def solution(mesh):
    in_specs = (P(None, "row", "col"), P("row", "col"), P("col", None, "row"), P(), P())
    out_specs = (P("col", None, "row"), P("row", "col"))
    return jax.shard_map(shards, mesh=mesh, in_specs=in_specs, out_specs=out_specs, check_vma=False)
```

```python
import jax
import jax.numpy as jnp
from jax import lax
from jax.experimental import pallas as pl
from jax.experimental.pallas import tpu as pltpu
from jax.sharding import PartitionSpec as P

PLANES = 8
CORES = 2
ROWS = PLANES * CORES
HALF_RING = ROWS // 2
COLS = 32
TAIL = 8
LANES = 256
MIB = 1024 * 1024


def core_swap():
    return [(row, row ^ 1) for row in range(ROWS)]


def apart(step):
    return [
        (plane * CORES + core, (plane + (step, -step)[core]) % PLANES * CORES + core)
        for plane in range(PLANES)
        for core in range(CORES)
    ]


def work_to_window():
    return [
        (row * COLS + col, (col // 2) * COLS + 2 * row + col % 2)
        for row in range(ROWS)
        for col in range(COLS)
    ]


def halves(x):
    high = x.astype(jnp.bfloat16)
    return high, (x - high.astype(jnp.float32)).astype(jnp.bfloat16)


def rounded_dot(left, right, contract):
    (left_up, left_down), (right_up, right_down) = left, right

    def one(x, y):
        return lax.dot_general(x, y, (contract, ((), ())), preferred_element_type=jnp.float32)

    return one(left_up, right_up) + one(left_down, right_up) + one(left_up, right_down)


def in_vmem():
    return pl.BlockSpec(memory_space=pltpu.VMEM)


def kernel_call(body, out_shape, in_specs, out_specs, scratch=(), mib=16, flops=0, moved=0):
    return pl.pallas_call(
        body,
        out_shape=out_shape,
        in_specs=in_specs,
        out_specs=out_specs,
        scratch_shapes=scratch,
        compiler_params=pltpu.CompilerParams(vmem_limit_bytes=mib * MIB),
        cost_estimate=pl.CostEstimate(flops=flops, bytes_accessed=moved, transcendentals=0),
    )


def position():
    row = lax.axis_index("row")
    return row // CORES, row % CORES


def anywhere():
    return pl.BlockSpec(memory_space=pl.ANY)


def in_hbm():
    return pl.BlockSpec(memory_space=pltpu.MemorySpace.HBM)


def with_window(factor, rhs_window):
    panels, part, width = factor.shape
    rows = panels * part
    groups = width // LANES

    def body(factor_ref, window_ref, out_ref):
        count = window_ref.shape[0]
        for k in range(panels):
            turned = window_ref[:, k].T
            for g in range(part // TAIL):
                at = (k * (part // TAIL) + g) * count
                out_ref[groups * rows :, at : at + count] = turned[g * TAIL : (g + 1) * TAIL]
            for g in range(groups):
                at = g * rows + k * part
                out_ref[at : at + part] = factor_ref[k, :, g * LANES : (g + 1) * LANES]

    return kernel_call(
        body,
        jax.ShapeDtypeStruct((groups * rows + TAIL, LANES), factor.dtype),
        [in_vmem()] * 2,
        in_vmem(),
        mib=16,
        moved=8 * factor.size,
    )(factor, rhs_window)


def join(one, two, arrivals=()):
    def body(one_ref, two_ref, *refs):
        out_ref, sems = refs[-2:]
        rows = one_ref.shape[0]
        first = pltpu.make_async_copy(one_ref, out_ref.at[:rows], sems.at[0])
        second = pltpu.make_async_copy(two_ref, out_ref.at[rows:], sems.at[1])
        first.start()
        second.start()
        first.wait()
        second.wait()

    shape = (one.shape[0] + two.shape[0], one.shape[1])
    return kernel_call(
        body,
        jax.ShapeDtypeStruct(shape, one.dtype),
        [anywhere()] * (2 + len(arrivals)),
        anywhere(),
        scratch=[pltpu.SemaphoreType.DMA((2,))],
        mib=2,
        moved=16 * one.size,
    )(one, two, *arrivals)


def anywhere():
    return pl.BlockSpec(memory_space=pl.ANY)


def reduce_panel(solved, solved_other, pairs, last):
    rows, width = solved.shape
    groups = width // LANES
    block = last.shape[0]
    part = (block - TAIL) // (2 * groups)
    side = HALF_RING * part
    unknowns = 2 * side
    each = rows // COLS
    count = rows // 2

    def body(solved_ref, other_ref, *refs):
        *pair_refs, last_ref, out_ref, panel, window, partial = refs
        (plane, core), col = position(), lax.axis_index("col")

        def put(place, ref, at):
            base = at * block
            first = jnp.where(core == 0, HALF_RING - 1 - place, place) * part
            for k in range(2):
                start = pl.multiple_of(first + k * side, part)
                for g in range(groups):
                    row = base + (2 * g + k) * part
                    panel[pl.ds(start, part), g * LANES : (g + 1) * LANES] = ref[row : row + part]
                for g in range(part // TAIL):
                    lanes = (k * (part // TAIL) + g) * count
                    window[pl.ds(start + g * TAIL, TAIL)] = ref[
                        base + block - TAIL : base + block, lanes : lanes + count
                    ]

        put(0, pair_refs[0], 0)
        for step, ref in enumerate(pair_refs[1:], start=1):
            put(2 * step, ref, 0)
            put(2 * step - 1, ref, 1)
        put(HALF_RING - 1, last_ref, 0)
        solved_pair = jnp.concatenate([solved_ref[...], other_ref[...]], axis=0)
        total = rounded_dot(halves(panel[...]), halves(solved_pair), ((1,), (1,)))
        spread = jnp.concatenate([window[...]] * (2 * rows // count), axis=1)
        lane = lax.broadcasted_iota(jnp.int32, spread.shape, 1)
        mine = 2 * ((col // 2 % CORES) ^ core) + col % 2
        mine = jnp.where(plane == col // (2 * CORES), mine, -1)
        partial[...] = (jnp.where(lane // count == mine, spread, 0.0) - total).T
        for member in range(COLS):
            at = member * each
            out_ref[member, :each] = partial[at : at + each]
            out_ref[member, each:] = partial[rows + at : rows + at + each]

    return kernel_call(
        body,
        [
            jax.ShapeDtypeStruct((COLS, 2 * each, unknowns), jnp.float32),
            jax.ShapeDtypeStruct((unknowns, width), jnp.float32),
        ],
        [in_vmem()] * (3 + len(pairs)),
        [in_vmem()] * 2,
        scratch=[
            pltpu.VMEM((unknowns, count), jnp.float32),
            pltpu.VMEM((2 * rows, unknowns), jnp.float32),
        ],
        mib=32,
        flops=12 * rows * unknowns * width,
        moved=8 * unknowns * width,
    )(solved, solved_other, *pairs, last)


def panel_solve(residual, residual_other, inverses, coupling, arrival):
    each, size = residual.shape
    side = size // 2
    part = side // HALF_RING
    deep = 16

    def body(residual_ref, other_ref, inverses_ref, coupling_ref, _, out_ref, padded):
        plane, core = position()
        first = (CORES * plane + HALF_RING + 1 + core * HALF_RING) % ROWS

        def times(x, matrix, across):
            up, down = halves(x)
            contract = (((1,), (1 if across else 0,)), ((), ()))
            both = lax.dot_general(
                jnp.concatenate([up, down], axis=0),
                matrix[0],
                contract,
                preferred_element_type=jnp.float32,
            )
            rest = lax.dot_general(up, matrix[1], contract, preferred_element_type=jnp.float32)
            return both[:deep] + both[deep:] + rest

        padded[...] = jnp.zeros_like(padded)
        for k in range(2):
            padded[k, :each, :side] = residual_ref[:, k * side : (k + 1) * side]
            padded[k, :each, side:] = other_ref[:, k * side : (k + 1) * side]
        turned = [pltpu.roll(padded[k], first * part, 1) for k in range(2)]
        lead, follow, link = halves(inverses_ref[0]), halves(inverses_ref[1]), halves(coupling_ref[...])
        forward_lead = times(turned[0], lead, True)
        forward_next = times(turned[1] - times(forward_lead, link, True), follow, True)
        backward_next = times(forward_next, follow, False)
        backward_lead = times(forward_lead - times(backward_next, link, False), lead, False)
        back = (ROWS - first) % ROWS
        for k, found in enumerate((backward_lead, backward_next)):
            found = pltpu.roll(found, back * part, 1)[:each]
            out_ref[:, k * side : (k + 1) * side] = found[:, :side]
            out_ref[:, size + k * side : size + (k + 1) * side] = found[:, side:]

    return kernel_call(
        body,
        jax.ShapeDtypeStruct((each, 2 * size), residual.dtype),
        [in_vmem()] * 5,
        in_vmem(),
        scratch=[pltpu.VMEM((2, deep, size), jnp.float32)],
        flops=36 * deep * size * size,
        moved=12 * size * size,
    )(residual, residual_other, inverses, coupling, arrival)


def correct(solved, found, panel, panel_other):
    rows, width = solved.shape
    size = panel.shape[0]
    chunk = size // 2

    def body(solved_ref, found_ref, panel_ref, other_ref, out_ref, held, sems):
        copies = [
            pltpu.make_async_copy(ref.at[at : at + chunk], held.at[i], sems.at[i])
            for i, (ref, at) in enumerate(
                (ref, at) for ref in (panel_ref, other_ref) for at in range(0, size, chunk)
            )
        ]
        for copy in copies:
            copy.start()
        total = jnp.zeros((rows, width), jnp.float32)
        for i, copy in enumerate(copies):
            up, down = halves(found_ref[:, i * chunk : (i + 1) * chunk])
            copy.wait()
            panel_up, panel_down = halves(held[i])
            both = jnp.dot(
                jnp.concatenate([up, down], axis=0), panel_up, preferred_element_type=jnp.float32
            )
            rest = jnp.dot(up, panel_down, preferred_element_type=jnp.float32)
            total += both[:rows] + both[rows:] + rest
        out_ref[...] = solved_ref[...] - total

    return kernel_call(
        body,
        jax.ShapeDtypeStruct(solved.shape, solved.dtype),
        [in_vmem()] * 2 + [in_hbm()] * 2,
        in_vmem(),
        scratch=[
            pltpu.VMEM((2 * size // chunk, chunk, width), jnp.float32),
            pltpu.SemaphoreType.DMA((2 * size // chunk,)),
        ],
        flops=36 * rows * found.shape[1] * width,
        moved=4 * found.shape[1] * width,
    )(solved, found, panel, panel_other)


def cut(found, part):
    rows, width = found.shape
    size = width // 2
    side = size // 2

    def body(found_ref, owned_ref):
        (plane, core), col = position(), lax.axis_index("col")
        place = (col // 2 - CORES * plane + ROWS + HALF_RING - 1) % ROWS
        keeper = (place // HALF_RING) ^ core
        first = pl.multiple_of(col % 2 * (rows // 2), rows // 2)
        back = (HALF_RING - place % HALF_RING) % HALF_RING
        for k in range(2):
            start = pl.multiple_of(keeper * size + k * side, side)
            block = found_ref[pl.ds(first, rows // 2), pl.ds(start, side)]
            owned_ref[:, k] = pltpu.roll(block, back * part, 1)[:, : owned_ref.shape[2]]

    return kernel_call(
        body,
        jax.ShapeDtypeStruct((rows // 2, 2, part), found.dtype),
        [in_vmem()],
        in_vmem(),
        moved=4 * rows * part,
    )(found)


def shards(factor, solved, rhs_window, inverses, coupling):
    rows = solved.shape[0]
    own = with_window(factor, rhs_window)
    other = lax.ppermute(own, "row", core_swap())
    two_own = lax.ppermute(own, "row", apart(2))
    two_other = lax.ppermute(other, "row", apart(2))
    both = join(own, other)
    one = lax.ppermute(both, "row", apart(1))
    solved_other = lax.ppermute(solved, "row", core_swap())
    four = lax.ppermute(two_other, "row", apart(2))
    two = join(two_own, two_other, (solved_other,))
    three = lax.ppermute(two, "row", apart(1))
    partial, panel = reduce_panel(solved, solved_other, [both, one, two, three], four)

    panel_other = lax.ppermute(panel, "row", core_swap())

    each = rows // COLS
    residual = jnp.sum(lax.all_to_all(partial, "col", 0, 0, tiled=True), axis=0)
    residual_other = lax.ppermute(residual[each:], "row", core_swap())
    found = panel_solve(residual[:each], residual_other, inverses, coupling, panel_other[:8, :128])
    gathered = lax.all_to_all(
        jnp.broadcast_to(found, (COLS,) + found.shape), "col", 0, 0, tiled=True
    ).reshape(rows, -1)
    part = rhs_window.shape[2]
    owned = lax.ppermute(cut(gathered, part), ("row", "col"), work_to_window())
    return owned, correct(solved, gathered, panel, panel_other)


def solution(mesh):
    in_specs = (P(None, "row", "col"), P("row", "col"), P("col", None, "row"), P(), P())
    out_specs = (P("col", None, "row"), P("row", "col"))
    return jax.shard_map(shards, mesh=mesh, in_specs=in_specs, out_specs=out_specs, check_vma=False)
```

```python
import jax
import jax.numpy as jnp
from jax import lax
from jax.experimental import pallas as pl
from jax.experimental.pallas import tpu as pltpu
from jax.sharding import PartitionSpec as P

PLANES = 8
CORES = 2
ROWS = PLANES * CORES
HALF_RING = ROWS // 2
COLS = 32
TAIL = 8
LANES = 256
GROUPS = 3
MIB = 1024 * 1024


def core_swap():
    return [(row, row ^ 1) for row in range(ROWS)]


def apart(step):
    return [
        (plane * CORES + core, (plane + (step, -step)[core]) % PLANES * CORES + core)
        for plane in range(PLANES)
        for core in range(CORES)
    ]


def work_to_window():
    return [
        (row * COLS + col, (col // 2) * COLS + 2 * row + col % 2)
        for row in range(ROWS)
        for col in range(COLS)
    ]


def halves(x):
    high = x.astype(jnp.bfloat16)
    return high, (x - high.astype(jnp.float32)).astype(jnp.bfloat16)


def rounded_dot(left, right, contract):
    (left_up, left_down), (right_up, right_down) = left, right

    def one(x, y):
        return lax.dot_general(x, y, (contract, ((), ())), preferred_element_type=jnp.float32)

    return one(left_up, right_up) + one(left_down, right_up) + one(left_up, right_down)


def in_vmem():
    return pl.BlockSpec(memory_space=pltpu.VMEM)


def kernel_call(body, out_shape, in_specs, out_specs, scratch=(), mib=16, flops=0, moved=0):
    return pl.pallas_call(
        body,
        out_shape=out_shape,
        in_specs=in_specs,
        out_specs=out_specs,
        scratch_shapes=scratch,
        compiler_params=pltpu.CompilerParams(vmem_limit_bytes=mib * MIB),
        cost_estimate=pl.CostEstimate(flops=flops, bytes_accessed=moved, transcendentals=0),
    )


def position():
    row = lax.axis_index("row")
    return row // CORES, row % CORES


def anywhere():
    return pl.BlockSpec(memory_space=pl.ANY)


def in_hbm():
    return pl.BlockSpec(memory_space=pltpu.MemorySpace.HBM)


def with_window(factor, rhs_window):
    panels, part, width = factor.shape
    rows = panels * part
    groups = width // LANES

    def body(factor_ref, window_ref, out_ref):
        count = window_ref.shape[0]
        for k in range(panels):
            turned = window_ref[:, k].T
            for g in range(part // TAIL):
                at = (k * (part // TAIL) + g) * count
                out_ref[groups * rows :, at : at + count] = turned[g * TAIL : (g + 1) * TAIL]
            for g in range(groups):
                at = g * rows + k * part
                out_ref[at : at + part] = factor_ref[k, :, g * LANES : (g + 1) * LANES]

    return kernel_call(
        body,
        jax.ShapeDtypeStruct((groups * rows + TAIL, LANES), factor.dtype),
        [in_vmem()] * 2,
        in_vmem(),
        mib=16,
        moved=8 * factor.size,
    )(factor, rhs_window)


def join(one, two, arrivals=()):
    def body(one_ref, two_ref, *refs):
        out_ref, sems = refs[-2:]
        rows = one_ref.shape[0]
        first = pltpu.make_async_copy(one_ref, out_ref.at[:rows], sems.at[0])
        second = pltpu.make_async_copy(two_ref, out_ref.at[rows:], sems.at[1])
        first.start()
        second.start()
        first.wait()
        second.wait()

    shape = (one.shape[0] + two.shape[0], one.shape[1])
    return kernel_call(
        body,
        jax.ShapeDtypeStruct(shape, one.dtype),
        [anywhere()] * (2 + len(arrivals)),
        anywhere(),
        scratch=[pltpu.SemaphoreType.DMA((2,))],
        mib=2,
        moved=16 * one.size,
    )(one, two, *arrivals)


def anywhere():
    return pl.BlockSpec(memory_space=pl.ANY)


def unit_rows(place, part):
    core = position()[1]
    first = jnp.where(core == 0, HALF_RING - 1 - place, place) * part
    return [pl.multiple_of(first + k * HALF_RING * part, part) for k in range(2)]


def block_rows(ref, base, part, k):
    return [ref[base + (2 * g + k) * part : base + (2 * g + k + 1) * part] for g in range(GROUPS)]


def block_window(ref, base, part, k, count):
    base += 2 * part * GROUPS
    per = part // TAIL
    return [
        ref[base : base + TAIL, (k * per + g) * count : (k * per + g + 1) * count]
        for g in range(per)
    ]


def spread_window(window, rows):
    (plane, core), col = position(), lax.axis_index("col")
    count = window.shape[1]
    spread = jnp.concatenate([window] * (2 * rows // count), axis=1)
    lane = lax.broadcasted_iota(jnp.int32, spread.shape, 1)
    mine = 2 * ((col // 2 % CORES) ^ core) + col % 2
    mine = jnp.where(plane == col // (2 * CORES), mine, -1)
    return jnp.where(lane // count == mine, spread, 0.0)


def reduce_early(solved, solved_other, blocks, part):
    rows, width = solved.shape
    unknowns = 2 * HALF_RING * part
    count = rows // 2
    arrays = list({id(array): array for array, _, _ in blocks}.values())
    index = {id(array): i for i, array in enumerate(arrays)}
    missing = [place for place in range(HALF_RING) if place not in {p for _, _, p in blocks}]

    def body(solved_ref, other_ref, *refs):
        *array_refs, total_ref, panel, window = refs
        for array, base, place in blocks:
            ref = array_refs[index[id(array)]]
            for k, start in enumerate(unit_rows(place, part)):
                for g, value in enumerate(block_rows(ref, base, part, k)):
                    panel[pl.ds(start, part), g * LANES : (g + 1) * LANES] = value
                for g, value in enumerate(block_window(ref, base, part, k, count)):
                    window[pl.ds(start + g * TAIL, TAIL)] = value
        for place in missing:
            for start in unit_rows(place, part):
                panel[pl.ds(start, part)] = jnp.zeros((part, width), jnp.float32)
                window[pl.ds(start, part)] = jnp.zeros((part, count), jnp.float32)
        solved_pair = jnp.concatenate([solved_ref[...], other_ref[...]], axis=0)
        total = rounded_dot(halves(panel[...]), halves(solved_pair), ((1,), (1,)))
        total_ref[...] = spread_window(window[...], rows) - total

    return kernel_call(
        body,
        [
            jax.ShapeDtypeStruct((unknowns, 2 * rows), jnp.float32),
            jax.ShapeDtypeStruct((unknowns, width), jnp.float32),
        ],
        [in_vmem()] * (2 + len(arrays)),
        [in_vmem()] * 2,
        scratch=[pltpu.VMEM((unknowns, count), jnp.float32)],
        mib=32,
        flops=12 * rows * unknowns * width,
        moved=8 * unknowns * width,
    )(solved, solved_other, *arrays)


def reduce_late(solved, solved_other, total, panel, array, places, part):
    rows, width = solved.shape
    unknowns = total.shape[0]
    each = rows // COLS
    count = rows // 2
    block = array.shape[0] // len(places)
    runs = 2 * len(places)

    def body(solved_ref, other_ref, total_ref, _, ref, out_ref, panel_ref, held, window, sums, sems):
        starts = [start for place in places for start in unit_rows(place, part)]
        for i in range(runs):
            at, k = i // 2 * block, i % 2
            for g, value in enumerate(block_rows(ref, at, part, k)):
                held[i * part : (i + 1) * part, g * LANES : (g + 1) * LANES] = value
            for g, value in enumerate(block_window(ref, at, part, k, count)):
                window[i * part + g * TAIL : i * part + (g + 1) * TAIL] = value
        copies = [
            pltpu.make_async_copy(
                held.at[i * part : (i + 1) * part], panel_ref.at[pl.ds(start, part)], sems.at[i]
            )
            for i, start in enumerate(starts)
        ]
        for copy in copies:
            copy.start()
        solved_pair = jnp.concatenate([solved_ref[...], other_ref[...]], axis=0)
        late = rounded_dot(halves(held[...]), halves(solved_pair), ((1,), (1,)))
        late = spread_window(window[...], rows) - late
        sums[...] = total_ref[...]
        for i, start in enumerate(starts):
            sums[pl.ds(start, part)] = late[i * part : (i + 1) * part]
        partial = sums[...].T
        for member in range(COLS):
            at = member * each
            out_ref[member, :each] = partial[at : at + each]
            out_ref[member, each:] = partial[rows + at : rows + at + each]
        for copy in copies:
            copy.wait()

    return pl.pallas_call(
        body,
        out_shape=[
            jax.ShapeDtypeStruct((COLS, 2 * each, unknowns), jnp.float32),
            jax.ShapeDtypeStruct(panel.shape, panel.dtype),
        ],
        in_specs=[in_vmem()] * 3 + [anywhere(), in_vmem()],
        out_specs=[in_vmem(), anywhere()],
        scratch_shapes=[
            pltpu.VMEM((runs * part, width), jnp.float32),
            pltpu.VMEM((runs * part, count), jnp.float32),
            pltpu.VMEM((unknowns, 2 * rows), jnp.float32),
            pltpu.SemaphoreType.DMA((runs,)),
        ],
        input_output_aliases={3: 1},
        compiler_params=pltpu.CompilerParams(vmem_limit_bytes=32 * MIB),
        cost_estimate=pl.CostEstimate(
            flops=12 * rows * runs * part * width, bytes_accessed=8 * unknowns * width, transcendentals=0
        ),
    )(solved, solved_other, total, panel, array)


def panel_solve(residual, residual_other, inverses, coupling, arrival):
    each, size = residual.shape
    side = size // 2
    part = side // HALF_RING
    deep = 16

    def body(residual_ref, other_ref, inverses_ref, coupling_ref, _, out_ref, padded):
        plane, core = position()
        first = (CORES * plane + HALF_RING + 1 + core * HALF_RING) % ROWS

        def times(x, matrix, across):
            up, down = halves(x)
            contract = (((1,), (1 if across else 0,)), ((), ()))
            both = lax.dot_general(
                jnp.concatenate([up, down], axis=0),
                matrix[0],
                contract,
                preferred_element_type=jnp.float32,
            )
            rest = lax.dot_general(up, matrix[1], contract, preferred_element_type=jnp.float32)
            return both[:deep] + both[deep:] + rest

        padded[...] = jnp.zeros_like(padded)
        for k in range(2):
            padded[k, :each, :side] = residual_ref[:, k * side : (k + 1) * side]
            padded[k, :each, side:] = other_ref[:, k * side : (k + 1) * side]
        turned = [pltpu.roll(padded[k], first * part, 1) for k in range(2)]
        lead, follow, link = halves(inverses_ref[0]), halves(inverses_ref[1]), halves(coupling_ref[...])
        forward_lead = times(turned[0], lead, True)
        forward_next = times(turned[1] - times(forward_lead, link, True), follow, True)
        backward_next = times(forward_next, follow, False)
        backward_lead = times(forward_lead - times(backward_next, link, False), lead, False)
        back = (ROWS - first) % ROWS
        for k, found in enumerate((backward_lead, backward_next)):
            found = pltpu.roll(found, back * part, 1)[:each]
            out_ref[:, k * side : (k + 1) * side] = found[:, :side]
            out_ref[:, size + k * side : size + (k + 1) * side] = found[:, side:]

    return kernel_call(
        body,
        jax.ShapeDtypeStruct((each, 2 * size), residual.dtype),
        [in_vmem()] * 5,
        in_vmem(),
        scratch=[pltpu.VMEM((2, deep, size), jnp.float32)],
        flops=36 * deep * size * size,
        moved=12 * size * size,
    )(residual, residual_other, inverses, coupling, arrival)


def correct(solved, found, panel, panel_other):
    rows, width = solved.shape
    size = panel.shape[0]
    chunk = size // 2

    def body(solved_ref, found_ref, panel_ref, other_ref, out_ref, held, sems):
        copies = [
            pltpu.make_async_copy(ref.at[at : at + chunk], held.at[i], sems.at[i])
            for i, (ref, at) in enumerate(
                (ref, at) for ref in (panel_ref, other_ref) for at in range(0, size, chunk)
            )
        ]
        for copy in copies:
            copy.start()
        total = jnp.zeros((rows, width), jnp.float32)
        for i, copy in enumerate(copies):
            up, down = halves(found_ref[:, i * chunk : (i + 1) * chunk])
            copy.wait()
            panel_up, panel_down = halves(held[i])
            both = jnp.dot(
                jnp.concatenate([up, down], axis=0), panel_up, preferred_element_type=jnp.float32
            )
            rest = jnp.dot(up, panel_down, preferred_element_type=jnp.float32)
            total += both[:rows] + both[rows:] + rest
        out_ref[...] = solved_ref[...] - total

    return kernel_call(
        body,
        jax.ShapeDtypeStruct(solved.shape, solved.dtype),
        [in_vmem()] * 2 + [in_hbm()] * 2,
        in_vmem(),
        scratch=[
            pltpu.VMEM((2 * size // chunk, chunk, width), jnp.float32),
            pltpu.SemaphoreType.DMA((2 * size // chunk,)),
        ],
        flops=36 * rows * found.shape[1] * width,
        moved=4 * found.shape[1] * width,
    )(solved, found, panel, panel_other)


def cut(found, part):
    rows, width = found.shape
    size = width // 2
    side = size // 2

    def body(found_ref, owned_ref):
        (plane, core), col = position(), lax.axis_index("col")
        place = (col // 2 - CORES * plane + ROWS + HALF_RING - 1) % ROWS
        keeper = (place // HALF_RING) ^ core
        first = pl.multiple_of(col % 2 * (rows // 2), rows // 2)
        back = (HALF_RING - place % HALF_RING) % HALF_RING
        for k in range(2):
            start = pl.multiple_of(keeper * size + k * side, side)
            block = found_ref[pl.ds(first, rows // 2), pl.ds(start, side)]
            owned_ref[:, k] = pltpu.roll(block, back * part, 1)[:, : owned_ref.shape[2]]

    return kernel_call(
        body,
        jax.ShapeDtypeStruct((rows // 2, 2, part), found.dtype),
        [in_vmem()],
        in_vmem(),
        moved=4 * rows * part,
    )(found)


def shards(factor, solved, rhs_window, inverses, coupling):
    rows = solved.shape[0]
    own = with_window(factor, rhs_window)
    other = lax.ppermute(own, "row", core_swap())
    two_own = lax.ppermute(own, "row", apart(2))
    two_other = lax.ppermute(other, "row", apart(2))
    both = join(own, other)
    one = lax.ppermute(both, "row", apart(1))
    solved_other = lax.ppermute(solved, "row", core_swap())
    four = lax.ppermute(two_other, "row", apart(2))
    two = join(two_own, two_other, (solved_other,))
    three = lax.ppermute(two, "row", apart(1))
    part, block = factor.shape[1], own.shape[0]
    early = [(both, 0, 0), (one, 0, 2), (one, block, 1), (two, 0, 4), (two, block, 3)]
    early += [(three, 0, 6), (three, block, 5)]
    total, panel = reduce_early(solved, solved_other, early, part)
    partial, panel = reduce_late(solved, solved_other, total, panel, four, (HALF_RING - 1,), part)

    panel_other = lax.ppermute(panel, "row", core_swap())

    each = rows // COLS
    residual = jnp.sum(lax.all_to_all(partial, "col", 0, 0, tiled=True), axis=0)
    residual_other = lax.ppermute(residual[each:], "row", core_swap())
    found = panel_solve(residual[:each], residual_other, inverses, coupling, panel_other[:8, :128])
    gathered = lax.all_to_all(
        jnp.broadcast_to(found, (COLS,) + found.shape), "col", 0, 0, tiled=True
    ).reshape(rows, -1)
    part = rhs_window.shape[2]
    owned = lax.ppermute(cut(gathered, part), ("row", "col"), work_to_window())
    return owned, correct(solved, gathered, panel, panel_other)


def solution(mesh):
    in_specs = (P(None, "row", "col"), P("row", "col"), P("col", None, "row"), P(), P())
    out_specs = (P("col", None, "row"), P("row", "col"))
    return jax.shard_map(shards, mesh=mesh, in_specs=in_specs, out_specs=out_specs, check_vma=False)
```

```python
import jax
import jax.numpy as jnp
from jax import lax
from jax.experimental import pallas as pl
from jax.experimental.pallas import tpu as pltpu
from jax.sharding import PartitionSpec as P

PLANES = 8
CORES = 2
ROWS = PLANES * CORES
HALF_RING = ROWS // 2
COLS = 32
TAIL = 8
LANES = 256
GROUPS = 3
MIB = 1024 * 1024


def core_swap():
    return [(row, row ^ 1) for row in range(ROWS)]


def apart(step):
    return [
        (plane * CORES + core, (plane + (step, -step)[core]) % PLANES * CORES + core)
        for plane in range(PLANES)
        for core in range(CORES)
    ]


def work_to_window():
    return [
        (row * COLS + col, (col // 2) * COLS + 2 * row + col % 2)
        for row in range(ROWS)
        for col in range(COLS)
    ]


def halves(x):
    high = x.astype(jnp.bfloat16)
    return high, (x - high.astype(jnp.float32)).astype(jnp.bfloat16)


def rounded_dot(left, right, contract):
    (left_up, left_down), (right_up, right_down) = left, right

    def one(x, y):
        return lax.dot_general(x, y, (contract, ((), ())), preferred_element_type=jnp.float32)

    return one(left_up, right_up) + one(left_down, right_up) + one(left_up, right_down)


def in_vmem():
    return pl.BlockSpec(memory_space=pltpu.VMEM)


def kernel_call(body, out_shape, in_specs, out_specs, scratch=(), mib=16, flops=0, moved=0):
    return pl.pallas_call(
        body,
        out_shape=out_shape,
        in_specs=in_specs,
        out_specs=out_specs,
        scratch_shapes=scratch,
        compiler_params=pltpu.CompilerParams(vmem_limit_bytes=mib * MIB),
        cost_estimate=pl.CostEstimate(flops=flops, bytes_accessed=moved, transcendentals=0),
    )


def position():
    row = lax.axis_index("row")
    return row // CORES, row % CORES


def anywhere():
    return pl.BlockSpec(memory_space=pl.ANY)


def in_hbm():
    return pl.BlockSpec(memory_space=pltpu.MemorySpace.HBM)


def with_window(factor, rhs_window):
    panels, part, width = factor.shape
    rows = panels * part
    groups = width // LANES

    def body(factor_ref, window_ref, out_ref):
        count = window_ref.shape[0]
        for k in range(panels):
            turned = window_ref[:, k].T
            for g in range(part // TAIL):
                at = (k * (part // TAIL) + g) * count
                out_ref[groups * rows :, at : at + count] = turned[g * TAIL : (g + 1) * TAIL]
            for g in range(groups):
                at = g * rows + k * part
                out_ref[at : at + part] = factor_ref[k, :, g * LANES : (g + 1) * LANES]

    return kernel_call(
        body,
        jax.ShapeDtypeStruct((groups * rows + TAIL, LANES), factor.dtype),
        [in_vmem()] * 2,
        in_vmem(),
        mib=16,
        moved=8 * factor.size,
    )(factor, rhs_window)


def anywhere():
    return pl.BlockSpec(memory_space=pl.ANY)


def in_hbm():
    return pl.BlockSpec(memory_space=pltpu.MemorySpace.HBM)


def with_window(factor, rhs_window):
    panels, part, width = factor.shape
    rows = panels * part
    groups = width // LANES

    def body(factor_ref, window_ref, out_ref):
        count = window_ref.shape[0]
        for k in range(panels):
            turned = window_ref[:, k].T
            for g in range(part // TAIL):
                at = (k * (part // TAIL) + g) * count
                out_ref[groups * rows :, at : at + count] = turned[g * TAIL : (g + 1) * TAIL]
            for g in range(groups):
                at = g * rows + k * part
                out_ref[at : at + part] = factor_ref[k, :, g * LANES : (g + 1) * LANES]

    return kernel_call(
        body,
        jax.ShapeDtypeStruct((groups * rows + TAIL, LANES), factor.dtype),
        [in_vmem()] * 2,
        in_vmem(),
        mib=16,
        moved=8 * factor.size,
    )(factor, rhs_window)


def join(one, two, arrivals=()):
    def body(one_ref, two_ref, *refs):
        out_ref, sems = refs[-2:]
        rows = one_ref.shape[0]
        first = pltpu.make_async_copy(one_ref, out_ref.at[:rows], sems.at[0])
        second = pltpu.make_async_copy(two_ref, out_ref.at[rows:], sems.at[1])
        first.start()
        second.start()
        first.wait()
        second.wait()

    shape = (one.shape[0] + two.shape[0], one.shape[1])
    return kernel_call(
        body,
        jax.ShapeDtypeStruct(shape, one.dtype),
        [anywhere()] * (2 + len(arrivals)),
        anywhere(),
        scratch=[pltpu.SemaphoreType.DMA((2,))],
        mib=2,
        moved=16 * one.size,
    )(one, two, *arrivals)


def anywhere():
    return pl.BlockSpec(memory_space=pl.ANY)


def after(block, arrivals):
    def body(*refs):
        del refs

    return pl.pallas_call(
        body,
        out_shape=jax.ShapeDtypeStruct(block.shape, block.dtype),
        in_specs=[anywhere()] * (1 + len(arrivals)),
        out_specs=anywhere(),
        input_output_aliases={0: 0},
        compiler_params=pltpu.CompilerParams(vmem_limit_bytes=MIB),
    )(block, *arrivals)


def unit_rows(place, part):
    core = position()[1]
    first = jnp.where(core == 0, HALF_RING - 1 - place, place) * part
    return [pl.multiple_of(first + k * HALF_RING * part, part) for k in range(2)]


def block_rows(ref, base, part, k):
    return [ref[base + (2 * g + k) * part : base + (2 * g + k + 1) * part] for g in range(GROUPS)]


def block_window(ref, base, part, k, count):
    base += 2 * part * GROUPS
    per = part // TAIL
    return [
        ref[base : base + TAIL, (k * per + g) * count : (k * per + g + 1) * count]
        for g in range(per)
    ]


def spread_window(window, rows):
    (plane, core), col = position(), lax.axis_index("col")
    count = window.shape[1]
    spread = jnp.concatenate([window] * (2 * rows // count), axis=1)
    lane = lax.broadcasted_iota(jnp.int32, spread.shape, 1)
    mine = 2 * ((col // 2 % CORES) ^ core) + col % 2
    mine = jnp.where(plane == col // (2 * CORES), mine, -1)
    return jnp.where(lane // count == mine, spread, 0.0)


def reduce_early(solved, solved_other, blocks, part):
    rows, width = solved.shape
    unknowns = 2 * HALF_RING * part
    count = rows // 2
    arrays = list({id(array): array for array, _, _ in blocks}.values())
    index = {id(array): i for i, array in enumerate(arrays)}
    missing = [place for place in range(HALF_RING) if place not in {p for _, _, p in blocks}]

    def body(solved_ref, other_ref, *refs):
        *array_refs, total_ref, panel, window = refs
        for array, base, place in blocks:
            ref = array_refs[index[id(array)]]
            for k, start in enumerate(unit_rows(place, part)):
                for g, value in enumerate(block_rows(ref, base, part, k)):
                    panel[pl.ds(start, part), g * LANES : (g + 1) * LANES] = value
                for g, value in enumerate(block_window(ref, base, part, k, count)):
                    window[pl.ds(start + g * TAIL, TAIL)] = value
        for place in missing:
            for start in unit_rows(place, part):
                panel[pl.ds(start, part)] = jnp.zeros((part, width), jnp.float32)
                window[pl.ds(start, part)] = jnp.zeros((part, count), jnp.float32)
        solved_pair = jnp.concatenate([solved_ref[...], other_ref[...]], axis=0)
        total = rounded_dot(halves(panel[...]), halves(solved_pair), ((1,), (1,)))
        total_ref[...] = spread_window(window[...], rows) - total

    return kernel_call(
        body,
        [
            jax.ShapeDtypeStruct((unknowns, 2 * rows), jnp.float32),
            jax.ShapeDtypeStruct((unknowns, width), jnp.float32),
        ],
        [in_vmem()] * (2 + len(arrays)),
        [in_vmem()] * 2,
        scratch=[pltpu.VMEM((unknowns, count), jnp.float32)],
        mib=32,
        flops=12 * rows * unknowns * width,
        moved=8 * unknowns * width,
    )(solved, solved_other, *arrays)


def reduce_late(solved, solved_other, total, panel, array, places, part):
    rows, width = solved.shape
    unknowns = total.shape[0]
    each = rows // COLS
    count = rows // 2
    block = array.shape[0] // len(places)
    runs = 2 * len(places)

    def body(solved_ref, other_ref, total_ref, _, ref, out_ref, panel_ref, held, window, sums, sems):
        starts = [start for place in places for start in unit_rows(place, part)]
        for i in range(runs):
            at, k = i // 2 * block, i % 2
            for g, value in enumerate(block_rows(ref, at, part, k)):
                held[i * part : (i + 1) * part, g * LANES : (g + 1) * LANES] = value
            for g, value in enumerate(block_window(ref, at, part, k, count)):
                window[i * part + g * TAIL : i * part + (g + 1) * TAIL] = value
        copies = [
            pltpu.make_async_copy(
                held.at[i * part : (i + 1) * part], panel_ref.at[pl.ds(start, part)], sems.at[i]
            )
            for i, start in enumerate(starts)
        ]
        for copy in copies:
            copy.start()
        solved_pair = jnp.concatenate([solved_ref[...], other_ref[...]], axis=0)
        late = rounded_dot(halves(held[...]), halves(solved_pair), ((1,), (1,)))
        late = spread_window(window[...], rows) - late
        sums[...] = total_ref[...]
        for i, start in enumerate(starts):
            sums[pl.ds(start, part)] = late[i * part : (i + 1) * part]
        partial = sums[...].T
        for member in range(COLS):
            at = member * each
            out_ref[member, :each] = partial[at : at + each]
            out_ref[member, each:] = partial[rows + at : rows + at + each]
        for copy in copies:
            copy.wait()

    return pl.pallas_call(
        body,
        out_shape=[
            jax.ShapeDtypeStruct((COLS, 2 * each, unknowns), jnp.float32),
            jax.ShapeDtypeStruct(panel.shape, panel.dtype),
        ],
        in_specs=[in_vmem()] * 3 + [anywhere(), in_vmem()],
        out_specs=[in_vmem(), anywhere()],
        scratch_shapes=[
            pltpu.VMEM((runs * part, width), jnp.float32),
            pltpu.VMEM((runs * part, count), jnp.float32),
            pltpu.VMEM((unknowns, 2 * rows), jnp.float32),
            pltpu.SemaphoreType.DMA((runs,)),
        ],
        input_output_aliases={3: 1},
        compiler_params=pltpu.CompilerParams(vmem_limit_bytes=32 * MIB),
        cost_estimate=pl.CostEstimate(
            flops=12 * rows * runs * part * width, bytes_accessed=8 * unknowns * width, transcendentals=0
        ),
    )(solved, solved_other, total, panel, array)


def panel_solve(residual, residual_other, inverses, coupling, arrival):
    each, size = residual.shape
    side = size // 2
    part = side // HALF_RING
    deep = 16

    def body(residual_ref, other_ref, inverses_ref, coupling_ref, _, out_ref, padded):
        plane, core = position()
        first = (CORES * plane + HALF_RING + 1 + core * HALF_RING) % ROWS

        def times(x, matrix, across):
            up, down = halves(x)
            contract = (((1,), (1 if across else 0,)), ((), ()))
            both = lax.dot_general(
                jnp.concatenate([up, down], axis=0),
                matrix[0],
                contract,
                preferred_element_type=jnp.float32,
            )
            rest = lax.dot_general(up, matrix[1], contract, preferred_element_type=jnp.float32)
            return both[:deep] + both[deep:] + rest

        padded[...] = jnp.zeros_like(padded)
        for k in range(2):
            padded[k, :each, :side] = residual_ref[:, k * side : (k + 1) * side]
            padded[k, :each, side:] = other_ref[:, k * side : (k + 1) * side]
        turned = [pltpu.roll(padded[k], first * part, 1) for k in range(2)]
        lead, follow, link = halves(inverses_ref[0]), halves(inverses_ref[1]), halves(coupling_ref[...])
        forward_lead = times(turned[0], lead, True)
        forward_next = times(turned[1] - times(forward_lead, link, True), follow, True)
        backward_next = times(forward_next, follow, False)
        backward_lead = times(forward_lead - times(backward_next, link, False), lead, False)
        back = (ROWS - first) % ROWS
        for k, found in enumerate((backward_lead, backward_next)):
            found = pltpu.roll(found, back * part, 1)[:each]
            out_ref[:, k * side : (k + 1) * side] = found[:, :side]
            out_ref[:, size + k * side : size + (k + 1) * side] = found[:, side:]

    return kernel_call(
        body,
        jax.ShapeDtypeStruct((each, 2 * size), residual.dtype),
        [in_vmem()] * 5,
        in_vmem(),
        scratch=[pltpu.VMEM((2, deep, size), jnp.float32)],
        flops=36 * deep * size * size,
        moved=12 * size * size,
    )(residual, residual_other, inverses, coupling, arrival)


def correct(solved, found, panel, panel_other):
    rows, width = solved.shape
    size = panel.shape[0]
    chunk = size // 2

    def body(solved_ref, found_ref, panel_ref, other_ref, out_ref, held, sems):
        copies = [
            pltpu.make_async_copy(ref.at[at : at + chunk], held.at[i], sems.at[i])
            for i, (ref, at) in enumerate(
                (ref, at) for ref in (panel_ref, other_ref) for at in range(0, size, chunk)
            )
        ]
        for copy in copies:
            copy.start()
        total = jnp.zeros((rows, width), jnp.float32)
        for i, copy in enumerate(copies):
            up, down = halves(found_ref[:, i * chunk : (i + 1) * chunk])
            copy.wait()
            panel_up, panel_down = halves(held[i])
            both = jnp.dot(
                jnp.concatenate([up, down], axis=0), panel_up, preferred_element_type=jnp.float32
            )
            rest = jnp.dot(up, panel_down, preferred_element_type=jnp.float32)
            total += both[:rows] + both[rows:] + rest
        out_ref[...] = solved_ref[...] - total

    return kernel_call(
        body,
        jax.ShapeDtypeStruct(solved.shape, solved.dtype),
        [in_vmem()] * 2 + [in_hbm()] * 2,
        in_vmem(),
        scratch=[
            pltpu.VMEM((2 * size // chunk, chunk, width), jnp.float32),
            pltpu.SemaphoreType.DMA((2 * size // chunk,)),
        ],
        flops=36 * rows * found.shape[1] * width,
        moved=4 * found.shape[1] * width,
    )(solved, found, panel, panel_other)


def cut(found, part):
    rows, width = found.shape
    size = width // 2
    side = size // 2

    def body(found_ref, owned_ref):
        (plane, core), col = position(), lax.axis_index("col")
        place = (col // 2 - CORES * plane + ROWS + HALF_RING - 1) % ROWS
        keeper = (place // HALF_RING) ^ core
        first = pl.multiple_of(col % 2 * (rows // 2), rows // 2)
        back = (HALF_RING - place % HALF_RING) % HALF_RING
        for k in range(2):
            start = pl.multiple_of(keeper * size + k * side, side)
            block = found_ref[pl.ds(first, rows // 2), pl.ds(start, side)]
            owned_ref[:, k] = pltpu.roll(block, back * part, 1)[:, : owned_ref.shape[2]]

    return kernel_call(
        body,
        jax.ShapeDtypeStruct((rows // 2, 2, part), found.dtype),
        [in_vmem()],
        in_vmem(),
        moved=4 * rows * part,
    )(found)


def shards(factor, solved, rhs_window, inverses, coupling):
    rows = solved.shape[0]
    own = with_window(factor, rhs_window)
    other = lax.ppermute(own, "row", core_swap())
    two_own = lax.ppermute(own, "row", apart(2))
    two_other = lax.ppermute(other, "row", apart(2))
    both = join(own, other)
    one = lax.ppermute(both, "row", apart(1))
    solved_other = lax.ppermute(solved, "row", core_swap())
    three_own = lax.ppermute(two_own, "row", apart(1))
    two_other = after(two_other, (solved_other,))
    four = lax.ppermute(two_other, "row", apart(2))
    three_other = lax.ppermute(two_other, "row", apart(1))
    part, block = factor.shape[1], own.shape[0]
    early = [(both, 0, 0), (one, 0, 2), (one, block, 1), (two_own, 0, 4), (two_other, 0, 3)]
    early += [(four, 0, HALF_RING - 1), (three_own, 0, 6)]
    total, panel = reduce_early(solved, solved_other, early, part)
    partial, panel = reduce_late(solved, solved_other, total, panel, three_other, (5,), part)

    panel_other = lax.ppermute(panel, "row", core_swap())

    each = rows // COLS
    residual = jnp.sum(lax.all_to_all(partial, "col", 0, 0, tiled=True), axis=0)
    residual_other = lax.ppermute(residual[each:], "row", core_swap())
    found = panel_solve(residual[:each], residual_other, inverses, coupling, panel_other[:8, :128])
    gathered = lax.all_to_all(
        jnp.broadcast_to(found, (COLS,) + found.shape), "col", 0, 0, tiled=True
    ).reshape(rows, -1)
    part = rhs_window.shape[2]
    owned = lax.ppermute(cut(gathered, part), ("row", "col"), work_to_window())
    return owned, correct(solved, gathered, panel, panel_other)


def solution(mesh):
    in_specs = (P(None, "row", "col"), P("row", "col"), P("col", None, "row"), P(), P())
    out_specs = (P("col", None, "row"), P("row", "col"))
    return jax.shard_map(shards, mesh=mesh, in_specs=in_specs, out_specs=out_specs, check_vma=False)
```

```python
import jax
import jax.numpy as jnp
from jax import lax
from jax.experimental import pallas as pl
from jax.experimental.pallas import tpu as pltpu
from jax.sharding import PartitionSpec as P

PLANES = 8
CORES = 2
ROWS = PLANES * CORES
HALF_RING = ROWS // 2
COLS = 32
TAIL = 8
LANES = 256
GROUPS = 3
MIB = 1024 * 1024


def core_swap():
    return [(row, row ^ 1) for row in range(ROWS)]


def apart(step):
    return [
        (plane * CORES + core, (plane + (step, -step)[core]) % PLANES * CORES + core)
        for plane in range(PLANES)
        for core in range(CORES)
    ]


def work_to_window():
    return [
        (row * COLS + col, (col // 2) * COLS + 2 * row + col % 2)
        for row in range(ROWS)
        for col in range(COLS)
    ]


def halves(x):
    high = x.astype(jnp.bfloat16)
    return high, (x - high.astype(jnp.float32)).astype(jnp.bfloat16)


def rounded_dot(left, right, contract):
    (left_up, left_down), (right_up, right_down) = left, right

    def one(x, y):
        return lax.dot_general(x, y, (contract, ((), ())), preferred_element_type=jnp.float32)

    return one(left_up, right_up) + one(left_down, right_up) + one(left_up, right_down)


def in_vmem():
    return pl.BlockSpec(memory_space=pltpu.VMEM)


def kernel_call(body, out_shape, in_specs, out_specs, scratch=(), mib=16, flops=0, moved=0):
    return pl.pallas_call(
        body,
        out_shape=out_shape,
        in_specs=in_specs,
        out_specs=out_specs,
        scratch_shapes=scratch,
        compiler_params=pltpu.CompilerParams(vmem_limit_bytes=mib * MIB),
        cost_estimate=pl.CostEstimate(flops=flops, bytes_accessed=moved, transcendentals=0),
    )


def position():
    row = lax.axis_index("row")
    return row // CORES, row % CORES


def anywhere():
    return pl.BlockSpec(memory_space=pl.ANY)


def in_hbm():
    return pl.BlockSpec(memory_space=pltpu.MemorySpace.HBM)


def with_window(factor, rhs_window):
    panels, part, width = factor.shape
    rows = panels * part
    groups = width // LANES

    def body(factor_ref, window_ref, out_ref):
        count = window_ref.shape[0]
        for k in range(panels):
            turned = window_ref[:, k].T
            for g in range(part // TAIL):
                at = (k * (part // TAIL) + g) * count
                out_ref[groups * rows :, at : at + count] = turned[g * TAIL : (g + 1) * TAIL]
            for g in range(groups):
                at = g * rows + k * part
                out_ref[at : at + part] = factor_ref[k, :, g * LANES : (g + 1) * LANES]

    return kernel_call(
        body,
        jax.ShapeDtypeStruct((groups * rows + TAIL, LANES), factor.dtype),
        [in_vmem()] * 2,
        in_vmem(),
        mib=16,
        moved=8 * factor.size,
    )(factor, rhs_window)


def anywhere():
    return pl.BlockSpec(memory_space=pl.ANY)


def in_hbm():
    return pl.BlockSpec(memory_space=pltpu.MemorySpace.HBM)


def with_window(factor, rhs_window):
    panels, part, width = factor.shape
    rows = panels * part
    groups = width // LANES

    def body(factor_ref, window_ref, out_ref):
        count = window_ref.shape[0]
        for k in range(panels):
            turned = window_ref[:, k].T
            for g in range(part // TAIL):
                at = (k * (part // TAIL) + g) * count
                out_ref[groups * rows :, at : at + count] = turned[g * TAIL : (g + 1) * TAIL]
            for g in range(groups):
                at = g * rows + k * part
                out_ref[at : at + part] = factor_ref[k, :, g * LANES : (g + 1) * LANES]

    return kernel_call(
        body,
        jax.ShapeDtypeStruct((groups * rows + TAIL, LANES), factor.dtype),
        [in_vmem()] * 2,
        in_vmem(),
        mib=16,
        moved=8 * factor.size,
    )(factor, rhs_window)


def join(one, two, arrivals=()):
    def body(one_ref, two_ref, *refs):
        out_ref, sems = refs[-2:]
        rows = one_ref.shape[0]
        first = pltpu.make_async_copy(one_ref, out_ref.at[:rows], sems.at[0])
        second = pltpu.make_async_copy(two_ref, out_ref.at[rows:], sems.at[1])
        first.start()
        second.start()
        first.wait()
        second.wait()

    shape = (one.shape[0] + two.shape[0], one.shape[1])
    return kernel_call(
        body,
        jax.ShapeDtypeStruct(shape, one.dtype),
        [anywhere()] * (2 + len(arrivals)),
        anywhere(),
        scratch=[pltpu.SemaphoreType.DMA((2,))],
        mib=2,
        moved=16 * one.size,
    )(one, two, *arrivals)


def anywhere():
    return pl.BlockSpec(memory_space=pl.ANY)


def after(block, arrivals):
    def body(*refs):
        del refs

    return pl.pallas_call(
        body,
        out_shape=jax.ShapeDtypeStruct(block.shape, block.dtype),
        in_specs=[anywhere()] * (1 + len(arrivals)),
        out_specs=anywhere(),
        input_output_aliases={0: 0},
        compiler_params=pltpu.CompilerParams(vmem_limit_bytes=MIB),
    )(block, *arrivals)


def unit_rows(place, part):
    core = position()[1]
    first = jnp.where(core == 0, HALF_RING - 1 - place, place) * part
    return [pl.multiple_of(first + k * HALF_RING * part, part) for k in range(2)]


def block_rows(ref, base, part, k):
    return [ref[base + (2 * g + k) * part : base + (2 * g + k + 1) * part] for g in range(GROUPS)]


def block_window(ref, base, part, k, count):
    base += 2 * part * GROUPS
    per = part // TAIL
    return [
        ref[base : base + TAIL, (k * per + g) * count : (k * per + g + 1) * count]
        for g in range(per)
    ]


def spread_window(window, rows):
    (plane, core), col = position(), lax.axis_index("col")
    count = window.shape[1]
    spread = jnp.concatenate([window] * (2 * rows // count), axis=1)
    lane = lax.broadcasted_iota(jnp.int32, spread.shape, 1)
    mine = 2 * ((col // 2 % CORES) ^ core) + col % 2
    mine = jnp.where(plane == col // (2 * CORES), mine, -1)
    return jnp.where(lane // count == mine, spread, 0.0)


def reduce_early(solved, solved_other, blocks, part):
    rows, width = solved.shape
    unknowns = 2 * HALF_RING * part
    count = rows // 2
    arrays = list({id(array): array for array, _, _ in blocks}.values())
    index = {id(array): i for i, array in enumerate(arrays)}
    missing = [place for place in range(HALF_RING) if place not in {p for _, _, p in blocks}]

    def body(solved_ref, other_ref, *refs):
        *array_refs, total_ref, panel, window = refs
        for array, base, place in blocks:
            ref = array_refs[index[id(array)]]
            for k, start in enumerate(unit_rows(place, part)):
                for g, value in enumerate(block_rows(ref, base, part, k)):
                    panel[pl.ds(start, part), g * LANES : (g + 1) * LANES] = value
                for g, value in enumerate(block_window(ref, base, part, k, count)):
                    window[pl.ds(start + g * TAIL, TAIL)] = value
        for place in missing:
            for start in unit_rows(place, part):
                panel[pl.ds(start, part)] = jnp.zeros((part, width), jnp.float32)
                window[pl.ds(start, part)] = jnp.zeros((part, count), jnp.float32)
        solved_pair = jnp.concatenate([solved_ref[...], other_ref[...]], axis=0)
        total = rounded_dot(halves(panel[...]), halves(solved_pair), ((1,), (1,)))
        total_ref[...] = spread_window(window[...], rows) - total

    return kernel_call(
        body,
        [
            jax.ShapeDtypeStruct((unknowns, 2 * rows), jnp.float32),
            jax.ShapeDtypeStruct((unknowns, width), jnp.float32),
        ],
        [in_vmem()] * (2 + len(arrays)),
        [in_vmem()] * 2,
        scratch=[pltpu.VMEM((unknowns, count), jnp.float32)],
        mib=32,
        flops=12 * rows * unknowns * width,
        moved=8 * unknowns * width,
    )(solved, solved_other, *arrays)


def reduce_late(solved, solved_other, total, panel, arrays, places, part):
    rows, width = solved.shape
    unknowns = total.shape[0]
    each = rows // COLS
    count = rows // 2
    runs = 2 * len(places)

    def body(solved_ref, other_ref, total_ref, _, *refs):
        *array_refs, out_ref, panel_ref, held, window, sums, sems = refs
        starts = [start for place in places for start in unit_rows(place, part)]
        for i in range(runs):
            ref, k = array_refs[i // 2], i % 2
            for g, value in enumerate(block_rows(ref, 0, part, k)):
                held[i * part : (i + 1) * part, g * LANES : (g + 1) * LANES] = value
            for g, value in enumerate(block_window(ref, 0, part, k, count)):
                window[i * part + g * TAIL : i * part + (g + 1) * TAIL] = value
        copies = [
            pltpu.make_async_copy(
                held.at[i * part : (i + 1) * part], panel_ref.at[pl.ds(start, part)], sems.at[i]
            )
            for i, start in enumerate(starts)
        ]
        for copy in copies:
            copy.start()
        solved_pair = jnp.concatenate([solved_ref[...], other_ref[...]], axis=0)
        late = rounded_dot(halves(held[...]), halves(solved_pair), ((1,), (1,)))
        late = spread_window(window[...], rows) - late
        sums[...] = total_ref[...]
        for i, start in enumerate(starts):
            sums[pl.ds(start, part)] = late[i * part : (i + 1) * part]
        partial = sums[...].T
        for member in range(COLS):
            at = member * each
            out_ref[member, :each] = partial[at : at + each]
            out_ref[member, each:] = partial[rows + at : rows + at + each]
        for copy in copies:
            copy.wait()

    return pl.pallas_call(
        body,
        out_shape=[
            jax.ShapeDtypeStruct((COLS, 2 * each, unknowns), jnp.float32),
            jax.ShapeDtypeStruct(panel.shape, panel.dtype),
        ],
        in_specs=[in_vmem()] * 3 + [anywhere()] + [in_vmem()] * len(arrays),
        out_specs=[in_vmem(), anywhere()],
        scratch_shapes=[
            pltpu.VMEM((runs * part, width), jnp.float32),
            pltpu.VMEM((runs * part, count), jnp.float32),
            pltpu.VMEM((unknowns, 2 * rows), jnp.float32),
            pltpu.SemaphoreType.DMA((runs,)),
        ],
        input_output_aliases={3: 1},
        compiler_params=pltpu.CompilerParams(vmem_limit_bytes=32 * MIB),
        cost_estimate=pl.CostEstimate(
            flops=12 * rows * runs * part * width, bytes_accessed=8 * unknowns * width, transcendentals=0
        ),
    )(solved, solved_other, total, panel, *arrays)


def panel_solve(residual, residual_other, inverses, coupling, arrival):
    each, size = residual.shape
    side = size // 2
    part = side // HALF_RING
    deep = 16

    def body(residual_ref, other_ref, inverses_ref, coupling_ref, _, out_ref, padded):
        plane, core = position()
        first = (CORES * plane + HALF_RING + 1 + core * HALF_RING) % ROWS

        def times(x, matrix, across):
            up, down = halves(x)
            contract = (((1,), (1 if across else 0,)), ((), ()))
            both = lax.dot_general(
                jnp.concatenate([up, down], axis=0),
                matrix[0],
                contract,
                preferred_element_type=jnp.float32,
            )
            rest = lax.dot_general(up, matrix[1], contract, preferred_element_type=jnp.float32)
            return both[:deep] + both[deep:] + rest

        padded[...] = jnp.zeros_like(padded)
        for k in range(2):
            padded[k, :each, :side] = residual_ref[:, k * side : (k + 1) * side]
            padded[k, :each, side:] = other_ref[:, k * side : (k + 1) * side]
        turned = [pltpu.roll(padded[k], first * part, 1) for k in range(2)]
        lead, follow, link = halves(inverses_ref[0]), halves(inverses_ref[1]), halves(coupling_ref[...])
        forward_lead = times(turned[0], lead, True)
        forward_next = times(turned[1] - times(forward_lead, link, True), follow, True)
        backward_next = times(forward_next, follow, False)
        backward_lead = times(forward_lead - times(backward_next, link, False), lead, False)
        back = (ROWS - first) % ROWS
        for k, found in enumerate((backward_lead, backward_next)):
            found = pltpu.roll(found, back * part, 1)[:each]
            out_ref[:, k * side : (k + 1) * side] = found[:, :side]
            out_ref[:, size + k * side : size + (k + 1) * side] = found[:, side:]

    return kernel_call(
        body,
        jax.ShapeDtypeStruct((each, 2 * size), residual.dtype),
        [in_vmem()] * 5,
        in_vmem(),
        scratch=[pltpu.VMEM((2, deep, size), jnp.float32)],
        flops=36 * deep * size * size,
        moved=12 * size * size,
    )(residual, residual_other, inverses, coupling, arrival)


def correct(solved, found, panel, panel_other):
    rows, width = solved.shape
    size = panel.shape[0]
    chunk = size // 2

    def body(solved_ref, found_ref, panel_ref, other_ref, out_ref, held, sems):
        copies = [
            pltpu.make_async_copy(ref.at[at : at + chunk], held.at[i], sems.at[i])
            for i, (ref, at) in enumerate(
                (ref, at) for ref in (panel_ref, other_ref) for at in range(0, size, chunk)
            )
        ]
        for copy in copies:
            copy.start()
        total = jnp.zeros((rows, width), jnp.float32)
        for i, copy in enumerate(copies):
            up, down = halves(found_ref[:, i * chunk : (i + 1) * chunk])
            copy.wait()
            panel_up, panel_down = halves(held[i])
            both = jnp.dot(
                jnp.concatenate([up, down], axis=0), panel_up, preferred_element_type=jnp.float32
            )
            rest = jnp.dot(up, panel_down, preferred_element_type=jnp.float32)
            total += both[:rows] + both[rows:] + rest
        out_ref[...] = solved_ref[...] - total

    return kernel_call(
        body,
        jax.ShapeDtypeStruct(solved.shape, solved.dtype),
        [in_vmem()] * 2 + [in_hbm()] * 2,
        in_vmem(),
        scratch=[
            pltpu.VMEM((2 * size // chunk, chunk, width), jnp.float32),
            pltpu.SemaphoreType.DMA((2 * size // chunk,)),
        ],
        flops=36 * rows * found.shape[1] * width,
        moved=4 * found.shape[1] * width,
    )(solved, found, panel, panel_other)


def cut(found, part):
    rows, width = found.shape
    size = width // 2
    side = size // 2

    def body(found_ref, owned_ref):
        (plane, core), col = position(), lax.axis_index("col")
        place = (col // 2 - CORES * plane + ROWS + HALF_RING - 1) % ROWS
        keeper = (place // HALF_RING) ^ core
        first = pl.multiple_of(col % 2 * (rows // 2), rows // 2)
        back = (HALF_RING - place % HALF_RING) % HALF_RING
        for k in range(2):
            start = pl.multiple_of(keeper * size + k * side, side)
            block = found_ref[pl.ds(first, rows // 2), pl.ds(start, side)]
            owned_ref[:, k] = pltpu.roll(block, back * part, 1)[:, : owned_ref.shape[2]]

    return kernel_call(
        body,
        jax.ShapeDtypeStruct((rows // 2, 2, part), found.dtype),
        [in_vmem()],
        in_vmem(),
        moved=4 * rows * part,
    )(found)


def shards(factor, solved, rhs_window, inverses, coupling):
    rows = solved.shape[0]
    own = with_window(factor, rhs_window)
    other = lax.ppermute(own, "row", core_swap())
    two_own = lax.ppermute(own, "row", apart(2))
    two_other = lax.ppermute(other, "row", apart(2))
    both = join(own, other)
    one = lax.ppermute(both, "row", apart(1))
    solved_other = lax.ppermute(solved, "row", core_swap())
    three_own = lax.ppermute(two_own, "row", apart(1))
    two_other = after(two_other, (solved_other,))
    four = lax.ppermute(two_other, "row", apart(2))
    three_other = lax.ppermute(two_other, "row", apart(1))
    part, block = factor.shape[1], own.shape[0]
    early = [(both, 0, 0), (one, 0, 2), (one, block, 1), (two_own, 0, 4), (two_other, 0, 3)]
    early += [(three_own, 0, 6)]
    total, panel = reduce_early(solved, solved_other, early, part)
    late = [four, three_other]
    partial, panel = reduce_late(
        solved, solved_other, total, panel, late, (HALF_RING - 1, 5), part
    )

    panel_other = lax.ppermute(panel, "row", core_swap())

    each = rows // COLS
    residual = jnp.sum(lax.all_to_all(partial, "col", 0, 0, tiled=True), axis=0)
    residual_other = lax.ppermute(residual[each:], "row", core_swap())
    found = panel_solve(residual[:each], residual_other, inverses, coupling, panel_other[:8, :128])
    gathered = lax.all_to_all(
        jnp.broadcast_to(found, (COLS,) + found.shape), "col", 0, 0, tiled=True
    ).reshape(rows, -1)
    part = rhs_window.shape[2]
    owned = lax.ppermute(cut(gathered, part), ("row", "col"), work_to_window())
    return owned, correct(solved, gathered, panel, panel_other)


def solution(mesh):
    in_specs = (P(None, "row", "col"), P("row", "col"), P("col", None, "row"), P(), P())
    out_specs = (P("col", None, "row"), P("row", "col"))
    return jax.shard_map(shards, mesh=mesh, in_specs=in_specs, out_specs=out_specs, check_vma=False)
```

```python
import jax
import jax.numpy as jnp
from jax import lax
from jax.experimental import pallas as pl
from jax.experimental.pallas import tpu as pltpu
from jax.sharding import PartitionSpec as P

PLANES = 8
CORES = 2
ROWS = PLANES * CORES
HALF_RING = ROWS // 2
COLS = 32
TAIL = 8
LANES = 256
GROUPS = 3
MIB = 1024 * 1024


def core_swap():
    return [(row, row ^ 1) for row in range(ROWS)]


def apart(step):
    return [
        (plane * CORES + core, (plane + (step, -step)[core]) % PLANES * CORES + core)
        for plane in range(PLANES)
        for core in range(CORES)
    ]


def work_to_window():
    return [
        (row * COLS + col, (col // 2) * COLS + 2 * row + col % 2)
        for row in range(ROWS)
        for col in range(COLS)
    ]


def halves(x):
    high = x.astype(jnp.bfloat16)
    return high, (x - high.astype(jnp.float32)).astype(jnp.bfloat16)


def rounded_dot(left, right, contract):
    (left_up, left_down), (right_up, right_down) = left, right

    def one(x, y):
        return lax.dot_general(x, y, (contract, ((), ())), preferred_element_type=jnp.float32)

    return one(left_up, right_up) + one(left_down, right_up) + one(left_up, right_down)


def in_vmem():
    return pl.BlockSpec(memory_space=pltpu.VMEM)


def kernel_call(body, out_shape, in_specs, out_specs, scratch=(), mib=16, flops=0, moved=0):
    return pl.pallas_call(
        body,
        out_shape=out_shape,
        in_specs=in_specs,
        out_specs=out_specs,
        scratch_shapes=scratch,
        compiler_params=pltpu.CompilerParams(vmem_limit_bytes=mib * MIB),
        cost_estimate=pl.CostEstimate(flops=flops, bytes_accessed=moved, transcendentals=0),
    )


def position():
    row = lax.axis_index("row")
    return row // CORES, row % CORES


def anywhere():
    return pl.BlockSpec(memory_space=pl.ANY)


def in_hbm():
    return pl.BlockSpec(memory_space=pltpu.MemorySpace.HBM)


def with_window(factor, rhs_window):
    panels, part, width = factor.shape
    rows = panels * part
    groups = width // LANES

    def body(factor_ref, window_ref, out_ref):
        count = window_ref.shape[0]
        for k in range(panels):
            turned = window_ref[:, k].T
            for g in range(part // TAIL):
                at = (k * (part // TAIL) + g) * count
                out_ref[groups * rows :, at : at + count] = turned[g * TAIL : (g + 1) * TAIL]
            for g in range(groups):
                at = g * rows + k * part
                out_ref[at : at + part] = factor_ref[k, :, g * LANES : (g + 1) * LANES]

    return kernel_call(
        body,
        jax.ShapeDtypeStruct((groups * rows + TAIL, LANES), factor.dtype),
        [in_vmem()] * 2,
        in_vmem(),
        mib=16,
        moved=8 * factor.size,
    )(factor, rhs_window)


def anywhere():
    return pl.BlockSpec(memory_space=pl.ANY)


def in_hbm():
    return pl.BlockSpec(memory_space=pltpu.MemorySpace.HBM)


def with_window(factor, rhs_window):
    panels, part, width = factor.shape
    rows = panels * part
    groups = width // LANES

    def body(factor_ref, window_ref, out_ref):
        count = window_ref.shape[0]
        for k in range(panels):
            turned = window_ref[:, k].T
            for g in range(part // TAIL):
                at = (k * (part // TAIL) + g) * count
                out_ref[groups * rows :, at : at + count] = turned[g * TAIL : (g + 1) * TAIL]
            for g in range(groups):
                at = g * rows + k * part
                out_ref[at : at + part] = factor_ref[k, :, g * LANES : (g + 1) * LANES]

    return kernel_call(
        body,
        jax.ShapeDtypeStruct((groups * rows + TAIL, LANES), factor.dtype),
        [in_vmem()] * 2,
        in_vmem(),
        mib=16,
        moved=8 * factor.size,
    )(factor, rhs_window)


def join(one, two, arrivals=()):
    def body(one_ref, two_ref, *refs):
        out_ref, sems = refs[-2:]
        rows = one_ref.shape[0]
        first = pltpu.make_async_copy(one_ref, out_ref.at[:rows], sems.at[0])
        second = pltpu.make_async_copy(two_ref, out_ref.at[rows:], sems.at[1])
        first.start()
        second.start()
        first.wait()
        second.wait()

    shape = (one.shape[0] + two.shape[0], one.shape[1])
    return kernel_call(
        body,
        jax.ShapeDtypeStruct(shape, one.dtype),
        [anywhere()] * (2 + len(arrivals)),
        anywhere(),
        scratch=[pltpu.SemaphoreType.DMA((2,))],
        mib=2,
        moved=16 * one.size,
    )(one, two, *arrivals)


def anywhere():
    return pl.BlockSpec(memory_space=pl.ANY)


def after(block, arrivals):
    def body(*refs):
        del refs

    return pl.pallas_call(
        body,
        out_shape=jax.ShapeDtypeStruct(block.shape, block.dtype),
        in_specs=[anywhere()] * (1 + len(arrivals)),
        out_specs=anywhere(),
        input_output_aliases={0: 0},
        compiler_params=pltpu.CompilerParams(vmem_limit_bytes=MIB),
    )(block, *arrivals)


def unit_rows(place, part):
    core = position()[1]
    first = jnp.where(core == 0, HALF_RING - 1 - place, place) * part
    return [pl.multiple_of(first + k * HALF_RING * part, part) for k in range(2)]


def block_rows(ref, base, part, k):
    return [ref[base + (2 * g + k) * part : base + (2 * g + k + 1) * part] for g in range(GROUPS)]


def block_window(ref, base, part, k, count):
    base += 2 * part * GROUPS
    per = part // TAIL
    return [
        ref[base : base + TAIL, (k * per + g) * count : (k * per + g + 1) * count]
        for g in range(per)
    ]


def spread_window(window, rows):
    (plane, core), col = position(), lax.axis_index("col")
    count = window.shape[1]
    spread = jnp.concatenate([window] * (2 * rows // count), axis=1)
    lane = lax.broadcasted_iota(jnp.int32, spread.shape, 1)
    mine = 2 * ((col // 2 % CORES) ^ core) + col % 2
    mine = jnp.where(plane == col // (2 * CORES), mine, -1)
    return jnp.where(lane // count == mine, spread, 0.0)


def reduce_early(solved, solved_other, blocks, part):
    rows, width = solved.shape
    unknowns = 2 * HALF_RING * part
    count = rows // 2
    arrays = list({id(array): array for array, _, _ in blocks}.values())
    index = {id(array): i for i, array in enumerate(arrays)}
    missing = [place for place in range(HALF_RING) if place not in {p for _, _, p in blocks}]

    def body(solved_ref, other_ref, *refs):
        *array_refs, total_ref, panel, window = refs
        for array, base, place in blocks:
            ref = array_refs[index[id(array)]]
            for k, start in enumerate(unit_rows(place, part)):
                for g, value in enumerate(block_rows(ref, base, part, k)):
                    panel[pl.ds(start, part), g * LANES : (g + 1) * LANES] = value
                for g, value in enumerate(block_window(ref, base, part, k, count)):
                    window[pl.ds(start + g * TAIL, TAIL)] = value
        for place in missing:
            for start in unit_rows(place, part):
                panel[pl.ds(start, part)] = jnp.zeros((part, width), jnp.float32)
                window[pl.ds(start, part)] = jnp.zeros((part, count), jnp.float32)
        solved_pair = jnp.concatenate([solved_ref[...], other_ref[...]], axis=0)
        total = rounded_dot(halves(panel[...]), halves(solved_pair), ((1,), (1,)))
        total_ref[...] = spread_window(window[...], rows) - total

    return kernel_call(
        body,
        [
            jax.ShapeDtypeStruct((unknowns, 2 * rows), jnp.float32),
            jax.ShapeDtypeStruct((unknowns, width), jnp.float32),
        ],
        [in_vmem()] * (2 + len(arrays)),
        [in_vmem()] * 2,
        scratch=[pltpu.VMEM((unknowns, count), jnp.float32)],
        mib=32,
        flops=12 * rows * unknowns * width,
        moved=8 * unknowns * width,
    )(solved, solved_other, *arrays)


def reduce_late(solved, solved_other, total, panel, array, places, part):
    rows, width = solved.shape
    unknowns = total.shape[0]
    each = rows // COLS
    count = rows // 2
    block = array.shape[0] // len(places)
    runs = 2 * len(places)

    def body(solved_ref, other_ref, total_ref, _, ref, out_ref, panel_ref, held, window, sums, sems):
        starts = [start for place in places for start in unit_rows(place, part)]
        for i in range(runs):
            at, k = i // 2 * block, i % 2
            for g, value in enumerate(block_rows(ref, at, part, k)):
                held[i * part : (i + 1) * part, g * LANES : (g + 1) * LANES] = value
            for g, value in enumerate(block_window(ref, at, part, k, count)):
                window[i * part + g * TAIL : i * part + (g + 1) * TAIL] = value
        copies = [
            pltpu.make_async_copy(
                held.at[i * part : (i + 1) * part], panel_ref.at[pl.ds(start, part)], sems.at[i]
            )
            for i, start in enumerate(starts)
        ]
        for copy in copies:
            copy.start()
        solved_pair = jnp.concatenate([solved_ref[...], other_ref[...]], axis=0)
        late = rounded_dot(halves(held[...]), halves(solved_pair), ((1,), (1,)))
        late = spread_window(window[...], rows) - late
        sums[...] = total_ref[...]
        for i, start in enumerate(starts):
            sums[pl.ds(start, part)] = late[i * part : (i + 1) * part]
        partial = sums[...].T
        for member in range(COLS):
            at = member * each
            out_ref[member, :each] = partial[at : at + each]
            out_ref[member, each:] = partial[rows + at : rows + at + each]
        for copy in copies:
            copy.wait()

    return pl.pallas_call(
        body,
        out_shape=[
            jax.ShapeDtypeStruct((COLS, 2 * each, unknowns), jnp.float32),
            jax.ShapeDtypeStruct(panel.shape, panel.dtype),
        ],
        in_specs=[in_vmem()] * 3 + [anywhere(), in_vmem()],
        out_specs=[in_vmem(), anywhere()],
        scratch_shapes=[
            pltpu.VMEM((runs * part, width), jnp.float32),
            pltpu.VMEM((runs * part, count), jnp.float32),
            pltpu.VMEM((unknowns, 2 * rows), jnp.float32),
            pltpu.SemaphoreType.DMA((runs,)),
        ],
        input_output_aliases={3: 1},
        compiler_params=pltpu.CompilerParams(vmem_limit_bytes=32 * MIB),
        cost_estimate=pl.CostEstimate(
            flops=12 * rows * runs * part * width, bytes_accessed=8 * unknowns * width, transcendentals=0
        ),
    )(solved, solved_other, total, panel, array)


def panel_solve(residual, residual_other, inverses, coupling, arrival):
    each, size = residual.shape
    side = size // 2
    part = side // HALF_RING
    deep = 16

    def body(residual_ref, other_ref, inverses_ref, coupling_ref, _, out_ref, padded):
        plane, core = position()
        first = (CORES * plane + HALF_RING + 1 + core * HALF_RING) % ROWS

        def times(x, matrix, across):
            up, down = halves(x)
            contract = (((1,), (1 if across else 0,)), ((), ()))
            both = lax.dot_general(
                jnp.concatenate([up, down], axis=0),
                matrix[0],
                contract,
                preferred_element_type=jnp.float32,
            )
            rest = lax.dot_general(up, matrix[1], contract, preferred_element_type=jnp.float32)
            return both[:deep] + both[deep:] + rest

        padded[...] = jnp.zeros_like(padded)
        for k in range(2):
            padded[k, :each, :side] = residual_ref[:, k * side : (k + 1) * side]
            padded[k, :each, side:] = other_ref[:, k * side : (k + 1) * side]
        turned = [pltpu.roll(padded[k], first * part, 1) for k in range(2)]
        lead, follow, link = halves(inverses_ref[0]), halves(inverses_ref[1]), halves(coupling_ref[...])
        forward_lead = times(turned[0], lead, True)
        forward_next = times(turned[1] - times(forward_lead, link, True), follow, True)
        backward_next = times(forward_next, follow, False)
        backward_lead = times(forward_lead - times(backward_next, link, False), lead, False)
        back = (ROWS - first) % ROWS
        for k, found in enumerate((backward_lead, backward_next)):
            found = pltpu.roll(found, back * part, 1)[:each]
            out_ref[:, k * side : (k + 1) * side] = found[:, :side]
            out_ref[:, size + k * side : size + (k + 1) * side] = found[:, side:]

    return kernel_call(
        body,
        jax.ShapeDtypeStruct((each, 2 * size), residual.dtype),
        [in_vmem()] * 5,
        in_vmem(),
        scratch=[pltpu.VMEM((2, deep, size), jnp.float32)],
        flops=36 * deep * size * size,
        moved=12 * size * size,
    )(residual, residual_other, inverses, coupling, arrival)


def correct(solved, found, panel, panel_other):
    rows, width = solved.shape
    size = panel.shape[0]
    chunk = size // 2

    def body(solved_ref, found_ref, panel_ref, other_ref, out_ref, held, sems):
        copies = [
            pltpu.make_async_copy(ref.at[at : at + chunk], held.at[i], sems.at[i])
            for i, (ref, at) in enumerate(
                (ref, at) for ref in (panel_ref, other_ref) for at in range(0, size, chunk)
            )
        ]
        for copy in copies:
            copy.start()
        total = jnp.zeros((rows, width), jnp.float32)
        for i, copy in enumerate(copies):
            up, down = halves(found_ref[:, i * chunk : (i + 1) * chunk])
            copy.wait()
            panel_up, panel_down = halves(held[i])
            both = jnp.dot(
                jnp.concatenate([up, down], axis=0), panel_up, preferred_element_type=jnp.float32
            )
            rest = jnp.dot(up, panel_down, preferred_element_type=jnp.float32)
            total += both[:rows] + both[rows:] + rest
        out_ref[...] = solved_ref[...] - total

    return kernel_call(
        body,
        jax.ShapeDtypeStruct(solved.shape, solved.dtype),
        [in_vmem()] * 2 + [in_hbm()] * 2,
        in_vmem(),
        scratch=[
            pltpu.VMEM((2 * size // chunk, chunk, width), jnp.float32),
            pltpu.SemaphoreType.DMA((2 * size // chunk,)),
        ],
        flops=36 * rows * found.shape[1] * width,
        moved=4 * found.shape[1] * width,
    )(solved, found, panel, panel_other)


def cut(found, part):
    rows, width = found.shape
    size = width // 2
    side = size // 2

    def body(found_ref, owned_ref):
        (plane, core), col = position(), lax.axis_index("col")
        place = (col // 2 - CORES * plane + ROWS + HALF_RING - 1) % ROWS
        keeper = (place // HALF_RING) ^ core
        first = pl.multiple_of(col % 2 * (rows // 2), rows // 2)
        back = (HALF_RING - place % HALF_RING) % HALF_RING
        for k in range(2):
            start = pl.multiple_of(keeper * size + k * side, side)
            block = found_ref[pl.ds(first, rows // 2), pl.ds(start, side)]
            owned_ref[:, k] = pltpu.roll(block, back * part, 1)[:, : owned_ref.shape[2]]

    return kernel_call(
        body,
        jax.ShapeDtypeStruct((rows // 2, 2, part), found.dtype),
        [in_vmem()],
        in_vmem(),
        moved=4 * rows * part,
    )(found)


def shards(factor, solved, rhs_window, inverses, coupling):
    rows = solved.shape[0]
    own = with_window(factor, rhs_window)
    other = lax.ppermute(own, "row", core_swap())
    two_own = lax.ppermute(own, "row", apart(2))
    two_other = lax.ppermute(other, "row", apart(2))
    both = join(own, other)
    one = lax.ppermute(both, "row", apart(1))
    solved_other = lax.ppermute(solved, "row", core_swap())
    three_own = lax.ppermute(two_own, "row", apart(1))
    two_other = after(two_other, (solved_other,))
    four = lax.ppermute(two_other, "row", apart(2))
    three_other = lax.ppermute(two_other, "row", apart(1))
    part, block = factor.shape[1], own.shape[0]
    early = [(both, 0, 0), (one, 0, 2), (one, block, 1), (two_own, 0, 4), (two_other, 0, 3)]
    early += [(three_other, 0, 5), (three_own, 0, 6)]
    total, panel = reduce_early(solved, solved_other, early, part)
    partial, panel = reduce_late(solved, solved_other, total, panel, four, (HALF_RING - 1,), part)

    panel_other = lax.ppermute(panel, "row", core_swap())

    each = rows // COLS
    residual = jnp.sum(lax.all_to_all(partial, "col", 0, 0, tiled=True), axis=0)
    residual_other = lax.ppermute(residual[each:], "row", core_swap())
    found = panel_solve(residual[:each], residual_other, inverses, coupling, panel_other[:8, :128])
    gathered = lax.all_to_all(
        jnp.broadcast_to(found, (COLS,) + found.shape), "col", 0, 0, tiled=True
    ).reshape(rows, -1)
    part = rhs_window.shape[2]
    owned = lax.ppermute(cut(gathered, part), ("row", "col"), work_to_window())
    return owned, correct(solved, gathered, panel, panel_other)


def solution(mesh):
    in_specs = (P(None, "row", "col"), P("row", "col"), P("col", None, "row"), P(), P())
    out_specs = (P("col", None, "row"), P("row", "col"))
    return jax.shard_map(shards, mesh=mesh, in_specs=in_specs, out_specs=out_specs, check_vma=False)
```
